32 devices in a mesh: section: 2 (over core), dp: 4 (over y, x), mp: 4 (over z).
Axes of the slice: x: 2, y: 2, z: 4, core: 2. Of those that a mesh axis runs over, the one named last changes fastest.
Arguments:
- tokens: bfloat16 [2, 1216, 4, 1024], P(None, 'mp', 'dp'), may hold values from -6 to 6
- cotangent: bfloat16 [2, 1216, 4, 1024], P(None, 'mp', 'dp'), may hold values from -6 to 6
- lengths: int32 [2, 4, 5], P(None, 'dp'), may hold values from 1 to 512, 1216 in all within a row
- qkv_weight: float32 [2, 3, 1024, 1024], P('section', None, 'dp', 'mp'), may hold values from -0.1875 to 0.1875
- qkv_bias: float32 [2, 3, 1024], P('section', None, 'mp'), may hold values from -3 to 3
- out_weight: float32 [2, 1024, 1024], P('section', 'mp', 'dp'), may hold values from -0.75 to 0.75
- out_bias: float32 [2, 1024], P('section'), may hold values from -3 to 3
- up_weight: float32 [2, 1024, 4096], P('section', 'dp', 'mp'), may hold values from -0.1875 to 0.1875
- up_bias: float32 [2, 4096], P('section', 'mp'), may hold values from -3 to 3
- down_weight: float32 [2, 4096, 1024], P('section', 'mp', 'dp'), may hold values from -0.09375 to 0.09375
- down_bias: float32 [2, 1024], P('section'), may hold values from -3 to 3
- norm_gain: float32 [2, 2, 1024], P('section'), may hold values from 0.1 to 1.9
- norm_shift: float32 [2, 2, 1024], P('section'), may hold values from -3 to 3
- prefix_keys: float32 [2, 64, 1024], P('section', None, 'mp'), may hold values from -6 to 6
- prefix_values: float32 [2, 64, 1024], P('section', None, 'mp'), may hold values from -6 to 6
Outputs:
- outputs: bfloat16 [2, 2, 1216, 4, 1024], P('section', None, 'mp', 'dp')
- input_grads: bfloat16 [2, 2, 1216, 4, 1024], P('section', None, 'mp', 'dp')
- key_grads: float32 [2, 64, 1024], P('section', None, 'mp')
- value_grads: float32 [2, 64, 1024], P('section', None, 'mp')
The draws below stay inside these ranges and needn't reach their ends.
Inputs may be any that keep to these rules, and one draw needn't show every extreme that they name: The last entry of a row is its number of padding positions at the row's end; the others are its segments' lengths in order; entries of a row sum to 1216.
All inputs are finite; a program needn't handle non-finite values.
Results may differ from the reference program's by a relative error of at most 0.019.
Values may be sent and summed in bfloat16 or wider, within the bound.
No kernel may reach another device: no remote copies, remote signals or barrier semaphores. Data moves between devices by JAX's collectives and lax.ppermute only.
A program may use at most 384 MiB of HBM per device.

```python
import math
import jax
import jax.numpy as jnp
import numpy as np
from jax import lax

D = 1024
HEADS = 16
HD = 64
FF = 4096
PREFIX = 64
SEQ = 1216
PIECES = 5
LMOST = 512
MICRO = 2
ROWS = 4


def block_scale(stream_key, shape, shards, low, largest):
    def one(dim, parts):
        draws = jax.random.uniform(jax.random.fold_in(jax.random.fold_in(stream_key, 6), dim), (parts,), jnp.float32, low / len(shards), largest / len(shards))
        return jnp.repeat(jnp.exp(draws), shape[dim] // parts).reshape((-1,) + (1,) * (len(shape) - dim - 1))

    level = one(*shards[0])
    for cut in shards[1:]:
        level = level * one(*cut)
    return level


def length_profile(count, total, most, lean):
    weights = [(1 << 20) // math.isqrt(rank ** lean) + 1 for rank in range(2, count + 1)]
    surplus, counts = total - most - (count - 1), [1] * (count - 1)
    while surplus > 0:
        movable = [i for i in range(count - 1) if counts[i] < most]
        mass, left = sum([weights[i] for i in movable]), surplus
        for i in movable:
            addition = min(most - counts[i], max(1, left * weights[i] // mass), surplus)
            counts[i] = counts[i] + addition
            surplus = surplus - addition
    return np.array([most] + counts)


def ragged_sizes(rng, count, total, reach, slope):
    if count == 2:
        one = jax.random.randint(rng, (), max(1, total - reach), min(reach, total - 1) + 1)
        return jnp.stack([one, total - one])
    sizes = jnp.asarray(length_profile(count, total, reach, slope), jnp.int32)
    pairs = (count - 1) // 2
    giver, receiver = sizes[1:1 + 2 * pairs:2], sizes[2:2 + 2 * pairs:2]
    slack = jnp.minimum(giver - 1, reach - receiver)
    moved = jax.random.randint(jax.random.fold_in(rng, 1), (pairs,), 0, 1 << 20) % (slack + 1)
    sizes = sizes.at[1:1 + 2 * pairs:2].set(giver - moved).at[2:2 + 2 * pairs:2].set(receiver + moved)
    return sizes[jax.random.permutation(jax.random.fold_in(rng, 2), count)]


def normal_values(rng, extent, width, bound, pieces=(), kind=jnp.bfloat16):
    drawn = width * jax.random.normal(rng, extent, jnp.float32)
    if pieces:
        drawn = drawn * block_scale(rng, extent, pieces, -0.22, 0.18)
    return jnp.clip(drawn, -bound, bound).astype(kind)


def setup_inputs(seed: int = 0) -> dict:
    seeds = jax.random.split(jax.random.key(seed), 16)
    return {
        "tokens": normal_values(seeds[0], (MICRO, SEQ, ROWS, D), 1.0, 6.0, ((1, 4), (2, 4))),
        "cotangent": normal_values(seeds[1], (MICRO, SEQ, ROWS, D), 1.0, 6.0, ((1, 4), (2, 4))),
        "lengths": jax.vmap(lambda own: ragged_sizes(own, PIECES, SEQ, LMOST, 2))(jax.random.split(seeds[2], MICRO * ROWS)).reshape((MICRO, ROWS, PIECES)).astype(jnp.int32),
        "qkv_weight": normal_values(seeds[3], (2, 3, D, D), D ** -0.5, 0.1875, ((0, 2), (2, 4), (3, 4)), jnp.float32),
        "qkv_bias": normal_values(seeds[4], (2, 3, D), 0.5, 3.0, ((0, 2), (2, 4)), jnp.float32),
        "out_weight": normal_values(seeds[5], (2, D, D), (D // 16) ** -0.5, 0.75, ((0, 2), (1, 4), (2, 4)), jnp.float32),
        "out_bias": normal_values(seeds[6], (2, D), 0.5, 3.0, ((0, 2),), jnp.float32),
        "up_weight": normal_values(seeds[7], (2, D, FF), D ** -0.5, 0.1875, ((0, 2), (1, 4), (2, 4)), jnp.float32),
        "up_bias": normal_values(seeds[8], (2, FF), 0.5, 3.0, ((0, 2), (1, 4)), jnp.float32),
        "down_weight": normal_values(seeds[9], (2, FF, D), FF ** -0.5, 0.09375, ((0, 2), (1, 4), (2, 4)), jnp.float32),
        "down_bias": normal_values(seeds[10], (2, D), 0.5, 3.0, ((0, 2),), jnp.float32),
        "norm_gain": jnp.clip(1.0 + 0.18 * jax.random.normal(seeds[11], (2, 2, D), jnp.float32), 0.1, 1.9),
        "norm_shift": normal_values(seeds[12], (2, 2, D), 0.5, 3.0, ((0, 2),), jnp.float32),
        "prefix_keys": normal_values(seeds[13], (2, PREFIX, D), 1.0, 6.0, ((0, 2), (2, 4)), jnp.float32),
        "prefix_values": normal_values(seeds[14], (2, PREFIX, D), 1.0, 6.0, ((0, 2), (2, 4)), jnp.float32),
    }


@jax.custom_vjp
def low(v):
    return lax.optimization_barrier(v.astype(jnp.bfloat16)).astype(jnp.float32)

@jax.custom_vjp
def low_back(v):
    return v

def low_keep(v):
    return (low(v), None)

def low_pass(kept, grad):
    return (grad,)

def back_keep(v):
    return (v, None)

def back_low(kept, grad):
    return (low(grad),)
low.defvjp(low_keep, low_pass)
low_back.defvjp(back_keep, back_low)
highest = lax.Precision.HIGHEST

def layer_norm(stream_value, gain, shift):
    center = lax.optimization_barrier(jnp.mean(stream_value, axis=-1, keepdims=True))
    centred = stream_value - center
    spread = lax.optimization_barrier(jnp.mean(centred * centred, axis=-1, keepdims=True))
    return centred * lax.rsqrt(spread + 1e-05) * gain + shift

def segment_ids(lengths):
    ends = jnp.cumsum(lengths, axis=-1)
    places = jnp.arange(SEQ, dtype=jnp.int32)
    return lax.optimization_barrier(jnp.sum((places[:, None] >= ends[..., None, :]).astype(jnp.int32), axis=-1))

def attend_row(queries, row_keys, row_values, segment, prefix_key_heads, prefix_value_heads):
    all_keys = jnp.concatenate([prefix_key_heads, row_keys], axis=1)
    all_values = jnp.concatenate([prefix_value_heads, row_values], axis=1)
    allowed = (segment[:, None] == segment[None, :]) & (segment[None, :] < PIECES - 1)
    allowed = jnp.concatenate([jnp.ones((SEQ, PREFIX), jnp.bool_), allowed], axis=1)
    scores = jnp.einsum('hqd,hkd->hqk', queries, all_keys, precision=highest) * HD ** (-0.5)
    scores = low_back(jnp.where(allowed[None], scores, -1e+30))
    probs = jax.nn.softmax(scores, axis=-1)
    return jnp.einsum('hqk,hkd->hqd', low(probs), all_values, precision=highest)

def encoder_layer(inputs, prefix_keys, prefix_values, segments, frozen):
    qkv_w, qkv_b, out_w, out_b, up_w, up_b, down_w, down_b, gains, shifts = frozen
    stream = low_back(inputs)
    flat_stream = stream.reshape(-1, D)
    projected = []
    for channel in range(3):
        value_c = low_back(low(jnp.dot(flat_stream, low(qkv_w[channel]), precision=highest) + qkv_b[channel]))
        value_c = value_c.reshape(MICRO, SEQ, ROWS, HEADS, HD).transpose(0, 2, 3, 1, 4).reshape(MICRO * ROWS, HEADS, SEQ, HD)
        projected.append(value_c)
    prefix_key_heads = low(prefix_keys).reshape(PREFIX, HEADS, HD).transpose(1, 0, 2)
    prefix_value_heads = low(prefix_values).reshape(PREFIX, HEADS, HD).transpose(1, 0, 2)

    def one_row(item):
        return attend_row(item[0], item[1], item[2], item[3], prefix_key_heads, prefix_value_heads)
    attended = lax.map(jax.checkpoint(one_row), (projected[0], projected[1], projected[2], segments))
    attended = attended.reshape(MICRO, ROWS, HEADS, SEQ, HD).transpose(0, 3, 1, 2, 4).reshape(-1, D)
    attended = low_back(low(attended))
    branch_attn = low_back(jnp.dot(attended, low(out_w), precision=highest) + out_b)
    normed = layer_norm(flat_stream + branch_attn, gains[0], shifts[0])
    hidden = low_back(jnp.dot(low(normed), low(up_w), precision=highest) + up_b)
    active = low(jax.nn.gelu(hidden, approximate=False))
    branch_ffn = low_back(jnp.dot(active, low(down_w), precision=highest) + down_b)
    result = low(layer_norm(normed + branch_ffn, gains[1], shifts[1]))
    return result.reshape(MICRO, SEQ, ROWS, D)

def reference(tokens, cotangent, lengths, qkv_weight, qkv_bias, out_weight, out_bias, up_weight, up_bias, down_weight, down_bias, norm_gain, norm_shift, prefix_keys, prefix_values):
    segments = segment_ids(lengths).reshape(MICRO * ROWS, SEQ)
    stream = tokens.astype(jnp.float32)
    everything = (qkv_weight, qkv_bias, out_weight, out_bias, up_weight, up_bias, down_weight, down_bias, norm_gain, norm_shift)
    section_inputs = []
    section_outputs = []
    for layer_index in range(2):
        frozen = tuple((array[layer_index] for array in everything))
        section_inputs.append(stream)
        stream = encoder_layer(stream, prefix_keys[layer_index], prefix_values[layer_index], segments, frozen)
        section_outputs.append(stream)
    gradient = cotangent.astype(jnp.float32)
    input_list = [None, None]
    key_list = [None, None]
    value_list = [None, None]
    for layer_index in (1, 0):
        frozen = tuple((array[layer_index] for array in everything))
        _, pullback = jax.vjp(lambda inputs, keys_in, values_in: encoder_layer(inputs, keys_in, values_in, segments, frozen), section_inputs[layer_index], prefix_keys[layer_index], prefix_values[layer_index])
        gradient, key_list[layer_index], value_list[layer_index] = pullback(gradient)
        input_list[layer_index] = gradient
    return (jnp.stack(section_outputs).astype(jnp.bfloat16), jnp.stack(input_list).astype(jnp.bfloat16), jnp.stack(key_list), jnp.stack(value_list))
```

```python
import jax
import jax.numpy as jnp
from jax import lax
from jax.sharding import PartitionSpec as P

HEADS = 16
HD = 64
EPS = 1e-5
BF = jnp.bfloat16
F32 = jnp.float32


def dot(a, b, dims):
    return lax.dot_general(a, b, (dims, ((), ())), preferred_element_type=F32)


def nn(a, b):
    return dot(a, b, ((1,), (0,)))


def nt(a, b):
    return dot(a, b, ((1,), (1,)))


def norm_stats(v):
    centred = v - jnp.mean(v, axis=-1, keepdims=True)
    inv = lax.rsqrt(jnp.mean(centred * centred, axis=-1, keepdims=True) + EPS)
    return centred * inv, inv


def norm_back(v, grad, gain):
    n, inv = norm_stats(v)
    e = grad * gain
    return inv * (e - jnp.mean(e, -1, keepdims=True) - n * jnp.mean(e * n, -1, keepdims=True))


class Place:
    def __init__(self):
        self.mp = lax.axis_size("mp")
        self.g = self.mp // 2
        self.c = lax.axis_index("section")
        self.z = lax.axis_index("mp")
        self.m = self.z // self.g
        self.p = self.z % self.g

    def send(self, value, route):
        pairs = []
        for c in range(2):
            for m in range(2):
                for p in range(self.g):
                    to = route(c, m, p)
                    if to is not None:
                        source = c * self.mp + m * self.g + p
                        pairs.append((source, to[0] * self.mp + to[1] * self.g + to[2]))
        return lax.ppermute(value, ("section", "mp"), pairs)

    def core(self, value):
        return lax.ppermute(value, "section", [(0, 1), (1, 0)])

    def chip(self, value, j):
        return lax.ppermute(value, "mp", [(z, z ^ j) for z in range(self.mp)])


def gather_weights(place, l, qkv, out, up, down):
    g = place.g
    attn = qkv[0].astype(BF).transpose(1, 0, 2).reshape(qkv.shape[2], -1)
    rest = jnp.concatenate([out[0].astype(BF).T, up[0].astype(BF), down[0].astype(BF).T], axis=1)
    attn = sum(
        place.send(attn, lambda c, m, p: (m, half, p) if c == l else None) for half in range(2)
    )
    qkv_full = lax.all_gather(attn, "dp", axis=0, tiled=True)
    panels = []
    for j in range(g):
        panel = sum(
            place.send(rest, lambda c, m, p: (m, half, p ^ j) if c == l else None)
            for half in range(2)
        )
        panels.append(lax.all_gather(panel, "dp", axis=0, tiled=True))
    return qkv_full, panels


def scores_of(queries, keys, allowed):
    scores = jnp.einsum("hqd,hkd->hqk", queries, keys, preferred_element_type=F32) * HD ** (-0.5)
    return jnp.where(allowed[None], scores, -1e30)


def attend(queries, keys, values, allowed):
    length = queries.shape[1]
    step = length // 2
    outs, totals = [], []
    for first in range(0, length, step):
        s = scores_of(queries[:, first : first + step], keys, allowed[first : first + step])
        peak = jnp.max(s, axis=-1, keepdims=True)
        e = jnp.exp(s - peak)
        total = jnp.sum(e, axis=-1, keepdims=True)
        w = (e / total).astype(BF)
        outs.append(jnp.einsum("hqk,hkd->hqd", w, values, preferred_element_type=F32))
        totals.append(peak + jnp.log(total))
    return jnp.concatenate(outs, 1).astype(BF), jnp.concatenate(totals, 1)


def attend_back(queries, keys, values, allowed, totals, grad):
    length = queries.shape[1]
    step = length // 2
    gk = jnp.zeros(keys.shape, F32)
    gv = jnp.zeros(values.shape, F32)
    gq = []
    for first in range(0, length, step):
        cut = slice(first, first + step)
        s = scores_of(queries[:, cut], keys, allowed[cut])
        prob = jnp.exp(s - totals[:, cut])
        go = grad[:, cut]
        gp = jnp.einsum("hqd,hkd->hqk", go, values, preferred_element_type=F32)
        inner = jnp.sum(prob * gp, axis=-1, keepdims=True)
        gs = (prob * (gp - inner)).astype(BF)
        gq.append(
            jnp.einsum("hqk,hkd->hqd", gs, keys, preferred_element_type=F32) * HD ** (-0.5)
        )
        gk = gk + jnp.einsum(
            "hqk,hqd->hkd", gs, queries[:, cut], preferred_element_type=F32
        ) * HD ** (-0.5)
        gv = gv + jnp.einsum("hqk,hqd->hkd", prob.astype(BF), go, preferred_element_type=F32)
    return jnp.concatenate(gq, 1), gk, gv


def to_heads(flat):
    return flat.reshape(flat.shape[0], -1, HD).transpose(1, 0, 2)


def from_heads(heads):
    return heads.transpose(1, 0, 2).reshape(heads.shape[1], -1)


def layer_forward(place, x_own, weights, small, allowed):
    qkv_w, panels = weights
    g, rows = place.g, x_own.shape[0]
    d_model = x_own.shape[1]
    gained, up_b, qkv_b, pre = small
    out_b, down_b, gain0, gain1, shift0, shift1 = gained
    blocks = []
    for j in range(g):
        own = x_own if j == 0 else place.chip(x_own, j)
        blocks += [own, place.core(own)]
    projected = [nn(b, qkv_w) + qkv_b for b in blocks]
    flat = jnp.concatenate(projected, 0).astype(BF)
    width = flat.shape[1] // 3
    q, k, v = (to_heads(flat[:, i * width : (i + 1) * width]) for i in range(3))
    keys = jnp.concatenate([to_heads(pre[0]), k], axis=1)
    values = jnp.concatenate([to_heads(pre[1]), v], axis=1)
    o, totals = attend(q, keys, values, allowed)
    o = from_heads(o)
    mine = 0.0
    for j in range(g):
        part = o[j * 2 * rows : (j + 1) * 2 * rows]
        part = part if j == 0 else place.chip(part, j)
        mine = mine + nt(part, panels[j][:, :width])
    a = x_own.astype(F32) + mine[:rows] + place.core(mine[rows:]) + out_b
    n, _ = norm_stats(a)
    x1 = n * gain0 + shift0
    x1_low = x1.astype(BF)
    both = jnp.concatenate([x1_low, place.core(x1_low)], 0)
    hidden, branch = [], 0.0
    ff = up_b[0].shape[0]
    for j in range(g):
        u = nn(both, panels[j][:, width : width + ff]) + up_b[j]
        f = jax.nn.gelu(u, approximate=False).astype(BF)
        branch = branch + nt(f, panels[j][:, width + ff :])
        hidden.append(u)
    z = x1 + branch[:rows] + place.core(branch[rows:]) + down_b
    n, _ = norm_stats(z)
    result = (n * gain1 + shift1).astype(BF)
    return result, (q, keys, values, totals, a, hidden, z)


def layer_backward(place, grad, saved, weights, small, allowed):
    q, keys, values, totals, a, hidden, z = saved
    qkv_w, panels = weights
    gained, up_b, _, _ = small
    _, _, gain0, gain1, _, _ = gained
    g, rows = place.g, grad.shape[0]
    ff = up_b[0].shape[0]
    width = q.shape[0] * HD
    dz = norm_back(z, grad.astype(F32), gain1)
    low = dz.astype(BF)
    both = jnp.concatenate([low, place.core(low)], 0)
    branch = 0.0
    for j in range(g):
        df = nn(both, panels[j][:, width + ff :])
        u = hidden[j]
        slope = 0.5 * (1 + lax.erf(u * 2 ** (-0.5))) + u * jnp.exp(-0.5 * u * u) * 0.3989422804014327
        branch = branch + nt((df * slope).astype(BF), panels[j][:, width : width + ff])
    dx1 = dz + branch[:rows] + place.core(branch[rows:])
    da = norm_back(a, dx1, gain0)
    low = da.astype(BF)
    both = jnp.concatenate([low, place.core(low)], 0)
    parts = []
    for j in range(g):
        do = nn(both, panels[j][:, :width]).astype(BF)
        parts.append(do if j == 0 else place.chip(do, j))
    go = to_heads(jnp.concatenate(parts, 0))
    gq, gk, gv = attend_back(q, keys, values, allowed, totals, go)
    prefix = keys.shape[1] - q.shape[1]
    kv_grad = jnp.stack([from_heads(gk[:, :prefix]), from_heads(gv[:, :prefix])])
    back = jnp.concatenate(
        [from_heads(t).astype(BF) for t in (gq, gk[:, prefix:], gv[:, prefix:])], axis=1
    )
    dx = nt(back, qkv_w).reshape(g, 2, rows, -1)
    summed = dx[:, 0] + place.core(dx[:, 1].astype(BF)).astype(F32)
    total = da + summed[0]
    for j in range(1, g):
        total = total + place.chip(summed[j].astype(BF), j).astype(F32)
    return total.astype(BF), kv_grad


def on_device(
    tokens,
    cotangent,
    lengths,
    qkv_weight,
    qkv_bias,
    out_weight,
    out_bias,
    up_weight,
    up_bias,
    down_weight,
    down_bias,
    norm_gain,
    norm_shift,
    prefix_keys,
    prefix_values,
):
    place = Place()
    g, mp, c, m, p = place.g, place.mp, place.c, place.m, place.p
    layers = [
        gather_weights(place, l, qkv_weight, out_weight, up_weight, down_weight) for l in range(2)
    ]

    d_model, ff = out_bias.shape[1], up_bias.shape[1]
    fixed = jnp.concatenate([out_bias, down_bias, norm_gain[0], norm_shift[0]], 0)
    flat = jnp.concatenate([fixed.reshape(-1), up_bias[0], qkv_bias[0].reshape(-1)])
    flat = lax.all_gather(flat, ("section", "mp"))
    pre = jnp.stack([prefix_keys[0], prefix_values[0]]).astype(BF)
    pre = lax.all_gather(pre, ("section", "mp"))
    shard = c * g + p
    smalls = []
    for l in range(2):
        mine = lax.dynamic_index_in_dim(flat, l * mp + shard, 0, keepdims=False)
        gained = [mine[i * d_model : (i + 1) * d_model] for i in range(6)]
        qkv_b = mine[6 * d_model + ff :]
        up_b = []
        for j in range(g):
            row = lax.dynamic_index_in_dim(flat, l * mp + c * g + (p ^ j), 0, keepdims=False)
            up_b.append(row[6 * d_model : 6 * d_model + ff])
        smalls.append(
            (gained, up_b, qkv_b, lax.dynamic_index_in_dim(pre, l * mp + shard, 0, keepdims=False))
        )

    rows = tokens.shape[1]

    def own_rows(array):
        other = lax.dynamic_index_in_dim(array, 1 - m, 0, keepdims=False)[:, 0]
        same = lax.dynamic_index_in_dim(array, m, 0, keepdims=False)[:, 0]
        moved = place.send(other, lambda c, m, p: (c, 1 - m, p) if c == m else None)
        return jnp.where(c == m, same, moved)

    x = own_rows(tokens)
    grad = own_rows(cotangent)

    row_lengths = lax.dynamic_index_in_dim(lengths, m, 0, keepdims=False)[0]
    places = jnp.concatenate(
        [
            ((c ^ i) * g + (p ^ j)) * rows + jnp.arange(rows, dtype=jnp.int32)
            for j in range(g)
            for i in range(2)
        ]
    )
    segment = jnp.sum((places[:, None] >= jnp.cumsum(row_lengths)[None]).astype(jnp.int32), -1)
    seen = (segment[:, None] == segment[None, :]) & (segment[None, :] != lengths.shape[-1] - 1)
    prefix = prefix_keys.shape[1]
    allowed = jnp.concatenate([jnp.ones((seen.shape[0], prefix), jnp.bool_), seen], axis=1)

    results, kept = [], []
    for l in range(2):
        x, saved = layer_forward(place, x, layers[l], smalls[l], allowed)
        results.append(x)
        kept.append(saved)
    grads, kv = [None, None], [None, None]
    for l in (1, 0):
        grad, kv[l] = layer_backward(place, grad, kept[l], layers[l], smalls[l], allowed)
        grads[l] = grad

    def home(pair, half):
        return sum(
            place.send(pair[l], lambda c, m, p: (l, c, p) if m == half else None) for l in range(2)
        )

    outs = jnp.stack([home(results, half) for half in range(2)])[:, :, None]
    gouts = jnp.stack([home(grads, half) for half in range(2)])[:, :, None]
    kv = lax.psum(home(kv, 0) + home(kv, 1), "dp")
    return outs[None], gouts[None], kv[None, 0], kv[None, 1]


def solution(mesh):
    placed = (
        P(None, "mp", "dp", None),
        P(None, "mp", "dp", None),
        P(None, "dp", None),
        P("section", None, "dp", "mp"),
        P("section", None, "mp"),
        P("section", "mp", "dp"),
        P("section", None),
        P("section", "dp", "mp"),
        P("section", "mp"),
        P("section", "mp", "dp"),
        P("section", None),
        P("section", None, None),
        P("section", None, None),
        P("section", None, "mp"),
        P("section", None, "mp"),
    )
    return jax.shard_map(
        on_device,
        mesh=mesh,
        in_specs=placed,
        out_specs=(
            P("section", None, "mp", "dp", None),
            P("section", None, "mp", "dp", None),
            P("section", None, "mp"),
            P("section", None, "mp"),
        ),
        check_vma=False,
    )
```

```python
from functools import partial

import jax
import jax.numpy as jnp
from jax import lax
from jax.experimental import pallas as pl
from jax.experimental.pallas import tpu as pltpu
from jax.sharding import PartitionSpec as P

HEADS = 16
HD = 64
EPS = 1e-5
BF = jnp.bfloat16
F32 = jnp.float32
TQ = 128
CK = 256
SIZES = (2, 3, 4, 5, 6, 7, 8, 10)
TH = 512
VMEM = 48 << 20


def dot(a, b, dims):
    return lax.dot_general(a, b, (dims, ((), ())), preferred_element_type=F32)


def nn(a, b):
    return dot(a, b, ((1,), (0,)))


def nt(a, b):
    return dot(a, b, ((1,), (1,)))


def norm_stats(v):
    centred = v - jnp.mean(v, axis=-1, keepdims=True)
    inv = lax.rsqrt(jnp.mean(centred * centred, axis=-1, keepdims=True) + EPS)
    return centred * inv, inv


def norm_back(v, grad, gain):
    n, inv = norm_stats(v)
    e = grad * gain
    return inv * (e - jnp.mean(e, -1, keepdims=True) - n * jnp.mean(e * n, -1, keepdims=True))


class Place:
    def __init__(self):
        self.mp = lax.axis_size("mp")
        self.g = self.mp // 2
        self.c = lax.axis_index("section")
        self.z = lax.axis_index("mp")
        self.m = self.z // self.g
        self.p = self.z % self.g

    def send(self, value, route):
        pairs = []
        for c in range(2):
            for m in range(2):
                for p in range(self.g):
                    to = route(c, m, p)
                    if to is not None:
                        source = c * self.mp + m * self.g + p
                        pairs.append((source, to[0] * self.mp + to[1] * self.g + to[2]))
        return lax.ppermute(value, ("section", "mp"), pairs)

    def core(self, value):
        return lax.ppermute(value, "section", [(0, 1), (1, 0)])

    def chip(self, value, j):
        return lax.ppermute(value, "mp", [(z, z ^ j) for z in range(self.mp)])


def tie(value, *after):
    return lax.optimization_barrier((value,) + after)[0]


def high_low(v):
    high = v.astype(BF)
    return high, (v - high.astype(F32)).astype(BF)


def gather(block):
    return lax.all_gather(block, "dp", axis=0, tiled=True)


def sum_steps(place):
    count = lax.axis_size("dp")
    steps = [lambda value: value + place.chip(value, place.g)]
    bit = 1
    while bit < count:
        pairs = [(i, i ^ bit) for i in range(count)]
        steps.append(partial(lambda pairs, v: v + lax.ppermute(v, "dp", pairs), pairs))
        bit *= 2
    return steps


def move_qkv(place, qkv, qkv_bias, pre):
    weight = qkv[0].astype(BF).transpose(1, 0, 2).reshape(qkv.shape[2], -1)
    width = weight.shape[1]
    bias = jnp.stack(high_low(qkv_bias[0].reshape(-1)))
    pre = jnp.concatenate([v[0].astype(BF) for v in pre], axis=1)
    pre = jnp.pad(pre, ((0, 0), (0, width - pre.shape[1])))
    block = jnp.concatenate([weight, pre, jnp.pad(bias, ((0, 14), (0, 0)))], axis=0)
    got = [place.send(block, lambda c, m, p: (m, c ^ turn, p)) for turn in range(2)]
    first = place.m == 0
    split = [jnp.where(first, got[0], got[1]), jnp.where(first, got[1], got[0])]
    rows, prefix = weight.shape[0], pre.shape[0]
    third = width // 3
    full = gather(jnp.concatenate([v[:rows] for v in split], axis=1))
    out = []
    for l, v in enumerate(split):
        b = v[rows + prefix].astype(F32) + v[rows + prefix + 1].astype(F32)
        p = v[rows : rows + prefix]
        w = full[:, l * width : (l + 1) * width]
        out.append((got[1], w, b, (p[:, :third], p[:, third : 2 * third])))
    return out, full


def own_shard(place, l, out, up, up_bias, down):
    block = jnp.concatenate([up[0].astype(BF), down[0].astype(BF).T, out[0].astype(BF).T], axis=1)
    bias = jnp.stack(high_low(up_bias[0]))
    bias = jnp.pad(bias, ((0, 14), (0, block.shape[1] - bias.shape[1])))
    block = jnp.concatenate([block, bias], 0)
    got = [place.send(block, lambda c, m, p: (m, half, p) if c == l else None) for half in range(2)]
    return jnp.where(place.m == 0, got[0], got[1])


def cut_shard(shard, rows, ff):
    bias = shard[rows : rows + 2, :ff].astype(F32)
    shard = shard[:rows]
    return shard[:, :ff], shard[:, ff : 2 * ff], shard[:, 2 * ff :], bias[0] + bias[1]


def spread_heads(block, heads):
    if heads == 1:
        return block
    lane = lax.broadcasted_iota(jnp.int32, block.shape, 1) // HD
    return jnp.concatenate([jnp.where(lane == h, block, jnp.zeros_like(block)) for h in range(heads)], 0)

def own_columns(wide, heads):
    return jnp.concatenate([wide[h*HD:(h+1)*HD, h*TQ:(h+1)*TQ] for h in range(heads)], 0)

def widen(mask, heads):
    return mask if heads == 1 else jnp.concatenate([mask] * heads, axis=1)

def each_size(range_ref, t, body):
    for index, size in enumerate(SIZES):
        @pl.when(range_ref[t, 1] == index)
        def _():
            body(pl.multiple_of(range_ref[t, 0], TQ), size * TQ)

def window_mask(start, size, span_ref, heads):
    key = lax.broadcasted_iota(jnp.int32, (size, TQ), 0) + start
    return widen((key >= span_ref[0:1, :]) & (key < span_ref[1:2, :]), heads)

def attn_fwd(prefix, heads, range_ref, span_ref, qkv_ref, o_ref, lse_ref, vt_ref):
    w = heads * HD
    t = pl.program_id(0)
    @pl.when(t == 0)
    def _():
        for i in range(vt_ref.shape[1] // CK):
            at = slice(i * CK, (i + 1) * CK)
            vt_ref[:, at] = qkv_ref[at, 2*w:3*w].astype(F32).T.astype(BF)
    def body(start, size):
        q = spread_heads(qkv_ref[pl.ds(pl.multiple_of(t*TQ, TQ), TQ), 0:w] * BF(HD ** -0.5), heads)
        at = pl.ds(start, size)
        first = nt(qkv_ref[0:prefix, w:2*w], q)
        rest = nt(qkv_ref[at, w:2*w], q)
        rest = jnp.where(window_mask(start, size, span_ref, heads), rest, -1e30)
        peak = jnp.maximum(jnp.max(first, axis=0, keepdims=True), jnp.max(rest, axis=0, keepdims=True))
        first, rest = jnp.exp(first - peak), jnp.exp(rest - peak)
        total = jnp.sum(first, axis=0, keepdims=True) + jnp.sum(rest, axis=0, keepdims=True)
        acc = nn(vt_ref[:, 0:prefix], first.astype(BF)) + nn(vt_ref[:, at], rest.astype(BF))
        o_ref[...] = own_columns(acc * (1.0 / total), heads).T.astype(BF)
        lse = peak + jnp.log(total)
        for h in range(heads):
            lse_ref[h:h+1, :] = lse[:, h*TQ:(h+1)*TQ]
    each_size(range_ref, t, body)

def attn_bwd(prefix, heads, range_ref, span_ref, qkv_ref, lse_ref, o_ref, do_ref, out_ref, pre_ref,
             kt_ref, dk_ref, dv_ref):
    w = heads * HD
    t = pl.program_id(0)
    @pl.when(t == 0)
    def _():
        for i in range(kt_ref.shape[1] // CK):
            at = slice(i * CK, (i + 1) * CK)
            kt_ref[:, at] = qkv_ref[at, w:2*w].astype(F32).T.astype(BF)
        dk_ref[...] = jnp.zeros_like(dk_ref)
        dv_ref[...] = jnp.zeros_like(dv_ref)
    def body(start, size):
        here = pl.ds(pl.multiple_of(t*TQ, TQ), TQ)
        q = spread_heads(qkv_ref[here, 0:w] * BF(HD ** -0.5), heads)
        do = do_ref[...]
        both = (do.astype(F32) * o_ref[...].astype(F32)).T
        delta = jnp.concatenate([jnp.sum(both[h*HD:(h+1)*HD], axis=0, keepdims=True) for h in range(heads)], 1)
        do = spread_heads(do, heads)
        lse = jnp.concatenate([lse_ref[h:h+1, :] for h in range(heads)], 1)
        dq = 0.0
        for at, mask in ((pl.ds(0, prefix), None), (pl.ds(start, size), window_mask(start, size, span_ref, heads))):
            prob = jnp.exp(nt(qkv_ref[at, w:2*w], q) - lse)
            if mask is not None:
                prob = jnp.where(mask, prob, 0.0)
            ds = (prob * (nt(qkv_ref[at, 2*w:3*w], do) - delta)).astype(BF)
            dv_ref[at, :] += nn(prob.astype(BF), do)
            dk_ref[at, :] += nn(ds, q)
            dq = dq + nn(kt_ref[:, at], ds)
        out_ref[here, 0:w] = (own_columns(dq, heads) * HD ** -0.5).T.astype(BF)
    each_size(range_ref, t, body)
    @pl.when(t == pl.num_programs(0) - 1)
    def _():
        out_ref[:, w:2*w] = dk_ref[...].astype(BF)
        out_ref[:, 2*w:3*w] = dv_ref[...].astype(BF)
        pre_ref[0] = dk_ref[0:prefix, :]
        pre_ref[1] = dv_ref[0:prefix, :]

def whole(shape):
    return pl.BlockSpec(shape, lambda t, *_: (0,) * len(shape))

def attend(ranges, span, qkv, prefix, heads):
    n, w = qkv.shape[0], heads*HD
    return pl.pallas_call(
        partial(attn_fwd, prefix, heads),
        grid_spec=pltpu.PrefetchScalarGridSpec(
            num_scalar_prefetch=1, grid=(n//TQ,),
            in_specs=[pl.BlockSpec((2, TQ), lambda t, *_: (0, t)), whole(qkv.shape)],
            out_specs=[pl.BlockSpec((TQ, w), lambda t, *_: (t, 0)), pl.BlockSpec((heads, TQ), lambda t, *_: (0, t))],
            scratch_shapes=[pltpu.VMEM((w, n), BF)]),
        out_shape=[jax.ShapeDtypeStruct((n, w), BF), jax.ShapeDtypeStruct((heads, n), F32)],
        compiler_params=pltpu.CompilerParams(dimension_semantics=("arbitrary",), vmem_limit_bytes=VMEM), name="attend",
        cost_estimate=pl.CostEstimate(flops=2*n*n*w*2, bytes_accessed=n*w*8, transcendentals=n*n*heads),
    )(ranges, span, qkv)

def attend_back(ranges, span, qkv, lse, o, do, prefix, heads):
    n, w = qkv.shape[0], heads*HD
    tile = pl.BlockSpec((TQ, w), lambda t, *_: (t, 0))
    return pl.pallas_call(
        partial(attn_bwd, prefix, heads),
        grid_spec=pltpu.PrefetchScalarGridSpec(
            num_scalar_prefetch=1, grid=(n//TQ,),
            in_specs=[pl.BlockSpec((2, TQ), lambda t, *_: (0, t)), whole(qkv.shape),
                      pl.BlockSpec((heads, TQ), lambda t, *_: (0, t)), tile, tile],
            out_specs=[whole((n, 3*w)), whole((2, prefix, w))],
            scratch_shapes=[pltpu.VMEM((w, n), BF), pltpu.VMEM((n, w), F32), pltpu.VMEM((n, w), F32)]),
        out_shape=[jax.ShapeDtypeStruct((n, 3*w), BF), jax.ShapeDtypeStruct((2, prefix, w), F32)],
        compiler_params=pltpu.CompilerParams(dimension_semantics=("arbitrary",), vmem_limit_bytes=VMEM), name="attend_back",
        cost_estimate=pl.CostEstimate(flops=5*n*n*w*2, bytes_accessed=n*w*14, transcendentals=n*n*heads),
    )(ranges, span, qkv, lse, o, do)

def take_size(index):
    return sum(jnp.where(index == i, size, 0) for i, size in enumerate(SIZES))


def spans(lengths, length, prefix):
    ends = jnp.cumsum(lengths)
    starts = ends - lengths
    place = jnp.arange(prefix + length, dtype=jnp.int32) - prefix
    last = lengths.shape[0] - 1
    inside = (place[:, None] >= starts[None, :last]) & (place[:, None] < ends[None, :last])
    low = jnp.sum(jnp.where(inside, starts[None, :last] + prefix, 0), -1)
    high = jnp.sum(jnp.where(inside, ends[None, :last] + prefix, 0), -1)
    tl, th = low.reshape(-1, TQ), high.reshape(-1, TQ)
    tiles = (prefix + length) // TQ
    first = jnp.min(jnp.where(th > 0, tl, prefix + length), axis=1) // TQ
    size = (jnp.max(th, axis=1) + TQ - 1) // TQ - first
    index = jnp.sum((size[:, None] > jnp.array(SIZES)[None]).astype(jnp.int32), 1)
    first = jnp.minimum(first, tiles - take_size(index))
    return jnp.stack([first * TQ, index], 1).astype(jnp.int32), jnp.stack([low, high]).astype(jnp.int32)


def bell_parts(u):
    bell = jnp.exp(-0.5 * u * u)
    t = 1.0 / (1.0 + (0.3275911 * 0.5**0.5) * jnp.abs(u))
    tail = 1.061405429 * t - 1.453152027
    for k in (1.421413741, -0.284496736, 0.254829592):
        tail = tail * t + k
    tail = 0.5 * tail * t * bell
    return bell, jnp.where(u > 0, 1.0 - tail, tail)


def slope_of(u, bell, phi):
    return phi + u * (bell * 0.3989422804014327)


def feed_kernel(mode, cuts, refs):
    count = len(cuts)
    panels, refs = refs[: 2 * count], refs[2 * count :]
    (own_ref, other_ref), refs = refs[:2], refs[2:]
    biases = ()
    if mode != "back":
        biases, refs = refs[:count], refs[count:]
    if mode == "again":
        inputs, refs = refs[:2], refs[2:]
    if mode == "back":
        slope_ref, refs = refs[0], refs[1:]
    x_ref, acc_ref, *again = refs[-3:] if mode == "again" else refs[-2:]
    out_own_ref, out_other_ref, *kept = refs[: -2 - len(again)]
    rows = own_ref.shape[0]
    t = pl.program_id(0)

    @pl.when(t == 0)
    def _():
        x_ref[:rows] = own_ref[...]
        x_ref[rows:] = other_ref[...]
        if mode == "again":
            again[0][:rows] = inputs[0][...]
            again[0][rows:] = inputs[1][...]
        acc_ref[...] = jnp.zeros_like(acc_ref)

    def run(k):
        up_ref, down_ref = panels[2 * k], panels[2 * k + 1]
        if mode == "forward":
            u = nn(x_ref[...], up_ref[...]) + biases[k][...]
            bell, phi = bell_parts(u)
            if kept:
                kept[0][...] = slope_of(u, bell, phi).astype(BF)
            acc_ref[...] += nt((u * phi).astype(BF), down_ref[...])
        else:
            df = nn(x_ref[...], down_ref[...])
            if mode == "again":
                u = nn(again[0][...], up_ref[...]) + biases[k][...]
                slope = slope_of(u, *bell_parts(u))
            else:
                slope = slope_ref[...].astype(F32)
            acc_ref[...] += nt((df * slope).astype(BF), up_ref[...])

    for k, (first, last) in enumerate(cuts):
        if count == 1:
            run(k)
        else:
            pl.when((t >= first) & (t < last))(partial(run, k))

    @pl.when(t == pl.num_programs(0) - 1)
    def _():
        out_own_ref[...] = acc_ref[:rows]
        out_other_ref[...] = acc_ref[rows:].astype(BF)


def feed(mode, panels, own, other, biases=(), inputs=(), slopes=(), keep=False):
    rows, d = own.shape
    th = TH if all(units % TH == 0 for _, units in panels) else TH // 2
    specs, arrays, cuts, at = [], [], [], 0
    for panel, units in panels:
        steps = units // th
        low = partial(lambda at, steps, t: jnp.clip(t - at, 0, steps - 1), at, steps)
        if len(panels) == 1:
            low = lambda t: t
        specs.append(pl.BlockSpec((d, th), partial(lambda low, t: (0, low(t)), low)))
        specs.append(pl.BlockSpec((d, th), partial(lambda low, n, t: (0, n + low(t)), low, steps)))
        arrays += [panel, panel]
        cuts.append((at, at + steps))
        at += steps
    full = pl.BlockSpec((rows, d), lambda t: (0, 0))
    part = pl.BlockSpec((2 * rows, th), lambda t: (0, t))
    specs += [full, full]
    arrays += [own, other]
    if mode != "back":
        for k, bias in enumerate(biases):
            specs.append(pl.BlockSpec((1, th), specs[2 * k].index_map))
            arrays.append(bias)
    specs += [full] * len(inputs) + [part] * len(slopes)
    arrays += list(inputs) + list(slopes)
    outs = [jax.ShapeDtypeStruct((rows, d), F32), jax.ShapeDtypeStruct((rows, d), BF)]
    out_specs = [full, full]
    if keep:
        outs.append(jax.ShapeDtypeStruct((2 * rows, at * th), BF))
        out_specs.append(part)
    matmuls = 3 if mode == "again" else 2
    scratch = [pltpu.VMEM((2 * rows, d), BF), pltpu.VMEM((2 * rows, d), F32)]
    if mode == "again":
        scratch.append(pltpu.VMEM((2 * rows, d), BF))
    return pl.pallas_call(
        lambda *refs: feed_kernel(mode, cuts, refs),
        grid=(at,),
        in_specs=specs,
        out_specs=out_specs,
        out_shape=outs,
        scratch_shapes=scratch,
        compiler_params=pltpu.CompilerParams(
            dimension_semantics=("arbitrary",), vmem_limit_bytes=VMEM
        ),
        cost_estimate=pl.CostEstimate(
            flops=4 * matmuls * rows * d * at * th,
            bytes_accessed=4 * d * at * th,
            transcendentals=0,
        ),
        name="feed_" + mode,
    )(*arrays)


class Order:
    def __init__(self, place, prefix, rows):
        self.place, self.prefix, self.rows = place, prefix, rows
        self.length = prefix + place.mp * rows

    def start(self, j, i):
        place = self.place
        return self.prefix + ((place.c ^ i) * place.g + (place.p ^ j)) * self.rows

    def put(self, whole, block, j, i):
        return lax.dynamic_update_slice(whole, block, (self.start(j, i), 0))

    def get(self, whole, j, i):
        return lax.dynamic_slice(whole, (self.start(j, i), 0), (self.rows, whole.shape[1]))


def both_cores(place, mine, theirs):
    return mine + place.core(theirs).astype(F32)


def attention(place, order, blocks, weights, where):
    qkv_w, qkv_b, pre = weights
    prefix = order.prefix
    qkv = jnp.pad(
        jnp.concatenate([jnp.zeros_like(pre[0]), pre[0], pre[1]], axis=1),
        ((0, order.length - prefix), (0, 0)),
    )
    for (j, i), block in blocks.items():
        qkv = order.put(qkv, (nn(block, qkv_w) + qkv_b).astype(BF), j, i)
    return (qkv,) + tuple(attend(*where, qkv, prefix, qkv_w.shape[1] // 3 // HD))


def spread_rows(place, x_own):
    blocks = {}
    for j in range(place.g):
        blocks[j, 0] = x_own if j == 0 else place.chip(x_own, j)
        blocks[j, 1] = place.core(blocks[j, 0])
    return blocks


def out_project(place, order, x_own, o, outs, fixed):
    mine = [0.0, 0.0]
    for j in range(place.g):
        part = jnp.concatenate([order.get(o, j, i) for i in range(2)], 0)
        part = part if j == 0 else place.chip(part, j)
        for i in range(2):
            mine[i] = mine[i] + nt(part[i * order.rows : (i + 1) * order.rows], outs[j])
    a = x_own.astype(F32) + both_cores(place, mine[0], mine[1].astype(BF)) + fixed[0]
    x1 = norm_stats(a)[0] * fixed[2] + fixed[4]
    return a, x1


def out_back(place, order, dx1, a, outs, fixed):
    da = norm_back(a, dx1, fixed[2])
    low = da.astype(BF)
    both = jnp.concatenate([low, place.core(low)], 0)
    go = jnp.zeros((order.length, outs[0].shape[1]), BF)
    for j in range(place.g - 1, -1, -1):
        do = nn(both, outs[j]).astype(BF)
        do = do if j == 0 else place.chip(do, j)
        for i in range(2):
            go = order.put(go, do[i * order.rows : (i + 1) * order.rows], j, i)
    return da, go


def input_back(place, order, da, back, qkv_w):
    total = da
    for j in range(place.g - 1, -1, -1):
        other = nt(order.get(back, j, 1), qkv_w).astype(BF)
        summed = both_cores(place, nt(order.get(back, j, 0), qkv_w), other)
        total = total + (summed if j == 0 else place.chip(summed.astype(BF), j).astype(F32))
    return total.astype(BF)


def on_device(
    tokens,
    cotangent,
    lengths,
    qkv_weight,
    qkv_bias,
    out_weight,
    out_bias,
    up_weight,
    up_bias,
    down_weight,
    down_bias,
    norm_gain,
    norm_shift,
    prefix_keys,
    prefix_values,
):
    place = Place()
    g, mp, c, m, p = place.g, place.mp, place.c, place.m, place.p
    rows = tokens.shape[1]
    width, ff, dim = out_weight.shape[1], up_weight.shape[2], up_weight.shape[1]
    prefix = prefix_keys.shape[1]
    order = Order(place, prefix, rows)
    row_lengths = lax.dynamic_index_in_dim(lengths, m, 0, keepdims=False)[0]
    where = spans(row_lengths, mp * rows, prefix)
    fixed = jnp.concatenate([out_bias, down_bias, norm_gain[0], norm_shift[0]], 0)
    other = place.core(fixed)
    fixed = [jnp.where(c == 0, fixed, other), jnp.where(c == 0, other, fixed)]

    def own_rows(array):
        other = lax.dynamic_index_in_dim(array, 1 - m, 0, keepdims=False)[:, 0]
        same = lax.dynamic_index_in_dim(array, m, 0, keepdims=False)[:, 0]
        moved = place.send(other, lambda c, m, p: (c, 1 - m, p) if c == m else None)
        return jnp.where(c == m, same, moved)

    attn, full = move_qkv(place, qkv_weight, qkv_bias, (prefix_keys, prefix_values))
    x = own_rows(tie(tokens, attn[0][0]))
    raw = (out_weight, up_weight, up_bias, down_weight)

    def shard_of(l, *after):
        held = tie(raw, *after)
        return own_shard(place, l, *held)

    shard0 = shard_of(0, x)
    up0, down0, out0, bias0 = cut_shard(shard0, dim, ff)
    outs0 = [out0] + [place.chip(out0, j) for j in range(1, g)]
    first = jnp.concatenate([up0, down0] + outs0, axis=1)
    blocks = spread_rows(place, x)
    panel0 = gather(tie(first, full, blocks))
    shard1 = shard_of(1, first)
    shards1 = [cut_shard(shard1 if j == 0 else place.chip(shard1, j), dim, ff) for j in range(g)]
    second = jnp.concatenate([v[k] for k in range(3) for v in shards1], axis=1)
    bias1 = jnp.concatenate([v[3] for v in shards1])[None]
    panel1 = gather(tie(second, panel0))
    grad = own_rows(tie(cotangent, second))
    outs = []
    for panel, start in ((panel0, 2 * ff), (panel1, 2 * g * ff)):
        outs.append([panel[:, start + j * width : start + (j + 1) * width] for j in range(g)])

    qkv0, o0, lse0 = attention(place, order, blocks, attn[0][1:], where)
    a0, x1 = out_project(place, order, x, o0, outs[0], fixed[0])
    wide0 = spread_rows(place, x1.astype(BF))
    z = x1 + fixed[0][1]
    for j in range(g):
        mine, theirs = feed("forward", [(panel0, ff)], wide0[j, 0], wide0[j, 1], [bias0[None]])
        summed = both_cores(place, mine, theirs)
        z = z + (summed if j == 0 else place.chip(summed.astype(BF), j).astype(F32))
    z0 = z
    y0 = (norm_stats(z)[0] * fixed[0][3] + fixed[0][5]).astype(BF)

    blocks = spread_rows(place, y0)
    late = tie(shard0, blocks)
    late = [place.chip(late, j) for j in range(1, g)]
    qkv1, o1, lse1 = attention(place, order, tie(blocks, grad), attn[1][1:], where)
    a1, x1 = out_project(place, order, y0, o1, outs[1], fixed[1])
    low = x1.astype(BF)
    mine, theirs, slope = feed(
        "forward", [(panel1, g * ff)], low, place.core(low), [bias1], keep=True
    )
    z1 = x1 + both_cores(place, mine, theirs) + fixed[1][1]
    y1 = (norm_stats(z1)[0] * fixed[1][3] + fixed[1][5]).astype(BF)

    moved = [cut_shard(tie(v, o1), dim, ff) for v in late]
    rest = jnp.concatenate([v[k] for k in range(2) for v in moved], axis=1)
    rest_bias = jnp.concatenate([v[3] for v in moved])[None]
    rest = gather(tie(rest, panel1))

    def home(value, l, half):
        return place.send(value, lambda c, m, p: (l, c, p) if m == half else None)

    def home_kv(value, l):
        return place.send(value, lambda c, m, p: (l, c, p) if c == m else None)

    steps = sum_steps(place)

    dz = norm_back(z1, grad.astype(F32), fixed[1][3])
    low = dz.astype(BF)
    mine, theirs = feed("back", [(panel1, g * ff)], low, place.core(low), slopes=[slope])
    dx1 = dz + both_cores(place, mine, theirs)
    first = m == 0
    pair = [place.send(tie(jnp.where(first, y0, y1), mine), lambda c, m, p: (m, c, p))]
    pair += [place.send(tie(jnp.where(first, y1, y0), mine), lambda c, m, p: (1 - m, c, p))]
    results = [jnp.where(c == 0, pair[h], pair[1 - h]) for h in range(2)]
    da, go = out_back(place, order, dx1, a1, outs[1], fixed[1])
    back, kv1 = attend_back(*where, qkv1, lse1, o1, go, prefix, width // HD)
    back = tie(back, results)
    grad1 = input_back(place, order, da, back, attn[1][1])
    kv1 = steps[0](kv1)

    dz = norm_back(z0, grad1.astype(F32), fixed[0][3])
    low = dz.astype(BF)
    mine, theirs = feed(
        "again",
        [(panel0, ff), (rest, (g - 1) * ff)],
        low,
        place.core(low),
        [bias0[None], rest_bias],
        inputs=(wide0[0, 0], wide0[0, 1]),
    )
    gouts = [home(grad1, 1, h) for h in range(2)]
    kv1 = steps[1](tie(kv1, low))
    dx1 = dz + both_cores(place, mine, theirs)
    da, go = out_back(place, order, dx1, a0, outs[0], fixed[0])
    kv1 = tie(kv1, mine)
    for step in steps[2:]:
        kv1 = step(kv1)
    kv = home_kv(tie(kv1, go), 1)
    back, kv0 = attend_back(*where, qkv0, lse0, o0, go, prefix, width // HD)
    back = tie(back, gouts, kv)
    grad0 = input_back(place, order, da, back, attn[0][1])
    for step in steps:
        kv0 = step(kv0)
    gouts = [gouts[h] + home(grad0, 0, h) for h in range(2)]
    kv = kv + home_kv(kv0, 0)
    results = jnp.stack(results)[:, :, None]
    gouts = jnp.stack(gouts)[:, :, None]
    return results[None], gouts[None], kv[None, 0], kv[None, 1]


def solution(mesh):
    placed = (
        P(None, "mp", "dp", None),
        P(None, "mp", "dp", None),
        P(None, "dp", None),
        P("section", None, "dp", "mp"),
        P("section", None, "mp"),
        P("section", "mp", "dp"),
        P("section", None),
        P("section", "dp", "mp"),
        P("section", "mp"),
        P("section", "mp", "dp"),
        P("section", None),
        P("section", None, None),
        P("section", None, None),
        P("section", None, "mp"),
        P("section", None, "mp"),
    )
    return jax.shard_map(
        on_device,
        mesh=mesh,
        in_specs=placed,
        out_specs=(
            P("section", None, "mp", "dp", None),
            P("section", None, "mp", "dp", None),
            P("section", None, "mp"),
            P("section", None, "mp"),
        ),
        check_vma=False,
    )
```

```python
from functools import partial

import jax
import jax.numpy as jnp
from jax import lax
from jax.experimental import pallas as pl
from jax.experimental.pallas import tpu as pltpu
from jax.sharding import PartitionSpec as P

HEADS = 16
HD = 64
EPS = 1e-5
BF = jnp.bfloat16
F32 = jnp.float32
TQ = 128
CK = 256
SIZES = (2, 3, 4, 5, 6, 7, 8, 10)
TH = 512
VMEM = 48 << 20


def dot(a, b, dims):
    return lax.dot_general(a, b, (dims, ((), ())), preferred_element_type=F32)


def nn(a, b):
    return dot(a, b, ((1,), (0,)))


def nt(a, b):
    return dot(a, b, ((1,), (1,)))


def norm_stats(v):
    centred = v - jnp.mean(v, axis=-1, keepdims=True)
    inv = lax.rsqrt(jnp.mean(centred * centred, axis=-1, keepdims=True) + EPS)
    return centred * inv, inv


def norm_back(v, grad, gain):
    n, inv = norm_stats(v)
    e = grad * gain
    return inv * (e - jnp.mean(e, -1, keepdims=True) - n * jnp.mean(e * n, -1, keepdims=True))


class Place:
    def __init__(self):
        self.mp = lax.axis_size("mp")
        self.g = self.mp // 2
        self.c = lax.axis_index("section")
        self.z = lax.axis_index("mp")
        self.m = self.z // self.g
        self.p = self.z % self.g

    def send(self, value, route):
        pairs = []
        for c in range(2):
            for m in range(2):
                for p in range(self.g):
                    to = route(c, m, p)
                    if to is not None:
                        source = c * self.mp + m * self.g + p
                        pairs.append((source, to[0] * self.mp + to[1] * self.g + to[2]))
        return lax.ppermute(value, ("section", "mp"), pairs)

    def core(self, value):
        return lax.ppermute(value, "section", [(0, 1), (1, 0)])

    def chip(self, value, j):
        return lax.ppermute(value, "mp", [(z, z ^ j) for z in range(self.mp)])


def tie(value, *after):
    return lax.optimization_barrier((value,) + after)[0]


def high_low(v):
    high = v.astype(BF)
    return high, (v - high.astype(F32)).astype(BF)


def gather(block):
    return lax.all_gather(block, "dp", axis=0, tiled=True)


def own_layer(place, l, block):
    return [place.send(block, lambda c, m, p: (m, half, p) if c == l else None) for half in range(2)]


def merged(place, got):
    return jnp.where(place.m == 0, got[0], got[1])


def qkv_block(qkv, qkv_bias, pre):
    weight = qkv[0].astype(BF).transpose(1, 0, 2).reshape(qkv.shape[2], -1)
    width = weight.shape[1]
    bias = jnp.stack(high_low(qkv_bias[0].reshape(-1)))
    pre = jnp.concatenate([v[0].astype(BF) for v in pre], axis=1)
    pre = jnp.pad(pre, ((0, 0), (0, width - pre.shape[1])))
    return jnp.concatenate([weight, pre, jnp.pad(bias, ((0, 14), (0, 0)))], axis=0)


def cut_qkv(v, rows, prefix):
    third = v.shape[1] // 3
    bias = v[rows + prefix].astype(F32) + v[rows + prefix + 1].astype(F32)
    pre = v[rows : rows + prefix]
    return v[:rows], bias, (pre[:, :third], pre[:, third : 2 * third])


def own_shard(place, l, out, up, up_bias, down):
    block = jnp.concatenate([up[0].astype(BF), down[0].astype(BF).T, out[0].astype(BF).T], axis=1)
    bias = jnp.stack(high_low(up_bias[0]))
    bias = jnp.pad(bias, ((0, 14), (0, block.shape[1] - bias.shape[1])))
    block = jnp.concatenate([block, bias], 0)
    return own_layer(place, l, block)


def cut_shard(shard, rows, ff):
    bias = shard[rows : rows + 2, :ff].astype(F32)
    shard = shard[:rows]
    return shard[:, :ff], shard[:, ff : 2 * ff], shard[:, 2 * ff :], bias[0] + bias[1]


def spread_heads(block, heads):
    if heads == 1:
        return block
    lane = lax.broadcasted_iota(jnp.int32, block.shape, 1) // HD
    return jnp.concatenate([jnp.where(lane == h, block, jnp.zeros_like(block)) for h in range(heads)], 0)

def own_columns(wide, heads):
    return jnp.concatenate([wide[h*HD:(h+1)*HD, h*TQ:(h+1)*TQ] for h in range(heads)], 0)

def widen(mask, heads):
    return mask if heads == 1 else jnp.concatenate([mask] * heads, axis=1)

def each_size(range_ref, t, body):
    for index, size in enumerate(SIZES):
        @pl.when(range_ref[t, 1] == index)
        def _():
            body(pl.multiple_of(range_ref[t, 0], TQ), size * TQ)

def window_mask(start, size, span_ref, heads):
    key = lax.broadcasted_iota(jnp.int32, (size, TQ), 0) + start
    return widen((key >= span_ref[0:1, :]) & (key < span_ref[1:2, :]), heads)

def attn_fwd(prefix, heads, range_ref, span_ref, qkv_ref, o_ref, lse_ref, vt_ref):
    w = heads * HD
    t = pl.program_id(0)
    @pl.when(t == 0)
    def _():
        for i in range(vt_ref.shape[1] // CK):
            at = slice(i * CK, (i + 1) * CK)
            vt_ref[:, at] = qkv_ref[at, 2*w:3*w].astype(F32).T.astype(BF)
    def body(start, size):
        q = spread_heads(qkv_ref[pl.ds(pl.multiple_of(t*TQ, TQ), TQ), 0:w] * BF(HD ** -0.5), heads)
        at = pl.ds(start, size)
        first = nt(qkv_ref[0:prefix, w:2*w], q)
        rest = nt(qkv_ref[at, w:2*w], q)
        rest = jnp.where(window_mask(start, size, span_ref, heads), rest, -1e30)
        peak = jnp.maximum(jnp.max(first, axis=0, keepdims=True), jnp.max(rest, axis=0, keepdims=True))
        first, rest = jnp.exp(first - peak), jnp.exp(rest - peak)
        total = jnp.sum(first, axis=0, keepdims=True) + jnp.sum(rest, axis=0, keepdims=True)
        acc = nn(vt_ref[:, 0:prefix], first.astype(BF)) + nn(vt_ref[:, at], rest.astype(BF))
        o_ref[...] = own_columns(acc * (1.0 / total), heads).T.astype(BF)
        lse = peak + jnp.log(total)
        for h in range(heads):
            lse_ref[h:h+1, :] = lse[:, h*TQ:(h+1)*TQ]
    each_size(range_ref, t, body)

def attn_bwd(prefix, heads, range_ref, span_ref, qkv_ref, lse_ref, o_ref, do_ref, out_ref, pre_ref,
             kt_ref, dk_ref, dv_ref):
    w = heads * HD
    t = pl.program_id(0)
    @pl.when(t == 0)
    def _():
        for i in range(kt_ref.shape[1] // CK):
            at = slice(i * CK, (i + 1) * CK)
            kt_ref[:, at] = qkv_ref[at, w:2*w].astype(F32).T.astype(BF)
        dk_ref[...] = jnp.zeros_like(dk_ref)
        dv_ref[...] = jnp.zeros_like(dv_ref)
    def body(start, size):
        here = pl.ds(pl.multiple_of(t*TQ, TQ), TQ)
        q = spread_heads(qkv_ref[here, 0:w] * BF(HD ** -0.5), heads)
        do = do_ref[...]
        both = (do.astype(F32) * o_ref[...].astype(F32)).T
        delta = jnp.concatenate([jnp.sum(both[h*HD:(h+1)*HD], axis=0, keepdims=True) for h in range(heads)], 1)
        do = spread_heads(do, heads)
        lse = jnp.concatenate([lse_ref[h:h+1, :] for h in range(heads)], 1)
        dq = 0.0
        for at, mask in ((pl.ds(0, prefix), None), (pl.ds(start, size), window_mask(start, size, span_ref, heads))):
            prob = jnp.exp(nt(qkv_ref[at, w:2*w], q) - lse)
            if mask is not None:
                prob = jnp.where(mask, prob, 0.0)
            ds = (prob * (nt(qkv_ref[at, 2*w:3*w], do) - delta)).astype(BF)
            dv_ref[at, :] += nn(prob.astype(BF), do)
            dk_ref[at, :] += nn(ds, q)
            dq = dq + nn(kt_ref[:, at], ds)
        out_ref[here, 0:w] = (own_columns(dq, heads) * HD ** -0.5).T.astype(BF)
    each_size(range_ref, t, body)
    @pl.when(t == pl.num_programs(0) - 1)
    def _():
        out_ref[:, w:2*w] = dk_ref[...].astype(BF)
        out_ref[:, 2*w:3*w] = dv_ref[...].astype(BF)
        pre_ref[0] = dk_ref[0:prefix, :]
        pre_ref[1] = dv_ref[0:prefix, :]

def whole(shape):
    return pl.BlockSpec(shape, lambda t, *_: (0,) * len(shape))

def attend(ranges, span, qkv, prefix, heads):
    n, w = qkv.shape[0], heads*HD
    return pl.pallas_call(
        partial(attn_fwd, prefix, heads),
        grid_spec=pltpu.PrefetchScalarGridSpec(
            num_scalar_prefetch=1, grid=(n//TQ,),
            in_specs=[pl.BlockSpec((2, TQ), lambda t, *_: (0, t)), whole(qkv.shape)],
            out_specs=[pl.BlockSpec((TQ, w), lambda t, *_: (t, 0)), pl.BlockSpec((heads, TQ), lambda t, *_: (0, t))],
            scratch_shapes=[pltpu.VMEM((w, n), BF)]),
        out_shape=[jax.ShapeDtypeStruct((n, w), BF), jax.ShapeDtypeStruct((heads, n), F32)],
        compiler_params=pltpu.CompilerParams(dimension_semantics=("arbitrary",), vmem_limit_bytes=VMEM), name="attend",
        cost_estimate=pl.CostEstimate(flops=2*n*n*w*2//4000, bytes_accessed=1, transcendentals=0),
    )(ranges, span, qkv)

def attend_back(ranges, span, qkv, lse, o, do, prefix, heads):
    n, w = qkv.shape[0], heads*HD
    tile = pl.BlockSpec((TQ, w), lambda t, *_: (t, 0))
    return pl.pallas_call(
        partial(attn_bwd, prefix, heads),
        grid_spec=pltpu.PrefetchScalarGridSpec(
            num_scalar_prefetch=1, grid=(n//TQ,),
            in_specs=[pl.BlockSpec((2, TQ), lambda t, *_: (0, t)), whole(qkv.shape),
                      pl.BlockSpec((heads, TQ), lambda t, *_: (0, t)), tile, tile],
            out_specs=[whole((n, 3*w)), whole((2, prefix, w))],
            scratch_shapes=[pltpu.VMEM((w, n), BF), pltpu.VMEM((n, w), F32), pltpu.VMEM((n, w), F32)]),
        out_shape=[jax.ShapeDtypeStruct((n, 3*w), BF), jax.ShapeDtypeStruct((2, prefix, w), F32)],
        compiler_params=pltpu.CompilerParams(dimension_semantics=("arbitrary",), vmem_limit_bytes=VMEM), name="attend_back",
        cost_estimate=pl.CostEstimate(flops=5*n*n*w*2//4000, bytes_accessed=1, transcendentals=0),
    )(ranges, span, qkv, lse, o, do)

def take_size(index):
    return sum(jnp.where(index == i, size, 0) for i, size in enumerate(SIZES))


def spans(lengths, length, prefix):
    ends = jnp.cumsum(lengths)
    starts = ends - lengths
    place = jnp.arange(prefix + length, dtype=jnp.int32) - prefix
    last = lengths.shape[0] - 1
    inside = (place[:, None] >= starts[None, :last]) & (place[:, None] < ends[None, :last])
    low = jnp.sum(jnp.where(inside, starts[None, :last] + prefix, 0), -1)
    high = jnp.sum(jnp.where(inside, ends[None, :last] + prefix, 0), -1)
    tl, th = low.reshape(-1, TQ), high.reshape(-1, TQ)
    tiles = (prefix + length) // TQ
    first = jnp.min(jnp.where(th > 0, tl, prefix + length), axis=1) // TQ
    size = (jnp.max(th, axis=1) + TQ - 1) // TQ - first
    index = jnp.sum((size[:, None] > jnp.array(SIZES)[None]).astype(jnp.int32), 1)
    first = jnp.minimum(first, tiles - take_size(index))
    return jnp.stack([first * TQ, index], 1).astype(jnp.int32), jnp.stack([low, high]).astype(jnp.int32)


def bell_parts(u):
    bell = jnp.exp(-0.5 * u * u)
    t = 1.0 / (1.0 + (0.3275911 * 0.5**0.5) * jnp.abs(u))
    tail = 1.061405429 * t - 1.453152027
    for k in (1.421413741, -0.284496736, 0.254829592):
        tail = tail * t + k
    tail = 0.5 * tail * t * bell
    return bell, jnp.where(u > 0, 1.0 - tail, tail)


def slope_of(u, bell, phi):
    return phi + u * (bell * 0.3989422804014327)


def feed_kernel(mode, cuts, refs):
    count = len(cuts)
    panels, refs = refs[: 2 * count], refs[2 * count :]
    (own_ref, other_ref), refs = refs[:2], refs[2:]
    biases = ()
    if mode != "back":
        biases, refs = refs[:count], refs[count:]
    if mode == "again":
        inputs, refs = refs[:2], refs[2:]
    if mode == "back":
        slope_ref, refs = refs[0], refs[1:]
    x_ref, acc_ref, *again = refs[-3:] if mode == "again" else refs[-2:]
    out_own_ref, out_other_ref, *kept = refs[: -2 - len(again)]
    rows = own_ref.shape[0]
    t = pl.program_id(0)

    @pl.when(t == 0)
    def _():
        x_ref[:rows] = own_ref[...]
        x_ref[rows:] = other_ref[...]
        if mode == "again":
            again[0][:rows] = inputs[0][...]
            again[0][rows:] = inputs[1][...]
        acc_ref[...] = jnp.zeros_like(acc_ref)

    def run(k):
        up_ref, down_ref = panels[2 * k], panels[2 * k + 1]
        if mode == "forward":
            u = nn(x_ref[...], up_ref[...]) + biases[k][...]
            bell, phi = bell_parts(u)
            if kept:
                kept[0][...] = slope_of(u, bell, phi).astype(BF)
            acc_ref[...] += nt((u * phi).astype(BF), down_ref[...])
        else:
            df = nn(x_ref[...], down_ref[...])
            if mode == "again":
                u = nn(again[0][...], up_ref[...]) + biases[k][...]
                slope = slope_of(u, *bell_parts(u))
            else:
                slope = slope_ref[...].astype(F32)
            acc_ref[...] += nt((df * slope).astype(BF), up_ref[...])

    for k, (first, last) in enumerate(cuts):
        if count == 1:
            run(k)
        else:
            pl.when((t >= first) & (t < last))(partial(run, k))

    @pl.when(t == pl.num_programs(0) - 1)
    def _():
        out_own_ref[...] = acc_ref[:rows]
        out_other_ref[...] = acc_ref[rows:].astype(BF)


def feed(mode, panels, own, other, biases=(), inputs=(), slopes=(), keep=False):
    rows, d = own.shape
    th = TH if all(units % TH == 0 for _, units in panels) else TH // 2
    specs, arrays, cuts, at = [], [], [], 0
    for panel, units in panels:
        steps = units // th
        low = partial(lambda at, steps, t: jnp.clip(t - at, 0, steps - 1), at, steps)
        if len(panels) == 1:
            low = lambda t: t
        specs.append(pl.BlockSpec((d, th), partial(lambda low, t: (0, low(t)), low)))
        specs.append(pl.BlockSpec((d, th), partial(lambda low, n, t: (0, n + low(t)), low, steps)))
        arrays += [panel, panel]
        cuts.append((at, at + steps))
        at += steps
    full = pl.BlockSpec((rows, d), lambda t: (0, 0))
    part = pl.BlockSpec((2 * rows, th), lambda t: (0, t))
    specs += [full, full]
    arrays += [own, other]
    if mode != "back":
        for k, bias in enumerate(biases):
            specs.append(pl.BlockSpec((1, th), specs[2 * k].index_map))
            arrays.append(bias)
    specs += [full] * len(inputs) + [part] * len(slopes)
    arrays += list(inputs) + list(slopes)
    outs = [jax.ShapeDtypeStruct((rows, d), F32), jax.ShapeDtypeStruct((rows, d), BF)]
    out_specs = [full, full]
    if keep:
        outs.append(jax.ShapeDtypeStruct((2 * rows, at * th), BF))
        out_specs.append(part)
    matmuls = 3 if mode == "again" else 2
    scratch = [pltpu.VMEM((2 * rows, d), BF), pltpu.VMEM((2 * rows, d), F32)]
    if mode == "again":
        scratch.append(pltpu.VMEM((2 * rows, d), BF))
    return pl.pallas_call(
        lambda *refs: feed_kernel(mode, cuts, refs),
        grid=(at,),
        in_specs=specs,
        out_specs=out_specs,
        out_shape=outs,
        scratch_shapes=scratch,
        compiler_params=pltpu.CompilerParams(
            dimension_semantics=("arbitrary",), vmem_limit_bytes=VMEM
        ),
        cost_estimate=pl.CostEstimate(
            flops=4 * matmuls * rows * d * at * th // 4000,
            bytes_accessed=1,
            transcendentals=0,
        ),
        name="feed_" + mode,
    )(*arrays)


class Order:
    def __init__(self, place, prefix, rows):
        self.place, self.prefix, self.rows = place, prefix, rows
        self.length = prefix + place.mp * rows

    def start(self, j, i):
        place = self.place
        return self.prefix + ((place.c ^ i) * place.g + (place.p ^ j)) * self.rows

    def put(self, whole, block, j, i):
        return lax.dynamic_update_slice(whole, block, (self.start(j, i), 0))

    def get(self, whole, j, i):
        return lax.dynamic_slice(whole, (self.start(j, i), 0), (self.rows, whole.shape[1]))


def both_cores(place, mine, theirs):
    return mine + place.core(theirs).astype(F32)


def attention(place, order, blocks, weights, where):
    qkv_w, qkv_b, pre = weights
    prefix = order.prefix
    qkv = jnp.pad(
        jnp.concatenate([jnp.zeros_like(pre[0]), pre[0], pre[1]], axis=1),
        ((0, order.length - prefix), (0, 0)),
    )
    for (j, i), block in blocks.items():
        qkv = order.put(qkv, (nn(block, qkv_w) + qkv_b).astype(BF), j, i)
    return (qkv,) + tuple(attend(*where, qkv, prefix, qkv_w.shape[1] // 3 // HD))


def spread_rows(place, x_own):
    blocks = {}
    for j in range(place.g):
        blocks[j, 0] = x_own if j == 0 else place.chip(x_own, j)
        blocks[j, 1] = place.core(blocks[j, 0])
    return blocks


def out_parts(place, order, o):
    parts = [jnp.concatenate([order.get(o, j, i) for i in range(2)], 0) for j in range(place.g)]
    return [part if j == 0 else place.chip(part, j) for j, part in enumerate(parts)]


def out_project(place, order, x_own, parts, outs, fixed):
    mine = [0.0, 0.0]
    for j, part in enumerate(parts):
        for i in range(2):
            mine[i] = mine[i] + nt(part[i * order.rows : (i + 1) * order.rows], outs[j])
    a = x_own.astype(F32) + both_cores(place, mine[0], mine[1].astype(BF)) + fixed[0]
    x1 = norm_stats(a)[0] * fixed[2] + fixed[4]
    return a, x1


def out_back(place, order, dx1, a, outs, fixed):
    da = norm_back(a, dx1, fixed[2])
    low = da.astype(BF)
    both = jnp.concatenate([low, place.core(low)], 0)
    go = jnp.zeros((order.length, outs[0].shape[1]), BF)
    for j in range(place.g - 1, -1, -1):
        do = nn(both, outs[j]).astype(BF)
        do = do if j == 0 else place.chip(do, j)
        for i in range(2):
            go = order.put(go, do[i * order.rows : (i + 1) * order.rows], j, i)
    return da, go


def swap_add(value, bit):
    count = lax.axis_size("dp")
    return value + lax.ppermute(value, "dp", [(i, i ^ bit) for i in range(count)])


def input_back(place, order, da, back, qkv_w, kv=None):
    total, bit = da, 1
    if kv is not None:
        kv = swap_add(kv, bit)
    for j in range(place.g - 1, -1, -1):
        other = nt(order.get(back, j, 1), qkv_w).astype(BF)
        summed = both_cores(place, nt(order.get(back, j, 0), qkv_w), other)
        if kv is not None and bit == 1:
            summed, kv = tie((summed, kv), kv)
            bit = 2
        total = total + (summed if j == 0 else place.chip(summed.astype(BF), j).astype(F32))
    if kv is None:
        return total.astype(BF)
    while bit < lax.axis_size("dp"):
        kv = swap_add(kv, bit)
        bit *= 2
    return total.astype(BF), kv


def on_device(
    tokens,
    cotangent,
    lengths,
    qkv_weight,
    qkv_bias,
    out_weight,
    out_bias,
    up_weight,
    up_bias,
    down_weight,
    down_bias,
    norm_gain,
    norm_shift,
    prefix_keys,
    prefix_values,
):
    place = Place()
    g, mp, c, m, p = place.g, place.mp, place.c, place.m, place.p
    rows = tokens.shape[1]
    width, ff, dim = out_weight.shape[1], up_weight.shape[2], up_weight.shape[1]
    prefix = prefix_keys.shape[1]
    order = Order(place, prefix, rows)
    row_lengths = lax.dynamic_index_in_dim(lengths, m, 0, keepdims=False)[0]
    where = spans(row_lengths, mp * rows, prefix)
    fixed = jnp.concatenate([out_bias, down_bias, norm_gain[0], norm_shift[0]], 0)
    other = place.core(fixed)
    fixed = [jnp.where(c == 0, fixed, other), jnp.where(c == 0, other, fixed)]

    def own_rows(array):
        other = lax.dynamic_index_in_dim(array, 1 - m, 0, keepdims=False)[:, 0]
        same = lax.dynamic_index_in_dim(array, m, 0, keepdims=False)[:, 0]
        moved = place.send(other, lambda c, m, p: (c, 1 - m, p) if c == m else None)
        return jnp.where(c == m, same, moved)

    block = qkv_block(qkv_weight, qkv_bias, (prefix_keys, prefix_values))
    thin0 = merged(place, own_layer(place, 0, block))
    w0, qkv_b0, pre0 = cut_qkv(thin0, dim, prefix)
    w0 = gather(w0)
    raw = (out_weight, up_weight, up_bias, down_weight)

    def shard_of(l, *after):
        held = tie(raw, *after)
        return own_shard(place, l, *held)

    shard0 = merged(place, shard_of(0, thin0))
    up0, down0, out0, bias0 = cut_shard(shard0, dim, ff)
    outs0 = [out0] + [place.chip(out0, j) for j in range(1, g)]
    thin1 = merged(place, own_layer(place, 1, tie(block, shard0)))
    w1, qkv_b1, pre1 = cut_qkv(thin1, dim, prefix)
    first = jnp.concatenate([up0, down0] + outs0 + [w1], axis=1)
    panel0 = gather(tie(first, w0))
    x = own_rows(tie(tokens, thin1))
    blocks = spread_rows(place, x)
    shard1 = shard_of(1, blocks)
    qkv0, o0, lse0 = attention(place, order, blocks, (w0, qkv_b0, pre0), where)
    parts = out_parts(place, order, o0)
    shard1 = merged(place, tie(shard1, parts))
    shards1 = [shard1] + [place.chip(shard1, j) for j in range(1, g)]
    w1 = panel0[:, 2 * ff + g * width :]

    def outs_of(panel, start):
        return [panel[:, start + j * width : start + (j + 1) * width] for j in range(g)]

    outs = [outs_of(tie(panel0, parts), 2 * ff)]
    a0, x1 = out_project(place, order, x, parts, outs[0], fixed[0])
    low = x1.astype(BF)
    wide0 = [low] + [place.chip(low, j) for j in range(1, g)]
    z = x1 + fixed[0][1]
    mine, sums = low, []
    for j in range(g):
        own = tie(wide0[j], mine)
        other = place.core(own)
        if j == 0:
            both0 = (own, other)
        mine, theirs = feed("forward", [(panel0, ff)], own, other, [bias0[None]])
        if j == 0:
            shards1 = [cut_shard(v, dim, ff) for v in tie(shards1, mine)]
            second = jnp.concatenate([v[k] for k in range(3) for v in shards1], axis=1)
            bias1 = jnp.concatenate([v[3] for v in shards1])[None]
            panel1 = gather(tie(second, panel0))
            grad = own_rows(tie(cotangent, second))
            outs.append(outs_of(panel1, 2 * g * ff))
        summed = both_cores(place, mine, theirs)
        z = z + (summed if j == 0 else place.chip(summed.astype(BF), j).astype(F32))
    z0 = z
    y0 = (norm_stats(z)[0] * fixed[0][3] + fixed[0][5]).astype(BF)

    blocks = tie(spread_rows(place, y0), grad)
    qkv1, o1, lse1 = attention(place, order, blocks, (w1, qkv_b1, pre1), where)
    a1, x1 = out_project(place, order, y0, out_parts(place, order, o1), outs[1], fixed[1])
    low = x1.astype(BF)
    late = [place.chip(tie(shard0[:, : 2 * ff], low), j) for j in range(1, g)]
    mine, theirs, slope = feed(
        "forward", [(panel1, g * ff)], low, place.core(low), [bias1], keep=True
    )
    z1 = x1 + both_cores(place, mine, theirs) + fixed[1][1]
    y1 = (norm_stats(z1)[0] * fixed[1][3] + fixed[1][5]).astype(BF)

    def home(value, l, half):
        return place.send(value, lambda c, m, p: (l, c, p) if m == half else None)

    dz = norm_back(z1, grad.astype(F32), fixed[1][3])
    low = dz.astype(BF)
    mine, theirs = feed("back", [(panel1, g * ff)], low, place.core(low), slopes=[slope])
    dx1 = tie(dz + both_cores(place, mine, theirs), late)

    late = [cut_shard(v, dim, ff) for v in late]
    rest = jnp.concatenate([v[k] for k in range(2) for v in late], axis=1)
    rest_bias = jnp.concatenate([v[3] for v in late])[None]
    rest = gather(tie(rest, panel1))

    first = m == 0
    da, go = out_back(place, order, dx1, a1, outs[1], fixed[1])
    pair = [place.send(tie(jnp.where(first, y0, y1), go), lambda c, m, p: (m, c, p))]
    back, kv1 = attend_back(*where, qkv1, lse1, o1, go, prefix, width // HD)
    back = tie(back, pair)
    grad1 = input_back(place, order, da, back, w1)

    dz = norm_back(z0, grad1.astype(F32), fixed[0][3])
    low = dz.astype(BF)
    mine, theirs = feed(
        "again",
        [(panel0, ff), (rest, (g - 1) * ff)],
        low,
        place.core(low),
        [bias0[None], rest_bias],
        inputs=both0,
    )
    swapped = tie(jnp.where(first, y1, y0), low)
    pair.append(place.send(swapped, lambda c, m, p: (1 - m, c, p)))
    results = [jnp.where(c == 0, pair[h], pair[1 - h]) for h in range(2)]
    mine, theirs = tie((mine, theirs), pair)
    dx1 = dz + both_cores(place, mine, theirs)
    da, go = out_back(place, order, dx1, a0, outs[0], fixed[0])
    gouts = [home(tie(grad1, go), 1, h) for h in range(2)]
    back, kv0 = attend_back(*where, qkv0, lse0, o0, go, prefix, width // HD)
    back = tie(back, gouts)
    grad0, kv = input_back(place, order, da, back, w0, jnp.stack([kv0, kv1]))
    gouts = [gouts[h] + home(grad0, 0, h) for h in range(2)]
    kv = place.send(jnp.where(first, kv[0], kv[1]), lambda c, m, p: (m, c, p)) + place.send(
        jnp.where(first, kv[1], kv[0]), lambda c, m, p: (1 - m, c, p)
    )
    results = jnp.stack(results)[:, :, None]
    gouts = jnp.stack(gouts)[:, :, None]
    return results[None], gouts[None], kv[None, 0], kv[None, 1]


def solution(mesh):
    placed = (
        P(None, "mp", "dp", None),
        P(None, "mp", "dp", None),
        P(None, "dp", None),
        P("section", None, "dp", "mp"),
        P("section", None, "mp"),
        P("section", "mp", "dp"),
        P("section", None),
        P("section", "dp", "mp"),
        P("section", "mp"),
        P("section", "mp", "dp"),
        P("section", None),
        P("section", None, None),
        P("section", None, None),
        P("section", None, "mp"),
        P("section", None, "mp"),
    )
    return jax.shard_map(
        on_device,
        mesh=mesh,
        in_specs=placed,
        out_specs=(
            P("section", None, "mp", "dp", None),
            P("section", None, "mp", "dp", None),
            P("section", None, "mp"),
            P("section", None, "mp"),
        ),
        check_vma=False,
    )
```

```python
from functools import partial

import jax
import jax.numpy as jnp
from jax import lax
from jax.experimental import pallas as pl
from jax.experimental.pallas import tpu as pltpu
from jax.sharding import PartitionSpec as P

HEADS = 16
HD = 64
EPS = 1e-5
BF = jnp.bfloat16
F32 = jnp.float32
TQ = 128
CK = 256
KC = 64
SIZES = (2, 3, 4, 5, 6, 7, 8, 10)
TH = 512
VMEM = 48 << 20


def dot(a, b, dims):
    return lax.dot_general(a, b, (dims, ((), ())), preferred_element_type=F32)


def nn(a, b):
    return dot(a, b, ((1,), (0,)))


def nt(a, b):
    return dot(a, b, ((1,), (1,)))


def norm_stats(v):
    centred = v - jnp.mean(v, axis=-1, keepdims=True)
    inv = lax.rsqrt(jnp.mean(centred * centred, axis=-1, keepdims=True) + EPS)
    return centred * inv, inv


def norm_back(v, grad, gain):
    n, inv = norm_stats(v)
    e = grad * gain
    return inv * (e - jnp.mean(e, -1, keepdims=True) - n * jnp.mean(e * n, -1, keepdims=True))


class Place:
    def __init__(self):
        self.mp = lax.axis_size("mp")
        self.g = self.mp // 2
        self.c = lax.axis_index("section")
        self.z = lax.axis_index("mp")
        self.m = self.z // self.g
        self.p = self.z % self.g

    def send(self, value, route):
        pairs = []
        for c in range(2):
            for m in range(2):
                for p in range(self.g):
                    to = route(c, m, p)
                    if to is not None:
                        source = c * self.mp + m * self.g + p
                        pairs.append((source, to[0] * self.mp + to[1] * self.g + to[2]))
        return lax.ppermute(value, ("section", "mp"), pairs)

    def core(self, value):
        return lax.ppermute(value, "section", [(0, 1), (1, 0)])

    def chip(self, value, j):
        return lax.ppermute(value, "mp", [(z, z ^ j) for z in range(self.mp)])


def tie(value, *after):
    return lax.optimization_barrier((value,) + after)[0]


def high_low(v):
    high = v.astype(BF)
    return high, (v - high.astype(F32)).astype(BF)


def gather(block):
    return lax.all_gather(block, "dp", axis=0, tiled=True)


def own_layer(place, l, block):
    return [place.send(block, lambda c, m, p: (m, half, p) if c == l else None) for half in range(2)]


def merged(place, got):
    return jnp.where(place.m == 0, got[0], got[1])


def qkv_block(qkv, qkv_bias, pre):
    weight = qkv[0].astype(BF).transpose(1, 0, 2).reshape(qkv.shape[2], -1)
    width = weight.shape[1]
    bias = jnp.stack(high_low(qkv_bias[0].reshape(-1)))
    pre = jnp.concatenate([v[0].astype(BF) for v in pre], axis=1)
    pre = jnp.pad(pre, ((0, 0), (0, width - pre.shape[1])))
    return jnp.concatenate([weight, pre, jnp.pad(bias, ((0, 14), (0, 0)))], axis=0)


def cut_qkv(v, rows, prefix):
    third = v.shape[1] // 3
    bias = v[rows + prefix].astype(F32) + v[rows + prefix + 1].astype(F32)
    pre = v[rows : rows + prefix]
    return v[:rows], bias, (pre[:, :third], pre[:, third : 2 * third])


def own_shard(place, l, out, up, up_bias, down):
    block = jnp.concatenate([up[0].astype(BF), down[0].astype(BF).T, out[0].astype(BF).T], axis=1)
    bias = jnp.stack(high_low(up_bias[0]))
    bias = jnp.pad(bias, ((0, 14), (0, block.shape[1] - bias.shape[1])))
    block = jnp.concatenate([block, bias], 0)
    return own_layer(place, l, block)


def cut_shard(shard, rows, ff):
    bias = shard[rows : rows + 2, :ff].astype(F32)
    shard = shard[:rows]
    return shard[:, :ff], shard[:, ff : 2 * ff], shard[:, 2 * ff :], bias[0] + bias[1]


def spread_heads(block, heads):
    if heads == 1:
        return block
    lane = lax.broadcasted_iota(jnp.int32, block.shape, 1) // HD
    return jnp.concatenate([jnp.where(lane == h, block, jnp.zeros_like(block)) for h in range(heads)], 0)

def own_columns(wide, heads):
    return jnp.concatenate([wide[h*HD:(h+1)*HD, h*TQ:(h+1)*TQ] for h in range(heads)], 0)

def widen(mask, heads):
    return mask if heads == 1 else jnp.concatenate([mask] * heads, axis=1)

def each_size(range_ref, t, body):
    for index, size in enumerate(SIZES):
        @pl.when(range_ref[t, 1] == index)
        def _():
            body(pl.multiple_of(range_ref[t, 0], TQ), size * TQ)

def pieces(prefix, start, size):
    out = [(r, r, KC, False) for r in range(0, prefix, KC)]
    return out + [(prefix + r, start + r, KC, True) for r in range(0, size, KC)]

def piece_mask(first, span_ref, heads):
    key = lax.broadcasted_iota(jnp.int32, (KC, TQ), 0) + first
    return widen((key >= span_ref[0:1, :]) & (key < span_ref[1:2, :]), heads)

def attn_fwd(prefix, heads, range_ref, span_ref, qkv_ref, o_ref, lse_ref, vt_ref, s_ref, p_ref):
    w = heads * HD
    pair = min(2, heads)
    pw = pair * HD
    t = pl.program_id(0)
    @pl.when(t == 0)
    def _():
        for i in range(vt_ref.shape[1] // CK):
            at = slice(i * CK, (i + 1) * CK)
            vt_ref[:, at] = qkv_ref[at, 2*w:3*w].astype(F32).T.astype(BF)
    def body(start, size):
        here = pl.ds(pl.multiple_of(t*TQ, TQ), TQ)
        at = pl.ds(start, size)
        outs = []
        lanes = range(0, w, pw)
        for g, lane in enumerate(lanes):
            q = spread_heads(qkv_ref[here, lane:lane+pw] * BF(HD ** -0.5), pair)
            s_ref[g, 0:prefix] = nt(qkv_ref[0:prefix, w+lane:w+lane+pw], q)
            s_ref[g, prefix:prefix+size] = nt(qkv_ref[at, w+lane:w+lane+pw], q)
        for g, lane in enumerate(lanes):
            peak = jnp.full((8, pair*TQ), -1e30, F32)
            for row, first, n, masked in pieces(prefix, start, size):
                s = s_ref[g, row:row+n]
                if masked:
                    s = jnp.where(piece_mask(first, span_ref, pair), s, -1e30)
                    s_ref[g, row:row+n] = s
                peak = jnp.maximum(peak, jnp.max(s.reshape(n//8, 8, -1), axis=0))
            peak = jnp.max(peak, axis=0, keepdims=True)
            total = jnp.zeros((8, pair*TQ), F32)
            for row, first, n, masked in pieces(prefix, start, size):
                e = jnp.exp(s_ref[g, row:row+n] - peak)
                p_ref[g, row:row+n] = e.astype(BF)
                total = total + jnp.sum(e.reshape(n//8, 8, -1), axis=0)
            total = jnp.sum(total, axis=0, keepdims=True)
            acc = nn(vt_ref[lane:lane+pw, 0:prefix], p_ref[g, 0:prefix]) + nn(vt_ref[lane:lane+pw, at], p_ref[g, prefix:prefix+size])
            outs.append(own_columns(acc * (1.0 / total), pair))
            lse = peak + jnp.log(total)
            for h in range(pair):
                row = lane // HD + h
                lse_ref[row:row+1, :] = lse[:, h*TQ:(h+1)*TQ]
        o_ref[...] = jnp.concatenate(outs, 0).T.astype(BF)
    each_size(range_ref, t, body)

def attn_bwd(prefix, heads, range_ref, span_ref, qkv_ref, lse_ref, o_ref, do_ref, out_ref, pre_ref,
             kt_ref, dk_ref, dv_ref, s_ref, dp_ref, p_ref, ds_ref):
    w = heads * HD
    pair = min(2, heads)
    pw = pair * HD
    t = pl.program_id(0)
    @pl.when(t == 0)
    def _():
        for i in range(kt_ref.shape[1] // CK):
            at = slice(i * CK, (i + 1) * CK)
            kt_ref[:, at] = qkv_ref[at, w:2*w].astype(F32).T.astype(BF)
        dk_ref[...] = jnp.zeros_like(dk_ref)
        dv_ref[...] = jnp.zeros_like(dv_ref)
    def body(start, size):
        here = pl.ds(pl.multiple_of(t*TQ, TQ), TQ)
        both = (do_ref[...].astype(F32) * o_ref[...].astype(F32)).T
        outs = []
        at = pl.ds(start, size)
        parts = ((slice(0, prefix), slice(0, prefix)), (at, slice(prefix, prefix+size)))
        lanes = range(0, w, pw)
        qs, dos = [], []
        for g, lane in enumerate(lanes):
            q = spread_heads(qkv_ref[here, lane:lane+pw] * BF(HD ** -0.5), pair)
            do = spread_heads(do_ref[:, lane:lane+pw], pair)
            qs.append(q)
            dos.append(do)
            for src, dst in parts:
                s_ref[g, dst] = nt(qkv_ref[src, w+lane:w+lane+pw], q)
                dp_ref[g, dst] = nt(qkv_ref[src, 2*w+lane:2*w+lane+pw], do)
        for g, lane in enumerate(lanes):
            rows = range(lane // HD, lane // HD + pair)
            delta = jnp.concatenate([jnp.sum(both[h*HD:(h+1)*HD], axis=0, keepdims=True) for h in rows], 1)
            lse = jnp.concatenate([lse_ref[h:h+1, :] for h in rows], 1)
            for row, first, n, masked in pieces(prefix, start, size):
                prob = jnp.exp(s_ref[g, row:row+n] - lse)
                if masked:
                    prob = jnp.where(piece_mask(first, span_ref, pair), prob, 0.0)
                p_ref[g, row:row+n] = prob.astype(BF)
                ds_ref[g, row:row+n] = (prob * (dp_ref[g, row:row+n] - delta)).astype(BF)
            dq = 0.0
            for src, dst in parts:
                dv_ref[src, lane:lane+pw] += nn(p_ref[g, dst], dos[g])
                dk_ref[src, lane:lane+pw] += nn(ds_ref[g, dst], qs[g])
                dq = dq + nn(kt_ref[lane:lane+pw, src], ds_ref[g, dst])
            outs.append(own_columns(dq, pair))
        out_ref[here, 0:w] = (jnp.concatenate(outs, 0) * HD ** -0.5).T.astype(BF)
    each_size(range_ref, t, body)
    @pl.when(t == pl.num_programs(0) - 1)
    def _():
        out_ref[:, w:2*w] = dk_ref[...].astype(BF)
        out_ref[:, 2*w:3*w] = dv_ref[...].astype(BF)
        pre_ref[0] = dk_ref[0:prefix, :]
        pre_ref[1] = dv_ref[0:prefix, :]

def score_scratch(n, w, kind):
    pair = min(2, w // HD)
    return pltpu.VMEM((w // HD // pair, n + TQ, pair*TQ), kind)

def whole(shape):
    return pl.BlockSpec(shape, lambda t, *_: (0,) * len(shape))

def attend(ranges, span, qkv, prefix, heads):
    n, w = qkv.shape[0], heads*HD
    return pl.pallas_call(
        partial(attn_fwd, prefix, heads),
        grid_spec=pltpu.PrefetchScalarGridSpec(
            num_scalar_prefetch=1, grid=(n//TQ,),
            in_specs=[pl.BlockSpec((2, TQ), lambda t, *_: (0, t)), whole(qkv.shape)],
            out_specs=[pl.BlockSpec((TQ, w), lambda t, *_: (t, 0)), pl.BlockSpec((heads, TQ), lambda t, *_: (0, t))],
            scratch_shapes=[pltpu.VMEM((w, n), BF), score_scratch(n, w, F32), score_scratch(n, w, BF)]),
        out_shape=[jax.ShapeDtypeStruct((n, w), BF), jax.ShapeDtypeStruct((heads, n), F32)],
        compiler_params=pltpu.CompilerParams(dimension_semantics=("arbitrary",), vmem_limit_bytes=VMEM), name="attend",
        cost_estimate=pl.CostEstimate(flops=2*n*n*w*2//4000, bytes_accessed=1, transcendentals=0),
    )(ranges, span, qkv)

def attend_back(ranges, span, qkv, lse, o, do, prefix, heads):
    n, w = qkv.shape[0], heads*HD
    tile = pl.BlockSpec((TQ, w), lambda t, *_: (t, 0))
    return pl.pallas_call(
        partial(attn_bwd, prefix, heads),
        grid_spec=pltpu.PrefetchScalarGridSpec(
            num_scalar_prefetch=1, grid=(n//TQ,),
            in_specs=[pl.BlockSpec((2, TQ), lambda t, *_: (0, t)), whole(qkv.shape),
                      pl.BlockSpec((heads, TQ), lambda t, *_: (0, t)), tile, tile],
            out_specs=[whole((n, 3*w)), whole((2, prefix, w))],
            scratch_shapes=[pltpu.VMEM((w, n), BF), pltpu.VMEM((n, w), F32), pltpu.VMEM((n, w), F32),
                score_scratch(n, w, F32), score_scratch(n, w, F32), score_scratch(n, w, BF), score_scratch(n, w, BF)]),
        out_shape=[jax.ShapeDtypeStruct((n, 3*w), BF), jax.ShapeDtypeStruct((2, prefix, w), F32)],
        compiler_params=pltpu.CompilerParams(dimension_semantics=("arbitrary",), vmem_limit_bytes=VMEM), name="attend_back",
        cost_estimate=pl.CostEstimate(flops=5*n*n*w*2//4000, bytes_accessed=1, transcendentals=0),
    )(ranges, span, qkv, lse, o, do)

def take_size(index):
    return sum(jnp.where(index == i, size, 0) for i, size in enumerate(SIZES))


def spans(lengths, length, prefix):
    ends = jnp.cumsum(lengths)
    starts = ends - lengths
    place = jnp.arange(prefix + length, dtype=jnp.int32) - prefix
    last = lengths.shape[0] - 1
    inside = (place[:, None] >= starts[None, :last]) & (place[:, None] < ends[None, :last])
    low = jnp.sum(jnp.where(inside, starts[None, :last] + prefix, 0), -1)
    high = jnp.sum(jnp.where(inside, ends[None, :last] + prefix, 0), -1)
    tl, th = low.reshape(-1, TQ), high.reshape(-1, TQ)
    tiles = (prefix + length) // TQ
    first = jnp.min(jnp.where(th > 0, tl, prefix + length), axis=1) // TQ
    size = (jnp.max(th, axis=1) + TQ - 1) // TQ - first
    index = jnp.sum((size[:, None] > jnp.array(SIZES)[None]).astype(jnp.int32), 1)
    first = jnp.minimum(first, tiles - take_size(index))
    return jnp.stack([first * TQ, index], 1).astype(jnp.int32), jnp.stack([low, high]).astype(jnp.int32)


def bell_parts(u):
    bell = jnp.exp(-0.5 * u * u)
    t = 1.0 / (1.0 + (0.3275911 * 0.5**0.5) * jnp.abs(u))
    tail = 1.061405429 * t - 1.453152027
    for k in (1.421413741, -0.284496736, 0.254829592):
        tail = tail * t + k
    tail = 0.5 * tail * t * bell
    return bell, jnp.where(u > 0, 1.0 - tail, tail)


def slope_of(u, bell, phi):
    return phi + u * (bell * 0.3989422804014327)


def feed_kernel(mode, cuts, refs):
    count = len(cuts)
    panels, refs = refs[: 2 * count], refs[2 * count :]
    (own_ref, other_ref), refs = refs[:2], refs[2:]
    biases = ()
    if mode != "back":
        biases, refs = refs[:count], refs[count:]
    if mode == "back":
        slope_ref, refs = refs[0], refs[1:]
    out_own_ref, out_other_ref, *kept, x_ref, acc_ref, u_ref, f_ref = refs
    step = 16
    rows = own_ref.shape[0]
    t = pl.program_id(0)

    @pl.when(t == 0)
    def _():
        x_ref[:rows] = own_ref[...]
        x_ref[rows:] = other_ref[...]
        acc_ref[...] = jnp.zeros_like(acc_ref)

    def run(k):
        up_ref, down_ref = panels[2 * k], panels[2 * k + 1]
        if mode == "forward":
            u_ref[...] = nn(x_ref[...], up_ref[...])
            bias = biases[k][...]
            for row in range(0, 2 * rows, step):
                at = slice(row, min(row + step, 2 * rows))
                u = u_ref[at] + bias
                bell, phi = bell_parts(u)
                kept[0][at] = slope_of(u, bell, phi).astype(BF)
                f_ref[at] = (u * phi).astype(BF)
            acc_ref[...] += nt(f_ref[...], down_ref[...])
        else:
            u_ref[...] = nn(x_ref[...], down_ref[...])
            for row in range(0, 2 * rows, step):
                at = slice(row, min(row + step, 2 * rows))
                f_ref[at] = (u_ref[at] * slope_ref[at].astype(F32)).astype(BF)
            acc_ref[...] += nt(f_ref[...], up_ref[...])

    for k, (first, last) in enumerate(cuts):
        if count == 1:
            run(k)
        else:
            pl.when((t >= first) & (t < last))(partial(run, k))

    @pl.when(t == pl.num_programs(0) - 1)
    def _():
        out_own_ref[...] = acc_ref[:rows]
        out_other_ref[...] = acc_ref[rows:].astype(BF)


def feed(mode, panels, own, other, biases=(), slopes=(), keep=False):
    rows, d = own.shape
    th = TH if all(units % TH == 0 for _, units in panels) else TH // 2
    specs, arrays, cuts, at = [], [], [], 0
    for panel, units in panels:
        steps = units // th
        low = partial(lambda at, steps, t: jnp.clip(t - at, 0, steps - 1), at, steps)
        if len(panels) == 1:
            low = lambda t: t
        specs.append(pl.BlockSpec((d, th), partial(lambda low, t: (0, low(t)), low)))
        specs.append(pl.BlockSpec((d, th), partial(lambda low, n, t: (0, n + low(t)), low, steps)))
        arrays += [panel, panel]
        cuts.append((at, at + steps))
        at += steps
    full = pl.BlockSpec((rows, d), lambda t: (0, 0))
    part = pl.BlockSpec((2 * rows, th), lambda t: (0, t))
    specs += [full, full]
    arrays += [own, other]
    if mode != "back":
        for k, bias in enumerate(biases):
            specs.append(pl.BlockSpec((1, th), specs[2 * k].index_map))
            arrays.append(bias)
    specs += [part] * len(slopes)
    arrays += list(slopes)
    outs = [jax.ShapeDtypeStruct((rows, d), F32), jax.ShapeDtypeStruct((rows, d), BF)]
    out_specs = [full, full]
    if keep:
        outs.append(jax.ShapeDtypeStruct((2 * rows, at * th), BF))
        out_specs.append(part)
    scratch = [pltpu.VMEM((2 * rows, d), BF), pltpu.VMEM((2 * rows, d), F32)]
    scratch += [pltpu.VMEM((2 * rows, th), F32), pltpu.VMEM((2 * rows, th), BF)]
    return pl.pallas_call(
        lambda *refs: feed_kernel(mode, cuts, refs),
        grid=(at,),
        in_specs=specs,
        out_specs=out_specs,
        out_shape=outs,
        scratch_shapes=scratch,
        compiler_params=pltpu.CompilerParams(
            dimension_semantics=("arbitrary",), vmem_limit_bytes=VMEM
        ),
        cost_estimate=pl.CostEstimate(
            flops=8 * rows * d * at * th // 4000,
            bytes_accessed=1,
            transcendentals=0,
        ),
        name="feed_" + mode,
    )(*arrays)


class Order:
    def __init__(self, place, prefix, rows):
        self.place, self.prefix, self.rows = place, prefix, rows
        self.length = prefix + place.mp * rows

    def start(self, j, i):
        place = self.place
        return self.prefix + ((place.c ^ i) * place.g + (place.p ^ j)) * self.rows

    def put(self, whole, block, j, i):
        return lax.dynamic_update_slice(whole, block, (self.start(j, i), 0))

    def get(self, whole, j, i):
        return lax.dynamic_slice(whole, (self.start(j, i), 0), (self.rows, whole.shape[1]))


def both_cores(place, mine, theirs):
    return mine + place.core(theirs).astype(F32)


def attention(place, order, blocks, weights, where):
    qkv_w, qkv_b, pre = weights
    prefix = order.prefix
    qkv = jnp.pad(
        jnp.concatenate([jnp.zeros_like(pre[0]), pre[0], pre[1]], axis=1),
        ((0, order.length - prefix), (0, 0)),
    )
    for (j, i), block in blocks.items():
        qkv = order.put(qkv, (nn(block, qkv_w) + qkv_b).astype(BF), j, i)
    return (qkv,) + tuple(attend(*where, qkv, prefix, qkv_w.shape[1] // 3 // HD))


def spread_rows(place, x_own):
    blocks = {}
    for j in range(place.g):
        blocks[j, 0] = x_own if j == 0 else place.chip(x_own, j)
        blocks[j, 1] = place.core(blocks[j, 0])
    return blocks


def out_parts(place, order, o):
    parts = [jnp.concatenate([order.get(o, j, i) for i in range(2)], 0) for j in range(place.g)]
    return [part if j == 0 else place.chip(part, j) for j, part in enumerate(parts)]


def out_project(place, order, x_own, parts, outs, fixed):
    mine = [0.0, 0.0]
    for j, part in enumerate(parts):
        for i in range(2):
            mine[i] = mine[i] + nt(part[i * order.rows : (i + 1) * order.rows], outs[j])
    a = x_own.astype(F32) + both_cores(place, mine[0], mine[1].astype(BF)) + fixed[0]
    x1 = norm_stats(a)[0] * fixed[2] + fixed[4]
    return a, x1


def out_back(place, order, dx1, a, outs, fixed):
    da = norm_back(a, dx1, fixed[2])
    low = da.astype(BF)
    both = jnp.concatenate([low, place.core(low)], 0)
    go = jnp.zeros((order.length, outs[0].shape[1]), BF)
    for j in range(place.g - 1, -1, -1):
        do = nn(both, outs[j]).astype(BF)
        do = do if j == 0 else place.chip(do, j)
        for i in range(2):
            go = order.put(go, do[i * order.rows : (i + 1) * order.rows], j, i)
    return da, go


def swap_add(value, bit):
    count = lax.axis_size("dp")
    return value + lax.ppermute(value, "dp", [(i, i ^ bit) for i in range(count)])


def input_back(place, order, da, back, qkv_w, kv=None):
    total, sent = da, []
    for j in range(place.g - 1, -1, -1):
        other = nt(order.get(back, j, 1), qkv_w).astype(BF)
        summed = both_cores(place, nt(order.get(back, j, 0), qkv_w), other)
        if j == 0:
            total = total + summed
        else:
            sent.append(place.chip(summed.astype(BF), j))
    if kv is not None:
        bit = 1
        while bit < lax.axis_size("dp"):
            kv = swap_add(kv, bit)
            bit *= 2
        sent = tie(sent, kv)
    for value in sent:
        total = total + value.astype(F32)
    return total.astype(BF) if kv is None else (total.astype(BF), kv)


def on_device(
    tokens,
    cotangent,
    lengths,
    qkv_weight,
    qkv_bias,
    out_weight,
    out_bias,
    up_weight,
    up_bias,
    down_weight,
    down_bias,
    norm_gain,
    norm_shift,
    prefix_keys,
    prefix_values,
):
    place = Place()
    g, mp, c, m, p = place.g, place.mp, place.c, place.m, place.p
    rows = tokens.shape[1]
    width, ff, dim = out_weight.shape[1], up_weight.shape[2], up_weight.shape[1]
    prefix = prefix_keys.shape[1]
    order = Order(place, prefix, rows)
    row_lengths = lax.dynamic_index_in_dim(lengths, m, 0, keepdims=False)[0]
    where = spans(row_lengths, mp * rows, prefix)
    fixed = jnp.concatenate([out_bias, down_bias, norm_gain[0], norm_shift[0]], 0)
    other = place.core(fixed)
    fixed = [jnp.where(c == 0, fixed, other), jnp.where(c == 0, other, fixed)]

    def own_rows(array):
        other = lax.dynamic_index_in_dim(array, 1 - m, 0, keepdims=False)[:, 0]
        same = lax.dynamic_index_in_dim(array, m, 0, keepdims=False)[:, 0]
        moved = place.send(other, lambda c, m, p: (c, 1 - m, p) if c == m else None)
        return jnp.where(c == m, same, moved)

    block = qkv_block(qkv_weight, qkv_bias, (prefix_keys, prefix_values))
    thin0 = merged(place, own_layer(place, 0, block))
    w0, qkv_b0, pre0 = cut_qkv(thin0, dim, prefix)
    w0 = gather(w0)
    raw = (out_weight, up_weight, up_bias, down_weight)

    def shard_of(l, *after):
        held = tie(raw, *after)
        return own_shard(place, l, *held)

    shard0 = merged(place, shard_of(0, thin0))
    shards0 = [shard0] + [place.chip(shard0, j) for j in range(1, g)]
    thin1 = merged(place, own_layer(place, 1, tie(block, shard0)))
    w1, qkv_b1, pre1 = cut_qkv(thin1, dim, prefix)

    def panel_of(shards, *more):
        cuts = [cut_shard(v, dim, ff) for v in shards]
        parts = [v[k] for k in range(3) for v in cuts] + list(more)
        return jnp.concatenate(parts, axis=1), jnp.concatenate([v[3] for v in cuts])[None]

    def outs_of(panel, count):
        start = 2 * count * ff
        return [panel[:, start + j * width : start + (j + 1) * width] for j in range(count)]

    part_a, bias_a = panel_of(shards0[:1])
    panel_a = gather(tie(part_a, w0))
    x = own_rows(tie(tokens, thin1))
    part_b, bias_b = panel_of(shards0[1:], w1)
    panel_b = gather(tie(part_b, panel_a, x))
    shard1 = shard_of(1, x)
    blocks = spread_rows(place, x)
    qkv0, o0, lse0 = attention(place, order, blocks, (w0, qkv_b0, pre0), where)
    parts = out_parts(place, order, o0)
    shard1 = merged(place, tie(shard1, blocks))
    shards1 = [shard1] + [place.chip(shard1, j) for j in range(1, g)]
    second, bias1 = panel_of(tie(shards1, o0))
    panel1 = gather(tie(second, panel_b))
    grad = own_rows(tie(cotangent, second))
    panels0 = [(panel_a, ff), (panel_b, (g - 1) * ff)]
    panels1 = [(panel1, g * ff)]

    w1 = panel_b[:, (g - 1) * (2 * ff + width) :]
    outs = [outs_of(panel_a, 1) + outs_of(tie(panel_b, parts), g - 1), outs_of(panel1, g)]
    a0, x1 = out_project(place, order, x, parts, outs[0], fixed[0])
    low = x1.astype(BF)
    mine, theirs, slope0 = feed(
        "forward", panels0, low, place.core(low), [bias_a, bias_b], keep=True
    )
    z0 = x1 + both_cores(place, mine, theirs) + fixed[0][1]
    y0 = (norm_stats(z0)[0] * fixed[0][3] + fixed[0][5]).astype(BF)

    def home(value, l, half):
        return place.send(value, lambda c, m, p: (l, c, p) if m == half else None)

    blocks = tie(spread_rows(place, y0), grad)
    results0 = [home(tie(y0, blocks), 0, h) for h in range(2)]
    qkv1, o1, lse1 = attention(place, order, blocks, (w1, qkv_b1, pre1), where)
    a1, x1 = out_project(place, order, y0, out_parts(place, order, tie(o1, results0)), outs[1], fixed[1])
    low = x1.astype(BF)
    mine, theirs, slope1 = feed("forward", panels1, low, place.core(low), [bias1], keep=True)
    z1 = x1 + both_cores(place, mine, theirs) + fixed[1][1]
    y1 = (norm_stats(z1)[0] * fixed[1][3] + fixed[1][5]).astype(BF)

    dz = norm_back(z1, grad.astype(F32), fixed[1][3])
    low = dz.astype(BF)
    mine, theirs = feed("back", panels1, low, place.core(low), slopes=[slope1])
    dx1 = dz + both_cores(place, mine, theirs)

    first = m == 0
    da, go = out_back(place, order, dx1, a1, outs[1], fixed[1])
    results1 = [home(tie(y1, go), 1, h) for h in range(2)]
    back, kv1 = attend_back(*where, qkv1, lse1, o1, go, prefix, width // HD)
    back = tie(back, results1)
    grad1 = input_back(place, order, da, back, w1)

    dz = norm_back(z0, grad1.astype(F32), fixed[0][3])
    low = dz.astype(BF)
    mine, theirs = feed("back", panels0, low, place.core(low), slopes=[slope0])
    dx1 = dz + both_cores(place, mine, theirs)
    da, go = out_back(place, order, dx1, a0, outs[0], fixed[0])
    gouts = [home(tie(grad1, go), 1, h) for h in range(2)]
    back, kv0 = attend_back(*where, qkv0, lse0, o0, go, prefix, width // HD)
    back = tie(back, gouts)
    grad0, kv = input_back(place, order, da, back, w0, jnp.stack([kv0, kv1]))
    gouts = [gouts[h] + home(grad0, 0, h) for h in range(2)]
    kv = place.send(jnp.where(first, kv[0], kv[1]), lambda c, m, p: (m, c, p)) + place.send(
        jnp.where(first, kv[1], kv[0]), lambda c, m, p: (1 - m, c, p)
    )
    results = jnp.stack([results0[h] + results1[h] for h in range(2)])[:, :, None]
    gouts = jnp.stack(gouts)[:, :, None]
    return results[None], gouts[None], kv[None, 0], kv[None, 1]


def solution(mesh):
    placed = (
        P(None, "mp", "dp", None),
        P(None, "mp", "dp", None),
        P(None, "dp", None),
        P("section", None, "dp", "mp"),
        P("section", None, "mp"),
        P("section", "mp", "dp"),
        P("section", None),
        P("section", "dp", "mp"),
        P("section", "mp"),
        P("section", "mp", "dp"),
        P("section", None),
        P("section", None, None),
        P("section", None, None),
        P("section", None, "mp"),
        P("section", None, "mp"),
    )
    return jax.shard_map(
        on_device,
        mesh=mesh,
        in_specs=placed,
        out_specs=(
            P("section", None, "mp", "dp", None),
            P("section", None, "mp", "dp", None),
            P("section", None, "mp"),
            P("section", None, "mp"),
        ),
        check_vma=False,
    )
```

```python
from functools import partial

import jax
import jax.numpy as jnp
from jax import lax
from jax.experimental import pallas as pl
from jax.experimental.pallas import tpu as pltpu
from jax.sharding import PartitionSpec as P

HEADS = 16
HD = 64
EPS = 1e-5
BF = jnp.bfloat16
F32 = jnp.float32
TQ = 128
CK = 256
KC = 64
SIZES = (2, 3, 4, 5, 6, 7, 8, 10)
TH = 512
VMEM = 48 << 20


def dot(a, b, dims):
    return lax.dot_general(a, b, (dims, ((), ())), preferred_element_type=F32)


def nn(a, b):
    return dot(a, b, ((1,), (0,)))


def nt(a, b):
    return dot(a, b, ((1,), (1,)))


def norm_stats(v):
    centred = v - jnp.mean(v, axis=-1, keepdims=True)
    inv = lax.rsqrt(jnp.mean(centred * centred, axis=-1, keepdims=True) + EPS)
    return centred * inv, inv


def norm_back(v, grad, gain):
    n, inv = norm_stats(v)
    e = grad * gain
    return inv * (e - jnp.mean(e, -1, keepdims=True) - n * jnp.mean(e * n, -1, keepdims=True))


class Place:
    def __init__(self):
        self.mp = lax.axis_size("mp")
        self.g = self.mp // 2
        self.c = lax.axis_index("section")
        self.z = lax.axis_index("mp")
        self.m = self.z // self.g
        self.p = self.z % self.g

    def send(self, value, route):
        pairs = []
        for c in range(2):
            for m in range(2):
                for p in range(self.g):
                    to = route(c, m, p)
                    if to is not None:
                        source = c * self.mp + m * self.g + p
                        pairs.append((source, to[0] * self.mp + to[1] * self.g + to[2]))
        return lax.ppermute(value, ("section", "mp"), pairs)

    def core(self, value):
        return lax.ppermute(value, "section", [(0, 1), (1, 0)])

    def chip(self, value, j):
        return lax.ppermute(value, "mp", [(z, z ^ j) for z in range(self.mp)])


def tie(value, *after):
    return lax.optimization_barrier((value,) + after)[0]


def high_low(v):
    high = v.astype(BF)
    return high, (v - high.astype(F32)).astype(BF)


def gather(block):
    return lax.all_gather(block, "dp", axis=0, tiled=True)


def own_layer(place, l, block):
    return [place.send(block, lambda c, m, p: (m, half, p) if c == l else None) for half in range(2)]


def merged(place, got):
    return jnp.where(place.m == 0, got[0], got[1])


def qkv_block(qkv, qkv_bias, pre):
    weight = qkv[0].astype(BF).transpose(1, 0, 2).reshape(qkv.shape[2], -1)
    width = weight.shape[1]
    bias = jnp.stack(high_low(qkv_bias[0].reshape(-1)))
    pre = jnp.concatenate([v[0].astype(BF) for v in pre], axis=1)
    pre = jnp.pad(pre, ((0, 0), (0, width - pre.shape[1])))
    return jnp.concatenate([weight, pre, jnp.pad(bias, ((0, 14), (0, 0)))], axis=0)


def cut_qkv(v, rows, prefix):
    third = v.shape[1] // 3
    bias = v[rows + prefix].astype(F32) + v[rows + prefix + 1].astype(F32)
    pre = v[rows : rows + prefix]
    return v[:rows], bias, (pre[:, :third], pre[:, third : 2 * third])


def own_shard(place, l, out, up, up_bias, down):
    parts = [up[0].astype(BF), down[0].astype(BF).T, out[0].astype(BF).T]
    block = jnp.concatenate(parts[: 3 - l], axis=1)
    bias = jnp.stack(high_low(up_bias[0]))
    bias = jnp.pad(bias, ((0, 14), (0, block.shape[1] - bias.shape[1])))
    block = jnp.concatenate([block, bias], 0)
    return own_layer(place, l, block)


def cut_shard(shard, rows, ff):
    bias = shard[rows : rows + 2, :ff].astype(F32)
    shard = shard[:rows]
    return shard[:, :ff], shard[:, ff : 2 * ff], shard[:, 2 * ff :], bias[0] + bias[1]


def spread_heads(block, heads):
    if heads == 1:
        return block
    lane = lax.broadcasted_iota(jnp.int32, block.shape, 1) // HD
    return jnp.concatenate([jnp.where(lane == h, block, jnp.zeros_like(block)) for h in range(heads)], 0)

def own_columns(wide, heads):
    return jnp.concatenate([wide[h*HD:(h+1)*HD, h*TQ:(h+1)*TQ] for h in range(heads)], 0)

def widen(mask, heads):
    return mask if heads == 1 else jnp.concatenate([mask] * heads, axis=1)

def each_size(range_ref, t, body):
    for index, size in enumerate(SIZES):
        @pl.when(range_ref[t, 1] == index)
        def _():
            body(pl.multiple_of(range_ref[t, 0], TQ), size * TQ)

def pieces(prefix, start, size):
    out = [(r, r, KC, False) for r in range(0, prefix, KC)]
    return out + [(prefix + r, start + r, KC, True) for r in range(0, size, KC)]

def piece_mask(first, span_ref, heads):
    key = lax.broadcasted_iota(jnp.int32, (KC, TQ), 0) + first
    return widen((key >= span_ref[0:1, :]) & (key < span_ref[1:2, :]), heads)

def attn_fwd(prefix, heads, range_ref, span_ref, qkv_ref, o_ref, lse_ref, vt_ref, s_ref, p_ref):
    w = heads * HD
    pair = min(2, heads)
    pw = pair * HD
    t = pl.program_id(0)
    @pl.when(t == 0)
    def _():
        for i in range(vt_ref.shape[1] // CK):
            at = slice(i * CK, (i + 1) * CK)
            vt_ref[:, at] = qkv_ref[at, 2*w:3*w].astype(F32).T.astype(BF)
    def body(start, size):
        here = pl.ds(pl.multiple_of(t*TQ, TQ), TQ)
        at = pl.ds(start, size)
        outs = []
        lanes = range(0, w, pw)
        for g, lane in enumerate(lanes):
            q = spread_heads(qkv_ref[here, lane:lane+pw] * BF(HD ** -0.5), pair)
            s_ref[g, 0:prefix] = nt(qkv_ref[0:prefix, w+lane:w+lane+pw], q)
            s_ref[g, prefix:prefix+size] = nt(qkv_ref[at, w+lane:w+lane+pw], q)
        for g, lane in enumerate(lanes):
            peak = jnp.full((8, pair*TQ), -1e30, F32)
            for row, first, n, masked in pieces(prefix, start, size):
                s = s_ref[g, row:row+n]
                if masked:
                    s = jnp.where(piece_mask(first, span_ref, pair), s, -1e30)
                    s_ref[g, row:row+n] = s
                peak = jnp.maximum(peak, jnp.max(s.reshape(n//8, 8, -1), axis=0))
            peak = jnp.max(peak, axis=0, keepdims=True)
            total = jnp.zeros((8, pair*TQ), F32)
            for row, first, n, masked in pieces(prefix, start, size):
                e = jnp.exp(s_ref[g, row:row+n] - peak)
                p_ref[g, row:row+n] = e.astype(BF)
                total = total + jnp.sum(e.reshape(n//8, 8, -1), axis=0)
            total = jnp.sum(total, axis=0, keepdims=True)
            acc = nn(vt_ref[lane:lane+pw, 0:prefix], p_ref[g, 0:prefix]) + nn(vt_ref[lane:lane+pw, at], p_ref[g, prefix:prefix+size])
            outs.append(own_columns(acc * (1.0 / total), pair))
            lse = peak + jnp.log(total)
            for h in range(pair):
                row = lane // HD + h
                lse_ref[row:row+1, :] = lse[:, h*TQ:(h+1)*TQ]
        o_ref[...] = jnp.concatenate(outs, 0).T.astype(BF)
    each_size(range_ref, t, body)

def attn_bwd(prefix, heads, range_ref, span_ref, qkv_ref, lse_ref, o_ref, do_ref, out_ref, pre_ref,
             kt_ref, dk_ref, dv_ref, s_ref, dp_ref, p_ref, ds_ref):
    w = heads * HD
    pair = min(2, heads)
    pw = pair * HD
    t = pl.program_id(0)
    @pl.when(t == 0)
    def _():
        for i in range(kt_ref.shape[1] // CK):
            at = slice(i * CK, (i + 1) * CK)
            kt_ref[:, at] = qkv_ref[at, w:2*w].astype(F32).T.astype(BF)
        dk_ref[...] = jnp.zeros_like(dk_ref)
        dv_ref[...] = jnp.zeros_like(dv_ref)
    def body(start, size):
        here = pl.ds(pl.multiple_of(t*TQ, TQ), TQ)
        both = (do_ref[...].astype(F32) * o_ref[...].astype(F32)).T
        outs = []
        at = pl.ds(start, size)
        parts = ((slice(0, prefix), slice(0, prefix)), (at, slice(prefix, prefix+size)))
        lanes = range(0, w, pw)
        qs, dos = [], []
        for g, lane in enumerate(lanes):
            q = spread_heads(qkv_ref[here, lane:lane+pw] * BF(HD ** -0.5), pair)
            do = spread_heads(do_ref[:, lane:lane+pw], pair)
            qs.append(q)
            dos.append(do)
            for src, dst in parts:
                s_ref[g, dst] = nt(qkv_ref[src, w+lane:w+lane+pw], q)
                dp_ref[g, dst] = nt(qkv_ref[src, 2*w+lane:2*w+lane+pw], do)
        for g, lane in enumerate(lanes):
            rows = range(lane // HD, lane // HD + pair)
            delta = jnp.concatenate([jnp.sum(both[h*HD:(h+1)*HD], axis=0, keepdims=True) for h in rows], 1)
            lse = jnp.concatenate([lse_ref[h:h+1, :] for h in rows], 1)
            for row, first, n, masked in pieces(prefix, start, size):
                prob = jnp.exp(s_ref[g, row:row+n] - lse)
                if masked:
                    prob = jnp.where(piece_mask(first, span_ref, pair), prob, 0.0)
                p_ref[g, row:row+n] = prob.astype(BF)
                ds_ref[g, row:row+n] = (prob * (dp_ref[g, row:row+n] - delta)).astype(BF)
            dq = 0.0
            for src, dst in parts:
                dv_ref[src, lane:lane+pw] += nn(p_ref[g, dst], dos[g])
                dk_ref[src, lane:lane+pw] += nn(ds_ref[g, dst], qs[g])
                dq = dq + nn(kt_ref[lane:lane+pw, src], ds_ref[g, dst])
            outs.append(own_columns(dq, pair))
        out_ref[here, 0:w] = (jnp.concatenate(outs, 0) * HD ** -0.5).T.astype(BF)
    each_size(range_ref, t, body)
    @pl.when(t == pl.num_programs(0) - 1)
    def _():
        out_ref[:, w:2*w] = dk_ref[...].astype(BF)
        out_ref[:, 2*w:3*w] = dv_ref[...].astype(BF)
        pre_ref[0] = dk_ref[0:prefix, :]
        pre_ref[1] = dv_ref[0:prefix, :]

def score_scratch(n, w, kind):
    pair = min(2, w // HD)
    return pltpu.VMEM((w // HD // pair, n + TQ, pair*TQ), kind)

def whole(shape):
    return pl.BlockSpec(shape, lambda t, *_: (0,) * len(shape))

def attend(ranges, span, qkv, prefix, heads):
    n, w = qkv.shape[0], heads*HD
    return pl.pallas_call(
        partial(attn_fwd, prefix, heads),
        grid_spec=pltpu.PrefetchScalarGridSpec(
            num_scalar_prefetch=1, grid=(n//TQ,),
            in_specs=[pl.BlockSpec((2, TQ), lambda t, *_: (0, t)), whole(qkv.shape)],
            out_specs=[pl.BlockSpec((TQ, w), lambda t, *_: (t, 0)), pl.BlockSpec((heads, TQ), lambda t, *_: (0, t))],
            scratch_shapes=[pltpu.VMEM((w, n), BF), score_scratch(n, w, F32), score_scratch(n, w, BF)]),
        out_shape=[jax.ShapeDtypeStruct((n, w), BF), jax.ShapeDtypeStruct((heads, n), F32)],
        compiler_params=pltpu.CompilerParams(dimension_semantics=("arbitrary",), vmem_limit_bytes=VMEM), name="attend",
        cost_estimate=pl.CostEstimate(flops=2*n*n*w*2//4000, bytes_accessed=1, transcendentals=0),
    )(ranges, span, qkv)

def attend_back(ranges, span, qkv, lse, o, do, prefix, heads):
    n, w = qkv.shape[0], heads*HD
    tile = pl.BlockSpec((TQ, w), lambda t, *_: (t, 0))
    return pl.pallas_call(
        partial(attn_bwd, prefix, heads),
        grid_spec=pltpu.PrefetchScalarGridSpec(
            num_scalar_prefetch=1, grid=(n//TQ,),
            in_specs=[pl.BlockSpec((2, TQ), lambda t, *_: (0, t)), whole(qkv.shape),
                      pl.BlockSpec((heads, TQ), lambda t, *_: (0, t)), tile, tile],
            out_specs=[whole((n, 3*w)), whole((2, prefix, w))],
            scratch_shapes=[pltpu.VMEM((w, n), BF), pltpu.VMEM((n, w), F32), pltpu.VMEM((n, w), F32),
                score_scratch(n, w, F32), score_scratch(n, w, F32), score_scratch(n, w, BF), score_scratch(n, w, BF)]),
        out_shape=[jax.ShapeDtypeStruct((n, 3*w), BF), jax.ShapeDtypeStruct((2, prefix, w), F32)],
        compiler_params=pltpu.CompilerParams(dimension_semantics=("arbitrary",), vmem_limit_bytes=VMEM), name="attend_back",
        cost_estimate=pl.CostEstimate(flops=5*n*n*w*2//4000, bytes_accessed=1, transcendentals=0),
    )(ranges, span, qkv, lse, o, do)

def take_size(index):
    return sum(jnp.where(index == i, size, 0) for i, size in enumerate(SIZES))


def spans(lengths, length, prefix):
    ends = jnp.cumsum(lengths)
    starts = ends - lengths
    place = jnp.arange(prefix + length, dtype=jnp.int32) - prefix
    last = lengths.shape[0] - 1
    inside = (place[:, None] >= starts[None, :last]) & (place[:, None] < ends[None, :last])
    low = jnp.sum(jnp.where(inside, starts[None, :last] + prefix, 0), -1)
    high = jnp.sum(jnp.where(inside, ends[None, :last] + prefix, 0), -1)
    tl, th = low.reshape(-1, TQ), high.reshape(-1, TQ)
    tiles = (prefix + length) // TQ
    first = jnp.min(jnp.where(th > 0, tl, prefix + length), axis=1) // TQ
    size = (jnp.max(th, axis=1) + TQ - 1) // TQ - first
    index = jnp.sum((size[:, None] > jnp.array(SIZES)[None]).astype(jnp.int32), 1)
    first = jnp.minimum(first, tiles - take_size(index))
    return jnp.stack([first * TQ, index], 1).astype(jnp.int32), jnp.stack([low, high]).astype(jnp.int32)


def bell_parts(u):
    bell = jnp.exp(-0.5 * u * u)
    t = 1.0 / (1.0 + (0.3275911 * 0.5**0.5) * jnp.abs(u))
    tail = 1.061405429 * t - 1.453152027
    for k in (1.421413741, -0.284496736, 0.254829592):
        tail = tail * t + k
    tail = 0.5 * tail * t * bell
    return bell, jnp.where(u > 0, 1.0 - tail, tail)


def slope_of(u, bell, phi):
    return phi + u * (bell * 0.3989422804014327)


def feed_kernel(mode, cuts, refs):
    count = len(cuts)
    panels, refs = refs[: 2 * count], refs[2 * count :]
    (own_ref, other_ref), refs = refs[:2], refs[2:]
    biases = ()
    if mode != "back":
        biases, refs = refs[:count], refs[count:]
    if mode == "back":
        slope_ref, refs = refs[0], refs[1:]
    out_own_ref, out_other_ref, *kept, x_ref, acc_ref, u_ref, f_ref = refs
    step = 16
    rows = own_ref.shape[0]
    t = pl.program_id(0)

    @pl.when(t == 0)
    def _():
        x_ref[:rows] = own_ref[...]
        x_ref[rows:] = other_ref[...]
        acc_ref[...] = jnp.zeros_like(acc_ref)

    def run(k):
        up_ref, down_ref = panels[2 * k], panels[2 * k + 1]
        if mode == "forward":
            u_ref[...] = nn(x_ref[...], up_ref[...])
            bias = biases[k][...]
            for row in range(0, 2 * rows, step):
                at = slice(row, min(row + step, 2 * rows))
                u = u_ref[at] + bias
                bell, phi = bell_parts(u)
                kept[0][at] = slope_of(u, bell, phi).astype(BF)
                f_ref[at] = (u * phi).astype(BF)
            acc_ref[...] += nt(f_ref[...], down_ref[...])
        else:
            u_ref[...] = nn(x_ref[...], down_ref[...])
            for row in range(0, 2 * rows, step):
                at = slice(row, min(row + step, 2 * rows))
                f_ref[at] = (u_ref[at] * slope_ref[at].astype(F32)).astype(BF)
            acc_ref[...] += nt(f_ref[...], up_ref[...])

    for k, (first, last) in enumerate(cuts):
        if count == 1:
            run(k)
        else:
            pl.when((t >= first) & (t < last))(partial(run, k))

    @pl.when(t == pl.num_programs(0) - 1)
    def _():
        out_own_ref[...] = acc_ref[:rows]
        out_other_ref[...] = acc_ref[rows:].astype(BF)


def feed(mode, panels, own, other, biases=(), slopes=(), keep=False):
    rows, d = own.shape
    th = TH if all(units % TH == 0 for _, units in panels) else TH // 2
    specs, arrays, cuts, at = [], [], [], 0
    for panel, units in panels:
        steps = units // th
        low = partial(lambda at, steps, t: jnp.clip(t - at, 0, steps - 1), at, steps)
        if len(panels) == 1:
            low = lambda t: t
        specs.append(pl.BlockSpec((d, th), partial(lambda low, t: (0, low(t)), low)))
        specs.append(pl.BlockSpec((d, th), partial(lambda low, n, t: (0, n + low(t)), low, steps)))
        arrays += [panel, panel]
        cuts.append((at, at + steps))
        at += steps
    full = pl.BlockSpec((rows, d), lambda t: (0, 0))
    part = pl.BlockSpec((2 * rows, th), lambda t: (0, t))
    specs += [full, full]
    arrays += [own, other]
    if mode != "back":
        for k, bias in enumerate(biases):
            specs.append(pl.BlockSpec((1, th), specs[2 * k].index_map))
            arrays.append(bias)
    specs += [part] * len(slopes)
    arrays += list(slopes)
    outs = [jax.ShapeDtypeStruct((rows, d), F32), jax.ShapeDtypeStruct((rows, d), BF)]
    out_specs = [full, full]
    if keep:
        outs.append(jax.ShapeDtypeStruct((2 * rows, at * th), BF))
        out_specs.append(part)
    scratch = [pltpu.VMEM((2 * rows, d), BF), pltpu.VMEM((2 * rows, d), F32)]
    scratch += [pltpu.VMEM((2 * rows, th), F32), pltpu.VMEM((2 * rows, th), BF)]
    return pl.pallas_call(
        lambda *refs: feed_kernel(mode, cuts, refs),
        grid=(at,),
        in_specs=specs,
        out_specs=out_specs,
        out_shape=outs,
        scratch_shapes=scratch,
        compiler_params=pltpu.CompilerParams(
            dimension_semantics=("arbitrary",), vmem_limit_bytes=VMEM
        ),
        cost_estimate=pl.CostEstimate(
            flops=8 * rows * d * at * th // 4000,
            bytes_accessed=1,
            transcendentals=0,
        ),
        name="feed_" + mode,
    )(*arrays)


class Order:
    def __init__(self, place, prefix, rows):
        self.place, self.prefix, self.rows = place, prefix, rows
        self.length = prefix + place.mp * rows

    def start(self, j, i):
        place = self.place
        return self.prefix + ((place.c ^ i) * place.g + (place.p ^ j)) * self.rows

    def put(self, whole, block, j, i):
        return lax.dynamic_update_slice(whole, block, (self.start(j, i), 0))

    def get(self, whole, j, i):
        return lax.dynamic_slice(whole, (self.start(j, i), 0), (self.rows, whole.shape[1]))


def both_cores(place, mine, theirs):
    return mine + place.core(theirs).astype(F32)


def attention(place, order, blocks, weights, where):
    qkv_w, qkv_b, pre = weights
    prefix = order.prefix
    qkv = jnp.pad(
        jnp.concatenate([jnp.zeros_like(pre[0]), pre[0], pre[1]], axis=1),
        ((0, order.length - prefix), (0, 0)),
    )
    for (j, i), block in blocks.items():
        qkv = order.put(qkv, (nn(block, qkv_w) + qkv_b).astype(BF), j, i)
    return (qkv,) + tuple(attend(*where, qkv, prefix, qkv_w.shape[1] // 3 // HD))


def spread_rows(place, x_own):
    blocks = {}
    for j in range(place.g):
        blocks[j, 0] = x_own if j == 0 else place.chip(x_own, j)
        blocks[j, 1] = place.core(blocks[j, 0])
    return blocks


def out_parts(place, order, o):
    parts = [jnp.concatenate([order.get(o, j, i) for i in range(2)], 0) for j in range(place.g)]
    return [part if j == 0 else place.chip(part, j) for j, part in enumerate(parts)]


def out_project(place, order, x_own, parts, outs, fixed):
    mine = [0.0, 0.0]
    for j, part in enumerate(parts):
        for i in range(2):
            mine[i] = mine[i] + nt(part[i * order.rows : (i + 1) * order.rows], outs[j])
    a = x_own.astype(F32) + both_cores(place, mine[0], mine[1].astype(BF)) + fixed[0]
    x1 = norm_stats(a)[0] * fixed[2] + fixed[4]
    return a, x1


def out_back(place, order, dx1, a, outs, fixed):
    da = norm_back(a, dx1, fixed[2])
    low = da.astype(BF)
    both = jnp.concatenate([low, place.core(low)], 0)
    go = jnp.zeros((order.length, outs[0].shape[1]), BF)
    for j in range(place.g - 1, -1, -1):
        do = nn(both, outs[j]).astype(BF)
        do = do if j == 0 else place.chip(do, j)
        for i in range(2):
            go = order.put(go, do[i * order.rows : (i + 1) * order.rows], j, i)
    return da, go


def total_dp(value):
    count, low = lax.axis_size("dp"), value.astype(BF)
    terms = [low] + [
        lax.ppermute(low, "dp", [(i, i ^ x) for i in range(count)]) for x in range(1, count)
    ]
    terms = [term.astype(F32) for term in terms]
    while len(terms) > 1:
        terms = [terms[i] + terms[i + 1] for i in range(0, len(terms), 2)]
    return terms[0]


def input_back(place, order, da, back, qkv_w, kv=None):
    total, sent = da, []
    for j in range(place.g - 1, -1, -1):
        other = nt(order.get(back, j, 1), qkv_w).astype(BF)
        summed = both_cores(place, nt(order.get(back, j, 0), qkv_w), other)
        if j == 0:
            total = total + summed
        else:
            sent.append(place.chip(summed.astype(BF), j))
    if kv is not None:
        kv = total_dp(kv)
        first = place.m == 0
        kv = place.send(jnp.where(first, kv[0], kv[1]), lambda c, m, p: (m, c, p)) + place.send(
            jnp.where(first, kv[1], kv[0]), lambda c, m, p: (1 - m, c, p)
        )
        sent = tie(sent, kv)
    for value in sent:
        total = total + value.astype(F32)
    return total.astype(BF) if kv is None else (total.astype(BF), kv)


def on_device(
    tokens,
    cotangent,
    lengths,
    qkv_weight,
    qkv_bias,
    out_weight,
    out_bias,
    up_weight,
    up_bias,
    down_weight,
    down_bias,
    norm_gain,
    norm_shift,
    prefix_keys,
    prefix_values,
):
    place = Place()
    g, mp, c, m, p = place.g, place.mp, place.c, place.m, place.p
    rows = tokens.shape[1]
    width, ff, dim = out_weight.shape[1], up_weight.shape[2], up_weight.shape[1]
    prefix = prefix_keys.shape[1]
    order = Order(place, prefix, rows)
    row_lengths = lax.dynamic_index_in_dim(lengths, m, 0, keepdims=False)[0]
    where = spans(row_lengths, mp * rows, prefix)
    fixed = jnp.concatenate([out_bias, down_bias, norm_gain[0], norm_shift[0]], 0)
    other = place.core(fixed)
    fixed = [jnp.where(c == 0, fixed, other), jnp.where(c == 0, other, fixed)]

    def own_rows(array):
        other = lax.dynamic_index_in_dim(array, 1 - m, 0, keepdims=False)[:, 0]
        same = lax.dynamic_index_in_dim(array, m, 0, keepdims=False)[:, 0]
        moved = place.send(other, lambda c, m, p: (c, 1 - m, p) if c == m else None)
        return jnp.where(c == m, same, moved)

    block = qkv_block(qkv_weight, qkv_bias, (prefix_keys, prefix_values))
    thin0 = merged(place, own_layer(place, 0, block))
    w0, qkv_b0, pre0 = cut_qkv(thin0, dim, prefix)
    w0 = gather(w0)
    raw = (out_weight, up_weight, up_bias, down_weight)

    def shard_of(l, *after):
        held = tie(raw, *after)
        return own_shard(place, l, *held)

    shard0 = merged(place, shard_of(0, thin0))
    extra = jnp.pad(out_weight[0].astype(BF).T, ((0, block.shape[0] - dim), (0, 0)))
    wide = jnp.concatenate([block, extra], axis=1)
    thin1 = merged(place, own_layer(place, 1, tie(wide, shard0)))
    w1, qkv_b1, pre1 = cut_qkv(thin1[:, : 3 * width], dim, prefix)
    out1 = thin1[:dim, 3 * width :]
    outs1 = [out1] + [place.chip(out1, j) for j in range(1, g)]

    def panel_of(shards, kinds, *more):
        cuts = [cut_shard(v, dim, ff) for v in shards]
        parts = [v[k] for k in range(kinds) for v in cuts] + list(more)
        return jnp.concatenate(parts, axis=1), jnp.concatenate([v[3] for v in cuts])[None]

    def outs_of(panel, start, count):
        return [panel[:, start + j * width : start + (j + 1) * width] for j in range(count)]

    part_a, bias_a = panel_of([shard0], 3)
    panel_a = gather(tie(part_a, w0))
    x = own_rows(tie(tokens, thin1))
    shards0 = [place.chip(tie(shard0, thin1), j) for j in range(1, g)]
    part_b, bias_b = panel_of(shards0, 3, w1, *outs1)
    panel_b = gather(tie(part_b, panel_a, x))
    shard1 = shard_of(1, x)
    blocks = spread_rows(place, x)
    qkv0, o0, lse0 = attention(place, order, blocks, (w0, qkv_b0, pre0), where)
    parts = out_parts(place, order, o0)
    shard1 = merged(place, tie(shard1, blocks))
    shards1 = [shard1] + [place.chip(shard1, j) for j in range(1, g)]
    second, bias1 = panel_of(tie(shards1, parts), 2)
    panel1 = gather(tie(second, panel_b))
    panels0 = [(panel_a, ff), (panel_b, (g - 1) * ff)]
    panels1 = [(panel1, g * ff)]

    at = (g - 1) * (2 * ff + width)
    w1 = panel_b[:, at : at + 3 * width]
    outs = [
        outs_of(panel_a, 2 * ff, 1) + outs_of(tie(panel_b, parts), 2 * (g - 1) * ff, g - 1),
        outs_of(panel_b, at + 3 * width, g),
    ]
    a0, x1 = out_project(place, order, x, parts, outs[0], fixed[0])
    low = x1.astype(BF)
    mine, theirs, slope0 = feed(
        "forward", panels0, low, place.core(low), [bias_a, bias_b], keep=True
    )
    grad = own_rows(tie(cotangent, low))
    mine = tie(mine, grad)
    z0 = x1 + both_cores(place, mine, theirs) + fixed[0][1]
    y0 = (norm_stats(z0)[0] * fixed[0][3] + fixed[0][5]).astype(BF)

    def home(value, l, half):
        return place.send(value, lambda c, m, p: (l, c, p) if m == half else None)

    blocks = spread_rows(place, y0)
    results0 = [home(tie(y0, blocks), 0, h) for h in range(2)]
    qkv1, o1, lse1 = attention(place, order, blocks, (w1, qkv_b1, pre1), where)
    a1, x1 = out_project(place, order, y0, out_parts(place, order, tie(o1, results0)), outs[1], fixed[1])
    low = x1.astype(BF)
    mine, theirs, slope1 = feed("forward", panels1, low, place.core(low), [bias1], keep=True)
    z1 = x1 + both_cores(place, mine, theirs) + fixed[1][1]
    y1 = (norm_stats(z1)[0] * fixed[1][3] + fixed[1][5]).astype(BF)

    dz = norm_back(z1, grad.astype(F32), fixed[1][3])
    low = dz.astype(BF)
    mine, theirs = feed("back", panels1, low, place.core(low), slopes=[slope1])
    dx1 = dz + both_cores(place, mine, theirs)

    da, go = out_back(place, order, dx1, a1, outs[1], fixed[1])
    results1 = [home(tie(y1, go), 1, h) for h in range(2)]
    back, kv1 = attend_back(*where, qkv1, lse1, o1, go, prefix, width // HD)
    back = tie(back, results1)
    grad1 = input_back(place, order, da, back, w1)

    dz = norm_back(z0, grad1.astype(F32), fixed[0][3])
    low = dz.astype(BF)
    mine, theirs = feed("back", panels0, low, place.core(low), slopes=[slope0])
    dx1 = dz + both_cores(place, mine, theirs)
    da, go = out_back(place, order, dx1, a0, outs[0], fixed[0])
    gouts = [home(tie(grad1, go), 1, h) for h in range(2)]
    back, kv0 = attend_back(*where, qkv0, lse0, o0, go, prefix, width // HD)
    back = tie(back, gouts)
    grad0, kv = input_back(place, order, da, back, w0, jnp.stack([kv0, kv1]))
    gouts = [gouts[h] + home(grad0, 0, h) for h in range(2)]
    results = jnp.stack([results0[h] + results1[h] for h in range(2)])[:, :, None]
    gouts = jnp.stack(gouts)[:, :, None]
    return results[None], gouts[None], kv[None, 0], kv[None, 1]


def solution(mesh):
    placed = (
        P(None, "mp", "dp", None),
        P(None, "mp", "dp", None),
        P(None, "dp", None),
        P("section", None, "dp", "mp"),
        P("section", None, "mp"),
        P("section", "mp", "dp"),
        P("section", None),
        P("section", "dp", "mp"),
        P("section", "mp"),
        P("section", "mp", "dp"),
        P("section", None),
        P("section", None, None),
        P("section", None, None),
        P("section", None, "mp"),
        P("section", None, "mp"),
    )
    return jax.shard_map(
        on_device,
        mesh=mesh,
        in_specs=placed,
        out_specs=(
            P("section", None, "mp", "dp", None),
            P("section", None, "mp", "dp", None),
            P("section", None, "mp"),
            P("section", None, "mp"),
        ),
        check_vma=False,
    )
```

```python
from functools import partial

import jax
import jax.numpy as jnp
from jax import lax
from jax.experimental import pallas as pl
from jax.experimental.pallas import tpu as pltpu
from jax.sharding import PartitionSpec as P

HEADS = 16
HD = 64
EPS = 1e-5
BF = jnp.bfloat16
F32 = jnp.float32
TQ = 128
CK = 256
KC = 64
SIZES = (2, 3, 4, 5, 6, 7, 8, 10)
TH = 512
VMEM = 48 << 20


def dot(a, b, dims):
    return lax.dot_general(a, b, (dims, ((), ())), preferred_element_type=F32)


def nn(a, b):
    return dot(a, b, ((1,), (0,)))


def nt(a, b):
    return dot(a, b, ((1,), (1,)))


def norm_stats(v):
    centred = v - jnp.mean(v, axis=-1, keepdims=True)
    inv = lax.rsqrt(jnp.mean(centred * centred, axis=-1, keepdims=True) + EPS)
    return centred * inv, inv


def norm_back(v, grad, gain):
    n, inv = norm_stats(v)
    e = grad * gain
    return inv * (e - jnp.mean(e, -1, keepdims=True) - n * jnp.mean(e * n, -1, keepdims=True))


class Place:
    def __init__(self):
        self.mp = lax.axis_size("mp")
        self.g = self.mp // 2
        self.c = lax.axis_index("section")
        self.z = lax.axis_index("mp")
        self.m = self.z // self.g
        self.p = self.z % self.g

    def send(self, value, route):
        pairs = []
        for c in range(2):
            for m in range(2):
                for p in range(self.g):
                    to = route(c, m, p)
                    if to is not None:
                        source = c * self.mp + m * self.g + p
                        pairs.append((source, to[0] * self.mp + to[1] * self.g + to[2]))
        return lax.ppermute(value, ("section", "mp"), pairs)

    def core(self, value):
        return lax.ppermute(value, "section", [(0, 1), (1, 0)])

    def chip(self, value, j):
        return lax.ppermute(value, "mp", [(z, z ^ j) for z in range(self.mp)])


def tie(value, *after):
    return lax.optimization_barrier((value,) + after)[0]


def high_low(v):
    high = v.astype(BF)
    return high, (v - high.astype(F32)).astype(BF)


def gather(block):
    return lax.all_gather(block, "dp", axis=0, tiled=True)


def own_layer(place, l, block):
    return [place.send(block, lambda c, m, p: (m, half, p) if c == l else None) for half in range(2)]


def merged(place, got):
    return jnp.where(place.m == 0, got[0], got[1])


def qkv_block(qkv, qkv_bias, pre):
    weight = qkv[0].astype(BF).transpose(1, 0, 2).reshape(qkv.shape[2], -1)
    width = weight.shape[1]
    bias = jnp.stack(high_low(qkv_bias[0].reshape(-1)))
    pre = jnp.concatenate([v[0].astype(BF) for v in pre], axis=1)
    pre = jnp.pad(pre, ((0, 0), (0, width - pre.shape[1])))
    return jnp.concatenate([weight, pre, jnp.pad(bias, ((0, 14), (0, 0)))], axis=0)


def cut_qkv(v, rows, prefix):
    third = v.shape[1] // 3
    bias = v[rows + prefix].astype(F32) + v[rows + prefix + 1].astype(F32)
    pre = v[rows : rows + prefix]
    return v[:rows], bias, (pre[:, :third], pre[:, third : 2 * third])


def own_shard(place, l, out, up, up_bias, down):
    parts = [up[0].astype(BF), down[0].astype(BF).T, out[0].astype(BF).T]
    block = jnp.concatenate(parts[: 3 - l], axis=1)
    bias = jnp.stack(high_low(up_bias[0]))
    bias = jnp.pad(bias, ((0, 14), (0, block.shape[1] - bias.shape[1])))
    block = jnp.concatenate([block, bias], 0)
    return own_layer(place, l, block)


def cut_shard(shard, rows, ff):
    bias = shard[rows : rows + 2, :ff].astype(F32)
    shard = shard[:rows]
    return shard[:, :ff], shard[:, ff : 2 * ff], shard[:, 2 * ff :], bias[0] + bias[1]


def spread_heads(block, heads):
    if heads == 1:
        return block
    lane = lax.broadcasted_iota(jnp.int32, block.shape, 1) // HD
    return jnp.concatenate([jnp.where(lane == h, block, jnp.zeros_like(block)) for h in range(heads)], 0)

def own_columns(wide, heads):
    return jnp.concatenate([wide[h*HD:(h+1)*HD, h*TQ:(h+1)*TQ] for h in range(heads)], 0)

def widen(mask, heads):
    return mask if heads == 1 else jnp.concatenate([mask] * heads, axis=1)

def each_size(range_ref, t, body):
    for index, size in enumerate(SIZES):
        @pl.when(range_ref[t, 1] == index)
        def _():
            body(pl.multiple_of(range_ref[t, 0], TQ), size * TQ)

def pieces(prefix, start, size):
    out = [(r, start + r, KC, True) for r in range(0, size, KC)]
    return out + [(size + r, r, KC, False) for r in range(0, prefix, KC)]

def both_rows(ref, at, prefix, lane, width):
    return jnp.concatenate([ref[at, lane:lane+width], ref[0:prefix, lane:lane+width]], 0)

def both_lanes(ref, at, prefix, lane, width):
    return jnp.concatenate([ref[lane:lane+width, at], ref[lane:lane+width, 0:prefix]], 1)

def piece_mask(first, span_ref, heads):
    key = lax.broadcasted_iota(jnp.int32, (KC, TQ), 0) + first
    return widen((key >= span_ref[0:1, :]) & (key < span_ref[1:2, :]), heads)

def attn_fwd(prefix, heads, range_ref, span_ref, qkv_ref, o_ref, lse_ref, vt_ref, s_ref, p_ref):
    w = heads * HD
    pair = min(2, heads)
    pw = pair * HD
    t = pl.program_id(0)
    @pl.when(t == 0)
    def _():
        for i in range(vt_ref.shape[1] // CK):
            at = slice(i * CK, (i + 1) * CK)
            vt_ref[:, at] = qkv_ref[at, 2*w:3*w].astype(F32).T.astype(BF)
    def body(start, size):
        here = pl.ds(pl.multiple_of(t*TQ, TQ), TQ)
        at = pl.ds(start, size)
        outs = []
        lanes = range(0, w, pw)
        for g, lane in enumerate(lanes):
            q = spread_heads(qkv_ref[here, lane:lane+pw] * BF(HD ** -0.5), pair)
            s_ref[g, 0:size+prefix] = nt(both_rows(qkv_ref, at, prefix, w+lane, pw), q)
        for g, lane in enumerate(lanes):
            peak = jnp.full((8, pair*TQ), -1e30, F32)
            for row, first, n, masked in pieces(prefix, start, size):
                s = s_ref[g, row:row+n]
                if masked:
                    s = jnp.where(piece_mask(first, span_ref, pair), s, -1e30)
                    s_ref[g, row:row+n] = s
                peak = jnp.maximum(peak, jnp.max(s.reshape(n//8, 8, -1), axis=0))
            peak = jnp.max(peak, axis=0, keepdims=True)
            total = jnp.zeros((8, pair*TQ), F32)
            for row, first, n, masked in pieces(prefix, start, size):
                e = jnp.exp(s_ref[g, row:row+n] - peak)
                p_ref[g, row:row+n] = e.astype(BF)
                total = total + jnp.sum(e.reshape(n//8, 8, -1), axis=0)
            total = jnp.sum(total, axis=0, keepdims=True)
            acc = nn(both_lanes(vt_ref, at, prefix, lane, pw), p_ref[g, 0:size+prefix])
            outs.append(own_columns(acc * (1.0 / total), pair))
            lse = peak + jnp.log(total)
            for h in range(pair):
                row = lane // HD + h
                lse_ref[row:row+1, :] = lse[:, h*TQ:(h+1)*TQ]
        o_ref[...] = jnp.concatenate(outs, 0).T.astype(BF)
    each_size(range_ref, t, body)

def attn_bwd(prefix, heads, range_ref, span_ref, qkv_ref, lse_ref, o_ref, do_ref, out_ref, pre_ref,
             kt_ref, dk_ref, dv_ref, s_ref, dp_ref, p_ref, ds_ref):
    w = heads * HD
    pair = min(2, heads)
    pw = pair * HD
    t = pl.program_id(0)
    @pl.when(t == 0)
    def _():
        for i in range(kt_ref.shape[1] // CK):
            at = slice(i * CK, (i + 1) * CK)
            kt_ref[:, at] = qkv_ref[at, w:2*w].astype(F32).T.astype(BF)
        dk_ref[...] = jnp.zeros_like(dk_ref)
        dv_ref[...] = jnp.zeros_like(dv_ref)
    def body(start, size):
        here = pl.ds(pl.multiple_of(t*TQ, TQ), TQ)
        both = (do_ref[...].astype(F32) * o_ref[...].astype(F32)).T
        outs = []
        at = pl.ds(start, size)
        rows_in = slice(0, size + prefix)
        lanes = range(0, w, pw)
        qs, dos = [], []
        for g, lane in enumerate(lanes):
            q = spread_heads(qkv_ref[here, lane:lane+pw] * BF(HD ** -0.5), pair)
            do = spread_heads(do_ref[:, lane:lane+pw], pair)
            qs.append(q)
            dos.append(do)
            s_ref[g, rows_in] = nt(both_rows(qkv_ref, at, prefix, w+lane, pw), q)
            dp_ref[g, rows_in] = nt(both_rows(qkv_ref, at, prefix, 2*w+lane, pw), do)
        deltas, lses = [], []
        for g, lane in enumerate(lanes):
            rows = range(lane // HD, lane // HD + pair)
            deltas.append(jnp.concatenate([jnp.sum(both[h*HD:(h+1)*HD], axis=0, keepdims=True) for h in rows], 1))
            lses.append(jnp.concatenate([lse_ref[h:h+1, :] for h in rows], 1))
        for row, first, n, masked in pieces(prefix, start, size):
            mask = piece_mask(first, span_ref, pair) if masked else None
            for g in range(len(lanes)):
                prob = jnp.exp(s_ref[g, row:row+n] - lses[g])
                if masked:
                    prob = jnp.where(mask, prob, 0.0)
                p_ref[g, row:row+n] = prob.astype(BF)
                ds_ref[g, row:row+n] = (prob * (dp_ref[g, row:row+n] - deltas[g])).astype(BF)
        for g, lane in enumerate(lanes):
            for to_ref, value in ((dv_ref, nn(p_ref[g, rows_in], dos[g])), (dk_ref, nn(ds_ref[g, rows_in], qs[g]))):
                to_ref[at, lane:lane+pw] += value[0:size]
                to_ref[0:prefix, lane:lane+pw] += value[size:size+prefix]
            dq = nn(both_lanes(kt_ref, at, prefix, lane, pw), ds_ref[g, rows_in])
            outs.append(own_columns(dq, pair))
        out_ref[here, 0:w] = (jnp.concatenate(outs, 0) * HD ** -0.5).T.astype(BF)
    each_size(range_ref, t, body)
    @pl.when(t == pl.num_programs(0) - 1)
    def _():
        out_ref[:, w:2*w] = dk_ref[...].astype(BF)
        out_ref[:, 2*w:3*w] = dv_ref[...].astype(BF)
        pre_ref[0] = dk_ref[0:prefix, :]
        pre_ref[1] = dv_ref[0:prefix, :]

def score_scratch(n, w, kind):
    pair = min(2, w // HD)
    return pltpu.VMEM((w // HD // pair, n + TQ, pair*TQ), kind)

def whole(shape):
    return pl.BlockSpec(shape, lambda t, *_: (0,) * len(shape))

def attend(ranges, span, qkv, prefix, heads):
    n, w = qkv.shape[0], heads*HD
    return pl.pallas_call(
        partial(attn_fwd, prefix, heads),
        grid_spec=pltpu.PrefetchScalarGridSpec(
            num_scalar_prefetch=1, grid=(n//TQ,),
            in_specs=[pl.BlockSpec((2, TQ), lambda t, *_: (0, t)), whole(qkv.shape)],
            out_specs=[pl.BlockSpec((TQ, w), lambda t, *_: (t, 0)), pl.BlockSpec((heads, TQ), lambda t, *_: (0, t))],
            scratch_shapes=[pltpu.VMEM((w, n), BF), score_scratch(n, w, F32), score_scratch(n, w, BF)]),
        out_shape=[jax.ShapeDtypeStruct((n, w), BF), jax.ShapeDtypeStruct((heads, n), F32)],
        compiler_params=pltpu.CompilerParams(dimension_semantics=("arbitrary",), vmem_limit_bytes=VMEM), name="attend",
        cost_estimate=pl.CostEstimate(flops=2*n*n*w*2//4000, bytes_accessed=1, transcendentals=0),
    )(ranges, span, qkv)

def attend_back(ranges, span, qkv, lse, o, do, prefix, heads):
    n, w = qkv.shape[0], heads*HD
    tile = pl.BlockSpec((TQ, w), lambda t, *_: (t, 0))
    return pl.pallas_call(
        partial(attn_bwd, prefix, heads),
        grid_spec=pltpu.PrefetchScalarGridSpec(
            num_scalar_prefetch=1, grid=(n//TQ,),
            in_specs=[pl.BlockSpec((2, TQ), lambda t, *_: (0, t)), whole(qkv.shape),
                      pl.BlockSpec((heads, TQ), lambda t, *_: (0, t)), tile, tile],
            out_specs=[whole((n, 3*w)), whole((2, prefix, w))],
            scratch_shapes=[pltpu.VMEM((w, n), BF), pltpu.VMEM((n, w), F32), pltpu.VMEM((n, w), F32),
                score_scratch(n, w, F32), score_scratch(n, w, F32), score_scratch(n, w, BF), score_scratch(n, w, BF)]),
        out_shape=[jax.ShapeDtypeStruct((n, 3*w), BF), jax.ShapeDtypeStruct((2, prefix, w), F32)],
        compiler_params=pltpu.CompilerParams(dimension_semantics=("arbitrary",), vmem_limit_bytes=VMEM), name="attend_back",
        cost_estimate=pl.CostEstimate(flops=5*n*n*w*2//4000, bytes_accessed=1, transcendentals=0),
    )(ranges, span, qkv, lse, o, do)

def take_size(index):
    return sum(jnp.where(index == i, size, 0) for i, size in enumerate(SIZES))


def spans(lengths, length, prefix):
    ends = jnp.cumsum(lengths)
    starts = ends - lengths
    place = jnp.arange(prefix + length, dtype=jnp.int32) - prefix
    last = lengths.shape[0] - 1
    inside = (place[:, None] >= starts[None, :last]) & (place[:, None] < ends[None, :last])
    low = jnp.sum(jnp.where(inside, starts[None, :last] + prefix, 0), -1)
    high = jnp.sum(jnp.where(inside, ends[None, :last] + prefix, 0), -1)
    tl, th = low.reshape(-1, TQ), high.reshape(-1, TQ)
    tiles = (prefix + length) // TQ
    first = jnp.min(jnp.where(th > 0, tl, prefix + length), axis=1) // TQ
    size = (jnp.max(th, axis=1) + TQ - 1) // TQ - first
    index = jnp.sum((size[:, None] > jnp.array(SIZES)[None]).astype(jnp.int32), 1)
    first = jnp.minimum(first, tiles - take_size(index))
    return jnp.stack([first * TQ, index], 1).astype(jnp.int32), jnp.stack([low, high]).astype(jnp.int32)


def bell_parts(u):
    bell = jnp.exp(-0.5 * u * u)
    t = 1.0 / (1.0 + (0.3275911 * 0.5**0.5) * jnp.abs(u))
    tail = 1.061405429 * t - 1.453152027
    for k in (1.421413741, -0.284496736, 0.254829592):
        tail = tail * t + k
    tail = 0.5 * tail * t * bell
    return bell, jnp.where(u > 0, 1.0 - tail, tail)


def slope_of(u, bell, phi):
    return phi + u * (bell * 0.3989422804014327)


def feed_kernel(mode, cuts, refs):
    count = len(cuts)
    panels, refs = refs[: 2 * count], refs[2 * count :]
    (own_ref, other_ref), refs = refs[:2], refs[2:]
    biases = ()
    if mode != "back":
        biases, refs = refs[:count], refs[count:]
    if mode == "back":
        slope_ref, refs = refs[0], refs[1:]
    out_own_ref, out_other_ref, *kept, x_ref, acc_ref, u_ref, f_ref = refs
    step = 16
    rows = own_ref.shape[0]
    t = pl.program_id(0)

    @pl.when(t == 0)
    def _():
        x_ref[:rows] = own_ref[...]
        x_ref[rows:] = other_ref[...]
        acc_ref[...] = jnp.zeros_like(acc_ref)

    def run(k):
        up_ref, down_ref = panels[2 * k], panels[2 * k + 1]
        if mode == "forward":
            u_ref[...] = nn(x_ref[...], up_ref[...])
            bias = biases[k][...]
            for row in range(0, 2 * rows, step):
                at = slice(row, min(row + step, 2 * rows))
                u = u_ref[at] + bias
                bell, phi = bell_parts(u)
                kept[0][at] = slope_of(u, bell, phi).astype(BF)
                f_ref[at] = (u * phi).astype(BF)
            acc_ref[...] += nt(f_ref[...], down_ref[...])
        else:
            u_ref[...] = nn(x_ref[...], down_ref[...])
            for row in range(0, 2 * rows, step):
                at = slice(row, min(row + step, 2 * rows))
                f_ref[at] = (u_ref[at] * slope_ref[at].astype(F32)).astype(BF)
            acc_ref[...] += nt(f_ref[...], up_ref[...])

    for k, (first, last) in enumerate(cuts):
        if count == 1:
            run(k)
        else:
            pl.when((t >= first) & (t < last))(partial(run, k))

    @pl.when(t == pl.num_programs(0) - 1)
    def _():
        out_own_ref[...] = acc_ref[:rows]
        out_other_ref[...] = acc_ref[rows:].astype(BF)


def feed(mode, panels, own, other, biases=(), slopes=(), keep=False):
    rows, d = own.shape
    th = TH if all(units % TH == 0 for _, units in panels) else TH // 2
    specs, arrays, cuts, at = [], [], [], 0
    for panel, units in panels:
        steps = units // th
        low = partial(lambda at, steps, t: jnp.clip(t - at, 0, steps - 1), at, steps)
        if len(panels) == 1:
            low = lambda t: t
        specs.append(pl.BlockSpec((d, th), partial(lambda low, t: (0, low(t)), low)))
        specs.append(pl.BlockSpec((d, th), partial(lambda low, n, t: (0, n + low(t)), low, steps)))
        arrays += [panel, panel]
        cuts.append((at, at + steps))
        at += steps
    full = pl.BlockSpec((rows, d), lambda t: (0, 0))
    part = pl.BlockSpec((2 * rows, th), lambda t: (0, t))
    specs += [full, full]
    arrays += [own, other]
    if mode != "back":
        for k, bias in enumerate(biases):
            specs.append(pl.BlockSpec((1, th), specs[2 * k].index_map))
            arrays.append(bias)
    specs += [part] * len(slopes)
    arrays += list(slopes)
    outs = [jax.ShapeDtypeStruct((rows, d), F32), jax.ShapeDtypeStruct((rows, d), BF)]
    out_specs = [full, full]
    if keep:
        outs.append(jax.ShapeDtypeStruct((2 * rows, at * th), BF))
        out_specs.append(part)
    scratch = [pltpu.VMEM((2 * rows, d), BF), pltpu.VMEM((2 * rows, d), F32)]
    scratch += [pltpu.VMEM((2 * rows, th), F32), pltpu.VMEM((2 * rows, th), BF)]
    return pl.pallas_call(
        lambda *refs: feed_kernel(mode, cuts, refs),
        grid=(at,),
        in_specs=specs,
        out_specs=out_specs,
        out_shape=outs,
        scratch_shapes=scratch,
        compiler_params=pltpu.CompilerParams(
            dimension_semantics=("arbitrary",), vmem_limit_bytes=VMEM
        ),
        cost_estimate=pl.CostEstimate(
            flops=8 * rows * d * at * th // 4000,
            bytes_accessed=1,
            transcendentals=0,
        ),
        name="feed_" + mode,
    )(*arrays)


class Order:
    def __init__(self, place, prefix, rows):
        self.place, self.prefix, self.rows = place, prefix, rows
        self.length = prefix + place.mp * rows

    def start(self, j, i):
        place = self.place
        return self.prefix + ((place.c ^ i) * place.g + (place.p ^ j)) * self.rows

    def put(self, whole, block, j, i):
        return lax.dynamic_update_slice(whole, block, (self.start(j, i), 0))

    def get(self, whole, j, i):
        return lax.dynamic_slice(whole, (self.start(j, i), 0), (self.rows, whole.shape[1]))


def both_cores(place, mine, theirs):
    return mine + place.core(theirs).astype(F32)


def attention(place, order, blocks, weights, where):
    qkv_w, qkv_b, pre = weights
    prefix = order.prefix
    qkv = jnp.pad(
        jnp.concatenate([jnp.zeros_like(pre[0]), pre[0], pre[1]], axis=1),
        ((0, order.length - prefix), (0, 0)),
    )
    for (j, i), block in blocks.items():
        qkv = order.put(qkv, (nn(block, qkv_w) + qkv_b).astype(BF), j, i)
    return (qkv,) + tuple(attend(*where, qkv, prefix, qkv_w.shape[1] // 3 // HD))


def spread_rows(place, x_own):
    blocks = {}
    for j in range(place.g):
        blocks[j, 0] = x_own if j == 0 else place.chip(x_own, j)
        blocks[j, 1] = place.core(blocks[j, 0])
    return blocks


def out_parts(place, order, o):
    parts = [jnp.concatenate([order.get(o, j, i) for i in range(2)], 0) for j in range(place.g)]
    return [part if j == 0 else place.chip(part, j) for j, part in enumerate(parts)]


def out_project(place, order, x_own, parts, outs, fixed):
    mine = [0.0, 0.0]
    for j, part in enumerate(parts):
        for i in range(2):
            mine[i] = mine[i] + nt(part[i * order.rows : (i + 1) * order.rows], outs[j])
    a = x_own.astype(F32) + both_cores(place, mine[0], mine[1].astype(BF)) + fixed[0]
    x1 = norm_stats(a)[0] * fixed[2] + fixed[4]
    return a, x1


def out_back(place, order, dx1, a, outs, fixed):
    da = norm_back(a, dx1, fixed[2])
    low = da.astype(BF)
    both = jnp.concatenate([low, place.core(low)], 0)
    go = jnp.zeros((order.length, outs[0].shape[1]), BF)
    for j in range(place.g - 1, -1, -1):
        do = nn(both, outs[j]).astype(BF)
        do = do if j == 0 else place.chip(do, j)
        for i in range(2):
            go = order.put(go, do[i * order.rows : (i + 1) * order.rows], j, i)
    return da, go


def total_dp(value):
    count, low = lax.axis_size("dp"), value.astype(BF)
    terms = [low] + [
        lax.ppermute(low, "dp", [(i, i ^ x) for i in range(count)]) for x in range(1, count)
    ]
    terms = [term.astype(F32) for term in terms]
    while len(terms) > 1:
        terms = [terms[i] + terms[i + 1] for i in range(0, len(terms), 2)]
    return terms[0]


def input_back(place, order, da, back, qkv_w, kv=None):
    total, sent = da, []
    for j in range(place.g - 1, -1, -1):
        other = nt(order.get(back, j, 1), qkv_w).astype(BF)
        summed = both_cores(place, nt(order.get(back, j, 0), qkv_w), other)
        if j == 0:
            total = total + summed
        else:
            sent.append(place.chip(summed.astype(BF), j))
    if kv is not None:
        kv = total_dp(kv)
        first = place.m == 0
        kv = place.send(jnp.where(first, kv[0], kv[1]), lambda c, m, p: (m, c, p)) + place.send(
            jnp.where(first, kv[1], kv[0]), lambda c, m, p: (1 - m, c, p)
        )
        sent = tie(sent, kv)
    for value in sent:
        total = total + value.astype(F32)
    return total.astype(BF) if kv is None else (total.astype(BF), kv)


def on_device(
    tokens,
    cotangent,
    lengths,
    qkv_weight,
    qkv_bias,
    out_weight,
    out_bias,
    up_weight,
    up_bias,
    down_weight,
    down_bias,
    norm_gain,
    norm_shift,
    prefix_keys,
    prefix_values,
):
    place = Place()
    g, mp, c, m, p = place.g, place.mp, place.c, place.m, place.p
    rows = tokens.shape[1]
    width, ff, dim = out_weight.shape[1], up_weight.shape[2], up_weight.shape[1]
    prefix = prefix_keys.shape[1]
    order = Order(place, prefix, rows)
    row_lengths = lax.dynamic_index_in_dim(lengths, m, 0, keepdims=False)[0]
    where = spans(row_lengths, mp * rows, prefix)
    fixed = jnp.concatenate([out_bias, down_bias, norm_gain[0], norm_shift[0]], 0)
    other = place.core(fixed)
    fixed = [jnp.where(c == 0, fixed, other), jnp.where(c == 0, other, fixed)]

    def own_rows(array):
        other = lax.dynamic_index_in_dim(array, 1 - m, 0, keepdims=False)[:, 0]
        same = lax.dynamic_index_in_dim(array, m, 0, keepdims=False)[:, 0]
        moved = place.send(other, lambda c, m, p: (c, 1 - m, p) if c == m else None)
        return jnp.where(c == m, same, moved)

    block = qkv_block(qkv_weight, qkv_bias, (prefix_keys, prefix_values))
    thin0 = merged(place, own_layer(place, 0, block))
    w0, qkv_b0, pre0 = cut_qkv(thin0, dim, prefix)
    w0 = gather(w0)
    raw = (out_weight, up_weight, up_bias, down_weight)

    def shard_of(l, *after):
        held = tie(raw, *after)
        return own_shard(place, l, *held)

    shard0 = merged(place, shard_of(0, thin0))
    extra = jnp.pad(out_weight[0].astype(BF).T, ((0, block.shape[0] - dim), (0, 0)))
    wide = jnp.concatenate([block, extra], axis=1)
    thin1 = merged(place, own_layer(place, 1, tie(wide, shard0)))
    w1, qkv_b1, pre1 = cut_qkv(thin1[:, : 3 * width], dim, prefix)
    out1 = thin1[:dim, 3 * width :]
    outs1 = [out1] + [place.chip(out1, j) for j in range(1, g)]

    def panel_of(shards, kinds, *more):
        cuts = [cut_shard(v, dim, ff) for v in shards]
        parts = [v[k] for k in range(kinds) for v in cuts] + list(more)
        return jnp.concatenate(parts, axis=1), jnp.concatenate([v[3] for v in cuts])[None]

    def outs_of(panel, start, count):
        return [panel[:, start + j * width : start + (j + 1) * width] for j in range(count)]

    part_a, bias_a = panel_of([shard0], 3)
    panel_a = gather(tie(part_a, w0))
    x = own_rows(tie(tokens, thin1))
    shards0 = [place.chip(tie(shard0, thin1), j) for j in range(1, g)]
    part_b, bias_b = panel_of(shards0, 3, w1, *outs1)
    panel_b = gather(tie(part_b, panel_a, x))
    shard1 = shard_of(1, x)
    blocks = spread_rows(place, x)
    qkv0, o0, lse0 = attention(place, order, blocks, (w0, qkv_b0, pre0), where)
    parts = out_parts(place, order, o0)
    shard1 = merged(place, tie(shard1, blocks))
    shards1 = [shard1] + [place.chip(shard1, j) for j in range(1, g)]
    second, bias1 = panel_of(tie(shards1, parts), 2)
    panel1 = gather(tie(second, panel_b))
    panels0 = [(panel_a, ff), (panel_b, (g - 1) * ff)]
    panels1 = [(panel1, g * ff)]

    at = (g - 1) * (2 * ff + width)
    w1 = panel_b[:, at : at + 3 * width]
    outs = [
        outs_of(panel_a, 2 * ff, 1) + outs_of(tie(panel_b, parts), 2 * (g - 1) * ff, g - 1),
        outs_of(panel_b, at + 3 * width, g),
    ]
    a0, x1 = out_project(place, order, x, parts, outs[0], fixed[0])
    low = x1.astype(BF)
    mine, theirs, slope0 = feed(
        "forward", panels0, low, place.core(low), [bias_a, bias_b], keep=True
    )
    grad = own_rows(tie(cotangent, low))
    mine = tie(mine, grad)
    z0 = x1 + both_cores(place, mine, theirs) + fixed[0][1]
    y0 = (norm_stats(z0)[0] * fixed[0][3] + fixed[0][5]).astype(BF)

    def home(value, l, half):
        return place.send(value, lambda c, m, p: (l, c, p) if m == half else None)

    blocks = spread_rows(place, y0)
    results0 = [home(tie(y0, blocks), 0, h) for h in range(2)]
    qkv1, o1, lse1 = attention(place, order, blocks, (w1, qkv_b1, pre1), where)
    a1, x1 = out_project(place, order, y0, out_parts(place, order, tie(o1, results0)), outs[1], fixed[1])
    low = x1.astype(BF)
    mine, theirs, slope1 = feed("forward", panels1, low, place.core(low), [bias1], keep=True)
    z1 = x1 + both_cores(place, mine, theirs) + fixed[1][1]
    y1 = (norm_stats(z1)[0] * fixed[1][3] + fixed[1][5]).astype(BF)

    dz = norm_back(z1, grad.astype(F32), fixed[1][3])
    low = dz.astype(BF)
    mine, theirs = feed("back", panels1, low, place.core(low), slopes=[slope1])
    dx1 = dz + both_cores(place, mine, theirs)

    da, go = out_back(place, order, dx1, a1, outs[1], fixed[1])
    results1 = [home(tie(y1, go), 1, h) for h in range(2)]
    back, kv1 = attend_back(*where, qkv1, lse1, o1, go, prefix, width // HD)
    back = tie(back, results1)
    grad1 = input_back(place, order, da, back, w1)

    dz = norm_back(z0, grad1.astype(F32), fixed[0][3])
    low = dz.astype(BF)
    mine, theirs = feed("back", panels0, low, place.core(low), slopes=[slope0])
    dx1 = dz + both_cores(place, mine, theirs)
    da, go = out_back(place, order, dx1, a0, outs[0], fixed[0])
    gouts = [home(tie(grad1, go), 1, h) for h in range(2)]
    back, kv0 = attend_back(*where, qkv0, lse0, o0, go, prefix, width // HD)
    back = tie(back, gouts)
    grad0, kv = input_back(place, order, da, back, w0, jnp.stack([kv0, kv1]))
    gouts = [gouts[h] + home(grad0, 0, h) for h in range(2)]
    results = jnp.stack([results0[h] + results1[h] for h in range(2)])[:, :, None]
    gouts = jnp.stack(gouts)[:, :, None]
    return results[None], gouts[None], kv[None, 0], kv[None, 1]


def solution(mesh):
    placed = (
        P(None, "mp", "dp", None),
        P(None, "mp", "dp", None),
        P(None, "dp", None),
        P("section", None, "dp", "mp"),
        P("section", None, "mp"),
        P("section", "mp", "dp"),
        P("section", None),
        P("section", "dp", "mp"),
        P("section", "mp"),
        P("section", "mp", "dp"),
        P("section", None),
        P("section", None, None),
        P("section", None, None),
        P("section", None, "mp"),
        P("section", None, "mp"),
    )
    return jax.shard_map(
        on_device,
        mesh=mesh,
        in_specs=placed,
        out_specs=(
            P("section", None, "mp", "dp", None),
            P("section", None, "mp", "dp", None),
            P("section", None, "mp"),
            P("section", None, "mp"),
        ),
        check_vma=False,
    )
```

```python
from functools import partial

import jax
import jax.numpy as jnp
from jax import lax
from jax.experimental import pallas as pl
from jax.experimental.pallas import tpu as pltpu
from jax.sharding import PartitionSpec as P

HEADS = 16
HD = 64
EPS = 1e-5
BF = jnp.bfloat16
F32 = jnp.float32
TQ = 128
CK = 256
KC = 64
SIZES = (2, 3, 4, 5, 6, 7, 8, 10)
TH = 512
VMEM = 48 << 20


def dot(a, b, dims):
    return lax.dot_general(a, b, (dims, ((), ())), preferred_element_type=F32)


def nn(a, b):
    return dot(a, b, ((1,), (0,)))


def nt(a, b):
    return dot(a, b, ((1,), (1,)))


def norm_stats(v):
    centred = v - jnp.mean(v, axis=-1, keepdims=True)
    inv = lax.rsqrt(jnp.mean(centred * centred, axis=-1, keepdims=True) + EPS)
    return centred * inv, inv


def norm_back(v, grad, gain):
    n, inv = norm_stats(v)
    e = grad * gain
    return inv * (e - jnp.mean(e, -1, keepdims=True) - n * jnp.mean(e * n, -1, keepdims=True))


class Place:
    def __init__(self):
        self.mp = lax.axis_size("mp")
        self.g = self.mp // 2
        self.c = lax.axis_index("section")
        self.z = lax.axis_index("mp")
        self.m = self.z // self.g
        self.p = self.z % self.g

    def send(self, value, route):
        pairs = []
        for c in range(2):
            for m in range(2):
                for p in range(self.g):
                    to = route(c, m, p)
                    if to is not None:
                        source = c * self.mp + m * self.g + p
                        pairs.append((source, to[0] * self.mp + to[1] * self.g + to[2]))
        return lax.ppermute(value, ("section", "mp"), pairs)

    def core(self, value):
        return lax.ppermute(value, "section", [(0, 1), (1, 0)])

    def chip(self, value, j):
        return lax.ppermute(value, "mp", [(z, z ^ j) for z in range(self.mp)])


def tie(value, *after):
    return lax.optimization_barrier((value,) + after)[0]


def high_low(v):
    high = v.astype(BF)
    return high, (v - high.astype(F32)).astype(BF)


def gather(block):
    return lax.all_gather(block, "dp", axis=0, tiled=True)


def own_layer(place, l, block):
    return [place.send(block, lambda c, m, p: (m, half, p) if c == l else None) for half in range(2)]


def merged(place, got):
    return jnp.where(place.m == 0, got[0], got[1])


def qkv_block(qkv, qkv_bias, pre):
    weight = qkv[0].astype(BF).transpose(1, 0, 2).reshape(qkv.shape[2], -1)
    width = weight.shape[1]
    bias = jnp.stack(high_low(qkv_bias[0].reshape(-1)))
    pre = jnp.concatenate([v[0].astype(BF) for v in pre], axis=1)
    pre = jnp.pad(pre, ((0, 0), (0, width - pre.shape[1])))
    return jnp.concatenate([weight, pre, jnp.pad(bias, ((0, 14), (0, 0)))], axis=0)


def cut_qkv(v, rows, prefix):
    third = v.shape[1] // 3
    bias = v[rows + prefix].astype(F32) + v[rows + prefix + 1].astype(F32)
    pre = v[rows : rows + prefix]
    return v[:rows], bias, (pre[:, :third], pre[:, third : 2 * third])


def own_shard(place, l, out, up, up_bias, down):
    parts = [up[0].astype(BF), down[0].astype(BF).T, out[0].astype(BF).T]
    block = jnp.concatenate(parts[: 3 - l], axis=1)
    bias = jnp.stack(high_low(up_bias[0]))
    bias = jnp.pad(bias, ((0, 14), (0, block.shape[1] - bias.shape[1])))
    block = jnp.concatenate([block, bias], 0)
    return own_layer(place, l, block)


def cut_shard(shard, rows, ff):
    bias = shard[rows : rows + 2, :ff].astype(F32)
    shard = shard[:rows]
    return shard[:, :ff], shard[:, ff : 2 * ff], shard[:, 2 * ff :], bias[0] + bias[1]


def spread_heads(block, heads):
    if heads == 1:
        return block
    lane = lax.broadcasted_iota(jnp.int32, block.shape, 1) // HD
    return jnp.concatenate([jnp.where(lane == h, block, jnp.zeros_like(block)) for h in range(heads)], 0)

def own_columns(wide, heads):
    return jnp.concatenate([wide[h*HD:(h+1)*HD, h*TQ:(h+1)*TQ] for h in range(heads)], 0)

def widen(mask, heads):
    return mask if heads == 1 else jnp.concatenate([mask] * heads, axis=1)

def each_size(range_ref, t, body):
    for index, size in enumerate(SIZES):
        @pl.when(range_ref[t, 1] == index)
        def _():
            body(pl.multiple_of(range_ref[t, 0], TQ), size * TQ)

def pieces(prefix, start, size):
    out = [(r, start + r, KC, True) for r in range(0, size, KC)]
    return out + [(size + r, r, KC, False) for r in range(0, prefix, KC)]

def both_rows(ref, at, prefix, lane, width):
    return jnp.concatenate([ref[at, lane:lane+width], ref[0:prefix, lane:lane+width]], 0)

def both_lanes(ref, at, prefix, lane, width):
    return jnp.concatenate([ref[lane:lane+width, at], ref[lane:lane+width, 0:prefix]], 1)

def piece_mask(first, span_ref, heads):
    key = lax.broadcasted_iota(jnp.int32, (KC, TQ), 0) + first
    return widen((key >= span_ref[0:1, :]) & (key < span_ref[1:2, :]), heads)

def attn_fwd(prefix, heads, range_ref, span_ref, qkv_ref, o_ref, lse_ref, vt_ref, s_ref, p_ref):
    w = heads * HD
    pair = min(2, heads)
    pw = pair * HD
    t = pl.program_id(0)
    @pl.when(t == 0)
    def _():
        for i in range(vt_ref.shape[1] // CK):
            at = slice(i * CK, (i + 1) * CK)
            vt_ref[:, at] = qkv_ref[at, 2*w:3*w].astype(F32).T.astype(BF)
    def body(start, size):
        here = pl.ds(pl.multiple_of(t*TQ, TQ), TQ)
        at = pl.ds(start, size)
        outs = []
        lanes = range(0, w, pw)
        for g, lane in enumerate(lanes):
            q = spread_heads(qkv_ref[here, lane:lane+pw] * BF(HD ** -0.5), pair)
            s_ref[g, 0:size+prefix] = nt(both_rows(qkv_ref, at, prefix, w+lane, pw), q)
        for g, lane in enumerate(lanes):
            peak = jnp.full((8, pair*TQ), -1e30, F32)
            for row, first, n, masked in pieces(prefix, start, size):
                s = s_ref[g, row:row+n]
                if masked:
                    s = jnp.where(piece_mask(first, span_ref, pair), s, -1e30)
                    s_ref[g, row:row+n] = s
                peak = jnp.maximum(peak, jnp.max(s.reshape(n//8, 8, -1), axis=0))
            peak = jnp.max(peak, axis=0, keepdims=True)
            total = jnp.zeros((8, pair*TQ), F32)
            for row, first, n, masked in pieces(prefix, start, size):
                e = jnp.exp(s_ref[g, row:row+n] - peak)
                p_ref[g, row:row+n] = e.astype(BF)
                total = total + jnp.sum(e.reshape(n//8, 8, -1), axis=0)
            total = jnp.sum(total, axis=0, keepdims=True)
            acc = nn(both_lanes(vt_ref, at, prefix, lane, pw), p_ref[g, 0:size+prefix])
            outs.append(own_columns(acc * (1.0 / total), pair))
            lse = peak + jnp.log(total)
            for h in range(pair):
                row = lane // HD + h
                lse_ref[row:row+1, :] = lse[:, h*TQ:(h+1)*TQ]
        o_ref[...] = jnp.concatenate(outs, 0).T.astype(BF)
    each_size(range_ref, t, body)

def attn_bwd(prefix, heads, range_ref, span_ref, qkv_ref, lse_ref, o_ref, do_ref, out_ref, pre_ref,
             kt_ref, dk_ref, dv_ref, s_ref, dp_ref, p_ref, ds_ref):
    w = heads * HD
    pair = min(2, heads)
    pw = pair * HD
    t = pl.program_id(0)
    @pl.when(t == 0)
    def _():
        for i in range(kt_ref.shape[1] // CK):
            at = slice(i * CK, (i + 1) * CK)
            kt_ref[:, at] = qkv_ref[at, w:2*w].astype(F32).T.astype(BF)
        dk_ref[...] = jnp.zeros_like(dk_ref)
        dv_ref[...] = jnp.zeros_like(dv_ref)
    def body(start, size):
        here = pl.ds(pl.multiple_of(t*TQ, TQ), TQ)
        both = (do_ref[...].astype(F32) * o_ref[...].astype(F32)).T
        outs = []
        at = pl.ds(start, size)
        rows_in = slice(0, size + prefix)
        lanes = range(0, w, pw)
        qs, dos = [], []
        for g, lane in enumerate(lanes):
            q = spread_heads(qkv_ref[here, lane:lane+pw] * BF(HD ** -0.5), pair)
            do = spread_heads(do_ref[:, lane:lane+pw], pair)
            qs.append(q)
            dos.append(do)
            s_ref[g, rows_in] = nt(both_rows(qkv_ref, at, prefix, w+lane, pw), q)
            dp_ref[g, rows_in] = nt(both_rows(qkv_ref, at, prefix, 2*w+lane, pw), do)
        deltas, lses = [], []
        for g, lane in enumerate(lanes):
            rows = range(lane // HD, lane // HD + pair)
            deltas.append(jnp.concatenate([jnp.sum(both[h*HD:(h+1)*HD], axis=0, keepdims=True) for h in rows], 1))
            lses.append(jnp.concatenate([lse_ref[h:h+1, :] for h in rows], 1))
        for row, first, n, masked in pieces(prefix, start, size):
            mask = piece_mask(first, span_ref, pair) if masked else None
            for g in range(len(lanes)):
                prob = jnp.exp(s_ref[g, row:row+n] - lses[g])
                if masked:
                    prob = jnp.where(mask, prob, 0.0)
                p_ref[g, row:row+n] = prob.astype(BF)
                ds_ref[g, row:row+n] = (prob * (dp_ref[g, row:row+n] - deltas[g])).astype(BF)
        for g, lane in enumerate(lanes):
            for to_ref, value in ((dv_ref, nn(p_ref[g, rows_in], dos[g])), (dk_ref, nn(ds_ref[g, rows_in], qs[g]))):
                to_ref[at, lane:lane+pw] += value[0:size]
                to_ref[0:prefix, lane:lane+pw] += value[size:size+prefix]
            dq = nn(both_lanes(kt_ref, at, prefix, lane, pw), ds_ref[g, rows_in])
            outs.append(own_columns(dq, pair))
        out_ref[here, 0:w] = (jnp.concatenate(outs, 0) * HD ** -0.5).T.astype(BF)
    each_size(range_ref, t, body)
    @pl.when(t == pl.num_programs(0) - 1)
    def _():
        out_ref[:, w:2*w] = dk_ref[...].astype(BF)
        out_ref[:, 2*w:3*w] = dv_ref[...].astype(BF)
        pre_ref[0] = dk_ref[0:prefix, :]
        pre_ref[1] = dv_ref[0:prefix, :]

def score_scratch(n, w, kind):
    pair = min(2, w // HD)
    return pltpu.VMEM((w // HD // pair, n + TQ, pair*TQ), kind)

def whole(shape):
    return pl.BlockSpec(shape, lambda t, *_: (0,) * len(shape))

def attend(ranges, span, qkv, prefix, heads):
    n, w = qkv.shape[0], heads*HD
    return pl.pallas_call(
        partial(attn_fwd, prefix, heads),
        grid_spec=pltpu.PrefetchScalarGridSpec(
            num_scalar_prefetch=1, grid=(n//TQ,),
            in_specs=[pl.BlockSpec((2, TQ), lambda t, *_: (0, t)), whole(qkv.shape)],
            out_specs=[pl.BlockSpec((TQ, w), lambda t, *_: (t, 0)), pl.BlockSpec((heads, TQ), lambda t, *_: (0, t))],
            scratch_shapes=[pltpu.VMEM((w, n), BF), score_scratch(n, w, F32), score_scratch(n, w, BF)]),
        out_shape=[jax.ShapeDtypeStruct((n, w), BF), jax.ShapeDtypeStruct((heads, n), F32)],
        compiler_params=pltpu.CompilerParams(dimension_semantics=("arbitrary",), vmem_limit_bytes=VMEM), name="attend",
        cost_estimate=pl.CostEstimate(flops=2*n*n*w*2//4000, bytes_accessed=1, transcendentals=0),
    )(ranges, span, qkv)

def attend_back(ranges, span, qkv, lse, o, do, prefix, heads):
    n, w = qkv.shape[0], heads*HD
    tile = pl.BlockSpec((TQ, w), lambda t, *_: (t, 0))
    return pl.pallas_call(
        partial(attn_bwd, prefix, heads),
        grid_spec=pltpu.PrefetchScalarGridSpec(
            num_scalar_prefetch=1, grid=(n//TQ,),
            in_specs=[pl.BlockSpec((2, TQ), lambda t, *_: (0, t)), whole(qkv.shape),
                      pl.BlockSpec((heads, TQ), lambda t, *_: (0, t)), tile, tile],
            out_specs=[whole((n, 3*w)), whole((2, prefix, w))],
            scratch_shapes=[pltpu.VMEM((w, n), BF), pltpu.VMEM((n, w), F32), pltpu.VMEM((n, w), F32),
                score_scratch(n, w, F32), score_scratch(n, w, F32), score_scratch(n, w, BF), score_scratch(n, w, BF)]),
        out_shape=[jax.ShapeDtypeStruct((n, 3*w), BF), jax.ShapeDtypeStruct((2, prefix, w), F32)],
        compiler_params=pltpu.CompilerParams(dimension_semantics=("arbitrary",), vmem_limit_bytes=VMEM), name="attend_back",
        cost_estimate=pl.CostEstimate(flops=5*n*n*w*2//4000, bytes_accessed=1, transcendentals=0),
    )(ranges, span, qkv, lse, o, do)

def take_size(index):
    return sum(jnp.where(index == i, size, 0) for i, size in enumerate(SIZES))


def spans(lengths, length, prefix):
    ends = jnp.cumsum(lengths)
    starts = ends - lengths
    place = jnp.arange(prefix + length, dtype=jnp.int32) - prefix
    last = lengths.shape[0] - 1
    inside = (place[:, None] >= starts[None, :last]) & (place[:, None] < ends[None, :last])
    low = jnp.sum(jnp.where(inside, starts[None, :last] + prefix, 0), -1)
    high = jnp.sum(jnp.where(inside, ends[None, :last] + prefix, 0), -1)
    tl, th = low.reshape(-1, TQ), high.reshape(-1, TQ)
    tiles = (prefix + length) // TQ
    first = jnp.min(jnp.where(th > 0, tl, prefix + length), axis=1) // TQ
    size = (jnp.max(th, axis=1) + TQ - 1) // TQ - first
    index = jnp.sum((size[:, None] > jnp.array(SIZES)[None]).astype(jnp.int32), 1)
    first = jnp.minimum(first, tiles - take_size(index))
    return jnp.stack([first * TQ, index], 1).astype(jnp.int32), jnp.stack([low, high]).astype(jnp.int32)


def bell_parts(u):
    bell = jnp.exp(-0.5 * u * u)
    t = 1.0 / (1.0 + (0.3275911 * 0.5**0.5) * jnp.abs(u))
    tail = 1.061405429 * t - 1.453152027
    for k in (1.421413741, -0.284496736, 0.254829592):
        tail = tail * t + k
    tail = 0.5 * tail * t * bell
    return bell, jnp.where(u > 0, 1.0 - tail, tail)


def slope_of(u, bell, phi):
    return phi + u * (bell * 0.3989422804014327)


def feed_kernel(mode, cuts, refs):
    count = len(cuts)
    panels, refs = refs[: 2 * count], refs[2 * count :]
    (own_ref, other_ref), refs = refs[:2], refs[2:]
    biases = ()
    if mode != "back":
        biases, refs = refs[:count], refs[count:]
    if mode == "back":
        slope_ref, refs = refs[0], refs[1:]
    out_own_ref, out_other_ref, *kept, x_ref, acc_ref, u_ref, f_ref = refs
    step = 16
    rows = own_ref.shape[0]
    t = pl.program_id(0)

    @pl.when(t == 0)
    def _():
        x_ref[:rows] = own_ref[...]
        x_ref[rows:] = other_ref[...]
        acc_ref[...] = jnp.zeros_like(acc_ref)

    def run(k):
        up_ref, down_ref = panels[2 * k], panels[2 * k + 1]
        if mode == "forward":
            u_ref[...] = nn(x_ref[...], up_ref[...])
            bias = biases[k][...]
            for row in range(0, 2 * rows, step):
                at = slice(row, min(row + step, 2 * rows))
                u = u_ref[at] + bias
                bell, phi = bell_parts(u)
                kept[0][at] = slope_of(u, bell, phi).astype(BF)
                f_ref[at] = (u * phi).astype(BF)
            acc_ref[...] += nt(f_ref[...], down_ref[...])
        else:
            u_ref[...] = nn(x_ref[...], down_ref[...])
            for row in range(0, 2 * rows, step):
                at = slice(row, min(row + step, 2 * rows))
                f_ref[at] = (u_ref[at] * slope_ref[at].astype(F32)).astype(BF)
            acc_ref[...] += nt(f_ref[...], up_ref[...])

    for k, (first, last) in enumerate(cuts):
        if count == 1:
            run(k)
        else:
            pl.when((t >= first) & (t < last))(partial(run, k))

    @pl.when(t == pl.num_programs(0) - 1)
    def _():
        out_own_ref[...] = acc_ref[:rows]
        out_other_ref[...] = acc_ref[rows:].astype(BF)


def feed(mode, panels, own, other, biases=(), slopes=(), keep=False):
    rows, d = own.shape
    th = TH if all(units % TH == 0 for _, units in panels) else TH // 2
    specs, arrays, cuts, at = [], [], [], 0
    for panel, units in panels:
        steps = units // th
        low = partial(lambda at, steps, t: jnp.clip(t - at, 0, steps - 1), at, steps)
        if len(panels) == 1:
            low = lambda t: t
        specs.append(pl.BlockSpec((d, th), partial(lambda low, t: (0, low(t)), low)))
        specs.append(pl.BlockSpec((d, th), partial(lambda low, n, t: (0, n + low(t)), low, steps)))
        arrays += [panel, panel]
        cuts.append((at, at + steps))
        at += steps
    full = pl.BlockSpec((rows, d), lambda t: (0, 0))
    part = pl.BlockSpec((2 * rows, th), lambda t: (0, t))
    specs += [full, full]
    arrays += [own, other]
    if mode != "back":
        for k, bias in enumerate(biases):
            specs.append(pl.BlockSpec((1, th), specs[2 * k].index_map))
            arrays.append(bias)
    specs += [part] * len(slopes)
    arrays += list(slopes)
    outs = [jax.ShapeDtypeStruct((rows, d), F32), jax.ShapeDtypeStruct((rows, d), BF)]
    out_specs = [full, full]
    if keep:
        outs.append(jax.ShapeDtypeStruct((2 * rows, at * th), BF))
        out_specs.append(part)
    scratch = [pltpu.VMEM((2 * rows, d), BF), pltpu.VMEM((2 * rows, d), F32)]
    scratch += [pltpu.VMEM((2 * rows, th), F32), pltpu.VMEM((2 * rows, th), BF)]
    return pl.pallas_call(
        lambda *refs: feed_kernel(mode, cuts, refs),
        grid=(at,),
        in_specs=specs,
        out_specs=out_specs,
        out_shape=outs,
        scratch_shapes=scratch,
        compiler_params=pltpu.CompilerParams(
            dimension_semantics=("arbitrary",), vmem_limit_bytes=VMEM
        ),
        cost_estimate=pl.CostEstimate(
            flops=8 * rows * d * at * th // 4000,
            bytes_accessed=1,
            transcendentals=0,
        ),
        name="feed_" + mode,
    )(*arrays)


class Order:
    def __init__(self, place, prefix, rows):
        self.place, self.prefix, self.rows = place, prefix, rows
        self.length = prefix + place.mp * rows

    def start(self, j, i):
        place = self.place
        return self.prefix + ((place.c ^ i) * place.g + (place.p ^ j)) * self.rows

    def put(self, whole, block, j, i):
        return lax.dynamic_update_slice(whole, block, (self.start(j, i), 0))

    def get(self, whole, j, i):
        return lax.dynamic_slice(whole, (self.start(j, i), 0), (self.rows, whole.shape[1]))


def both_cores(place, mine, theirs):
    return mine + place.core(theirs).astype(F32)


def attention(place, order, blocks, weights, where):
    qkv_w, qkv_b, pre = weights
    prefix = order.prefix
    qkv = jnp.pad(
        jnp.concatenate([jnp.zeros_like(pre[0]), pre[0], pre[1]], axis=1),
        ((0, order.length - prefix), (0, 0)),
    )
    for (j, i), block in blocks.items():
        qkv = order.put(qkv, (nn(block, qkv_w) + qkv_b).astype(BF), j, i)
    return (qkv,) + tuple(attend(*where, qkv, prefix, qkv_w.shape[1] // 3 // HD))


def spread_rows(place, x_own):
    blocks = {}
    for j in range(place.g):
        blocks[j, 0] = x_own if j == 0 else place.chip(x_own, j)
        blocks[j, 1] = place.core(blocks[j, 0])
    return blocks


def out_parts(place, order, o):
    parts = [jnp.concatenate([order.get(o, j, i) for i in range(2)], 0) for j in range(place.g)]
    return [part if j == 0 else place.chip(part, j) for j, part in enumerate(parts)]


def out_project(place, order, x_own, parts, outs, fixed):
    mine = [0.0, 0.0]
    for j, part in enumerate(parts):
        for i in range(2):
            mine[i] = mine[i] + nt(part[i * order.rows : (i + 1) * order.rows], outs[j])
    a = x_own.astype(F32) + both_cores(place, mine[0], mine[1].astype(BF)) + fixed[0]
    x1 = norm_stats(a)[0] * fixed[2] + fixed[4]
    return a, x1


def out_back(place, order, dx1, a, outs, fixed):
    da = norm_back(a, dx1, fixed[2])
    low = da.astype(BF)
    both = jnp.concatenate([low, place.core(low)], 0)
    go = jnp.zeros((order.length, outs[0].shape[1]), BF)
    for j in range(place.g - 1, -1, -1):
        do = nn(both, outs[j]).astype(BF)
        do = do if j == 0 else place.chip(do, j)
        for i in range(2):
            go = order.put(go, do[i * order.rows : (i + 1) * order.rows], j, i)
    return da, go


def total_dp(value):
    count, low = lax.axis_size("dp"), value.astype(BF)
    terms = [low] + [
        lax.ppermute(low, "dp", [(i, i ^ x) for i in range(count)]) for x in range(1, count)
    ]
    terms = [term.astype(F32) for term in terms]
    while len(terms) > 1:
        terms = [terms[i] + terms[i + 1] for i in range(0, len(terms), 2)]
    return terms[0]


def input_back(place, order, da, back, qkv_w, kv=None):
    total, sent = da, []
    for j in range(place.g - 1, -1, -1):
        other = nt(order.get(back, j, 1), qkv_w).astype(BF)
        summed = both_cores(place, nt(order.get(back, j, 0), qkv_w), other)
        if j == 0:
            total = total + summed
        else:
            sent.append(place.chip(summed.astype(BF), j))
    if kv is not None:
        kv = total_dp(kv)
        sent = tie(sent, kv)
    for value in sent:
        total = total + value.astype(F32)
    total = total.astype(BF)
    if kv is None:
        return total
    first, kv = place.m == 0, tie(kv, total).astype(BF)
    halves = (
        place.send(jnp.where(first, kv[0], kv[1]), lambda c, m, p: (m, c, p)),
        place.send(jnp.where(first, kv[1], kv[0]), lambda c, m, p: (1 - m, c, p)),
    )
    return total, halves[0].astype(F32) + halves[1].astype(F32)


def on_device(
    tokens,
    cotangent,
    lengths,
    qkv_weight,
    qkv_bias,
    out_weight,
    out_bias,
    up_weight,
    up_bias,
    down_weight,
    down_bias,
    norm_gain,
    norm_shift,
    prefix_keys,
    prefix_values,
):
    place = Place()
    g, mp, c, m, p = place.g, place.mp, place.c, place.m, place.p
    rows = tokens.shape[1]
    width, ff, dim = out_weight.shape[1], up_weight.shape[2], up_weight.shape[1]
    prefix = prefix_keys.shape[1]
    order = Order(place, prefix, rows)
    row_lengths = lax.dynamic_index_in_dim(lengths, m, 0, keepdims=False)[0]
    where = spans(row_lengths, mp * rows, prefix)
    fixed = jnp.concatenate([out_bias, down_bias, norm_gain[0], norm_shift[0]], 0)
    other = place.core(fixed)
    fixed = [jnp.where(c == 0, fixed, other), jnp.where(c == 0, other, fixed)]

    def own_rows(array):
        other = lax.dynamic_index_in_dim(array, 1 - m, 0, keepdims=False)[:, 0]
        same = lax.dynamic_index_in_dim(array, m, 0, keepdims=False)[:, 0]
        moved = place.send(other, lambda c, m, p: (c, 1 - m, p) if c == m else None)
        return jnp.where(c == m, same, moved)

    block = qkv_block(qkv_weight, qkv_bias, (prefix_keys, prefix_values))
    thin0 = merged(place, own_layer(place, 0, block))
    w0, qkv_b0, pre0 = cut_qkv(thin0, dim, prefix)
    w0 = gather(w0)
    raw = (out_weight, up_weight, up_bias, down_weight)

    def shard_of(l, *after):
        held = tie(raw, *after)
        return own_shard(place, l, *held)

    shard0 = merged(place, shard_of(0, thin0))
    extra = jnp.pad(out_weight[0].astype(BF).T, ((0, block.shape[0] - dim), (0, 0)))
    wide = jnp.concatenate([block, extra], axis=1)
    thin1 = merged(place, own_layer(place, 1, tie(wide, shard0)))
    w1, qkv_b1, pre1 = cut_qkv(thin1[:, : 3 * width], dim, prefix)
    out1 = thin1[:dim, 3 * width :]
    outs1 = [out1] + [place.chip(out1, j) for j in range(1, g)]

    def panel_of(shards, kinds, *more):
        cuts = [cut_shard(v, dim, ff) for v in shards]
        parts = [v[k] for k in range(kinds) for v in cuts] + list(more)
        return jnp.concatenate(parts, axis=1), jnp.concatenate([v[3] for v in cuts])[None]

    def outs_of(panel, start, count):
        return [panel[:, start + j * width : start + (j + 1) * width] for j in range(count)]

    part_a, bias_a = panel_of([shard0], 3)
    panel_a = gather(tie(part_a, w0))
    x = own_rows(tie(tokens, thin1))
    shards0 = [place.chip(tie(shard0, thin1), j) for j in range(1, g)]
    part_b, bias_b = panel_of(shards0, 3, w1, *outs1)
    panel_b = gather(tie(part_b, panel_a, x))
    shard1 = shard_of(1, x)
    blocks = spread_rows(place, x)
    qkv0, o0, lse0 = attention(place, order, blocks, (w0, qkv_b0, pre0), where)
    parts = out_parts(place, order, o0)
    shard1 = merged(place, tie(shard1, blocks))
    shards1 = [shard1] + [place.chip(shard1, j) for j in range(1, g)]
    second, bias1 = panel_of(tie(shards1, parts), 2)
    panel1 = gather(tie(second, panel_b))
    panels0 = [(panel_a, ff), (panel_b, (g - 1) * ff)]
    panels1 = [(panel1, g * ff)]

    at = (g - 1) * (2 * ff + width)
    w1 = panel_b[:, at : at + 3 * width]
    outs = [
        outs_of(panel_a, 2 * ff, 1) + outs_of(tie(panel_b, parts), 2 * (g - 1) * ff, g - 1),
        outs_of(panel_b, at + 3 * width, g),
    ]
    a0, x1 = out_project(place, order, x, parts, outs[0], fixed[0])
    low = x1.astype(BF)
    mine, theirs, slope0 = feed(
        "forward", panels0, low, place.core(low), [bias_a, bias_b], keep=True
    )
    grad = own_rows(tie(cotangent, low))
    mine = tie(mine, grad)
    z0 = x1 + both_cores(place, mine, theirs) + fixed[0][1]
    y0 = (norm_stats(z0)[0] * fixed[0][3] + fixed[0][5]).astype(BF)

    def home(value, l, half):
        return place.send(value, lambda c, m, p: (l, c, p) if m == half else None)

    blocks = spread_rows(place, y0)
    results0 = [home(tie(y0, blocks), 0, h) for h in range(2)]
    qkv1, o1, lse1 = attention(place, order, blocks, (w1, qkv_b1, pre1), where)
    a1, x1 = out_project(place, order, y0, out_parts(place, order, tie(o1, results0)), outs[1], fixed[1])
    low = x1.astype(BF)
    mine, theirs, slope1 = feed("forward", panels1, low, place.core(low), [bias1], keep=True)
    z1 = x1 + both_cores(place, mine, theirs) + fixed[1][1]
    y1 = (norm_stats(z1)[0] * fixed[1][3] + fixed[1][5]).astype(BF)

    dz = norm_back(z1, grad.astype(F32), fixed[1][3])
    low = dz.astype(BF)
    mine, theirs = feed("back", panels1, low, place.core(low), slopes=[slope1])
    dx1 = dz + both_cores(place, mine, theirs)

    da, go = out_back(place, order, dx1, a1, outs[1], fixed[1])
    results1 = [home(tie(y1, go), 1, h) for h in range(2)]
    back, kv1 = attend_back(*where, qkv1, lse1, o1, go, prefix, width // HD)
    back = tie(back, results1)
    grad1 = input_back(place, order, da, back, w1)

    dz = norm_back(z0, grad1.astype(F32), fixed[0][3])
    low = dz.astype(BF)
    mine, theirs = feed("back", panels0, low, place.core(low), slopes=[slope0])
    dx1 = dz + both_cores(place, mine, theirs)
    da, go = out_back(place, order, dx1, a0, outs[0], fixed[0])
    gouts = [home(tie(grad1, go), 1, h) for h in range(2)]
    back, kv0 = attend_back(*where, qkv0, lse0, o0, go, prefix, width // HD)
    back = tie(back, gouts)
    grad0, kv = input_back(place, order, da, back, w0, jnp.stack([kv0, kv1]))
    mine = place.send(grad0, lambda c, m, p: (m, c, p))
    grads0 = [mine, place.core(mine)]
    gouts = [jnp.where(c == 0, grads0[h], gouts[h]) for h in range(2)]
    results = jnp.stack([results0[h] + results1[h] for h in range(2)])[:, :, None]
    gouts = jnp.stack(gouts)[:, :, None]
    return results[None], gouts[None], kv[None, 0], kv[None, 1]


def solution(mesh):
    placed = (
        P(None, "mp", "dp", None),
        P(None, "mp", "dp", None),
        P(None, "dp", None),
        P("section", None, "dp", "mp"),
        P("section", None, "mp"),
        P("section", "mp", "dp"),
        P("section", None),
        P("section", "dp", "mp"),
        P("section", "mp"),
        P("section", "mp", "dp"),
        P("section", None),
        P("section", None, None),
        P("section", None, None),
        P("section", None, "mp"),
        P("section", None, "mp"),
    )
    return jax.shard_map(
        on_device,
        mesh=mesh,
        in_specs=placed,
        out_specs=(
            P("section", None, "mp", "dp", None),
            P("section", None, "mp", "dp", None),
            P("section", None, "mp"),
            P("section", None, "mp"),
        ),
        check_vma=False,
    )
```
